32 devices in a mesh: dp: 2 (over x), fsdp: 16 (over z, y, core).
Axes of the slice: x: 2, y: 2, z: 4, core: 2. Of those that a mesh axis runs over, the one named last changes fastest.
Arguments:
- hidden: bfloat16 [8192, 8192], P(('dp', 'fsdp')), may hold values from -6 to 6
- lengths: int32 [128], P(('dp', 'fsdp')), may hold values from 16 to 112, as said below
- learner: int32 [128], P(('dp', 'fsdp')), may hold values from 0 to 1, as said below
- slot_offset: int32 [128], P(('dp', 'fsdp')), may hold values from 0 to 240, as said below
- norm_gain: bfloat16 [8192], P('fsdp'), may hold values from 0.099609375 to 1.8984375
- query_weight: bfloat16 [8192, 512], P('fsdp'), may hold values from -2 to 2
- keyval_weight: bfloat16 [8192, 256], P('fsdp'), may hold values from -2 to 2
Outputs:
- attended: bfloat16 [8192, 512], P(('dp', 'fsdp'))
The draws below stay inside these ranges and needn't reach their ends.
Inputs may be any that keep to these rules, and one draw needn't show every extreme that they name: Rows 2k and 2k+1 of one device form a pair whose lengths sum to 128; a device's rows fill its 256 slots in order. Both rows of a pair go to the same learner; every learner receives exactly 2 pairs from the devices of its fsdp index. `slot_offset`: the rows that one learner receives tile its 256 slots without gaps, in some order.
All inputs are finite; a program needn't handle non-finite values.
Results may differ from the reference program's by a relative error of at most 0.0076.
Values may be sent and summed in bfloat16 or wider, within the bound.
A program may use at most 128 MiB of HBM per device.

```python
import jax
import jax.numpy as jnp
from jax import lax

D = 8192
HD = 128
QH = 4
PAIR_LEN = 128
PAIRS_DEV = 2
ROWS_DEV = 4
CAP = 256
LMIN = 16
MAX_LEN = 112
TOKENS = 8192
N_DP = 2
N_FSDP = 16


def routing_tables(key):
    lengths_key, chosen_key, pair_key, order_key = jax.random.split(jax.random.fold_in(key, 7), 4)
    lead_len = jax.random.randint(lengths_key, (N_DP, N_FSDP, PAIRS_DEV), LMIN, MAX_LEN + 1).astype(jnp.int32)
    chosen = jax.random.randint(chosen_key, (), 0, N_DP * N_FSDP * PAIRS_DEV).astype(jnp.int32)
    pair_index = jnp.arange(N_DP * N_FSDP * PAIRS_DEV, dtype=jnp.int32).reshape(N_DP, N_FSDP, PAIRS_DEV)
    lead_len = jnp.where(pair_index == chosen, LMIN, lead_len)
    pair_lengths = jnp.stack([lead_len, PAIR_LEN - lead_len], axis=-1).astype(jnp.int32)
    shuffles = jax.vmap(lambda k: jax.random.permutation(k, N_DP * PAIRS_DEV))(jax.random.split(pair_key, N_FSDP))
    slots = shuffles.astype(jnp.int32).reshape(N_FSDP, N_DP, PAIRS_DEV).transpose(1, 0, 2)
    learner_of = slots // PAIRS_DEV
    slot_index = slots % PAIRS_DEV
    local_row = slot_index[..., None] * 2 + jnp.arange(2, dtype=jnp.int32)[None, None, None, :]
    learner_full = jnp.broadcast_to(learner_of[..., None], local_row.shape)
    column_full = jnp.broadcast_to(jnp.arange(N_FSDP, dtype=jnp.int32)[None, :, None, None], local_row.shape)
    len_table = jnp.zeros((N_DP, N_FSDP, ROWS_DEV), jnp.int32).at[learner_full, column_full, local_row].set(pair_lengths)
    ranks = jax.vmap(lambda k: jax.random.permutation(k, ROWS_DEV))(jax.random.split(order_key, N_DP * N_FSDP))
    ranks = ranks.astype(jnp.int32).reshape(N_DP, N_FSDP, ROWS_DEV)
    chosen_owner = chosen // (N_FSDP * PAIRS_DEV)
    chosen_column = chosen // PAIRS_DEV % N_FSDP
    chosen_pair = chosen % PAIRS_DEV
    chosen_learner = learner_of[chosen_owner, chosen_column, chosen_pair]
    chosen_row = slot_index[chosen_owner, chosen_column, chosen_pair] * 2
    ranks = ranks.at[chosen_learner, chosen_column, chosen_row].set(ROWS_DEV)
    earlier = ranks[..., None, :] < ranks[..., :, None]
    offset_table = jnp.sum(jnp.where(earlier, len_table[..., None, :], 0), axis=-1).astype(jnp.int32)
    offsets = offset_table[learner_full, column_full, local_row]
    return (pair_lengths.reshape(-1), learner_full.reshape(-1).astype(jnp.int32), offsets.reshape(-1).astype(jnp.int32))


def draw_lengths(key, part):
    return routing_tables(key)[0]


def draw_learner(key, part):
    return routing_tables(key)[1]


def draw_slot_offset(key, part):
    return routing_tables(key)[2]


def projection_weights(key):
    query_key, fresh_key, value_key = jax.random.split(jax.random.fold_in(key, 11), 3)
    fan_scale = D ** (-0.5)
    query = jax.random.normal(query_key, (D, QH * HD), jnp.float32) * fan_scale
    value_part = jax.random.normal(value_key, (D, HD), jnp.float32) * fan_scale
    fresh = jax.random.normal(fresh_key, (D, HD), jnp.float32) * fan_scale
    key_part = fresh
    query = jnp.clip(query, -2.0, 2.0)
    both = jnp.clip(jnp.concatenate([key_part, value_part], axis=1), -2.0, 2.0)
    return (query, both)


def draw_query_weight(key, part):
    return projection_weights(key)[0].astype(jnp.bfloat16)


def draw_keyval_weight(key, part):
    return projection_weights(key)[1].astype(jnp.bfloat16)


def steps_of(key, extent, pieces, low, high):
    loudness, own = 1.0, jax.random.fold_in(key, 6)
    for dim, shards_of in pieces:
        draws = jnp.exp(jax.random.uniform(jax.random.fold_in(own, dim), (shards_of,), jnp.float32, low / len(pieces), high / len(pieces)))
        loudness = loudness * jnp.repeat(draws, extent[dim] // shards_of).reshape([-1 if axis == dim else 1 for axis in range(len(extent))])
    return loudness


def gaussian(own_key, extent, scale, limit, cuts=(), kind=jnp.bfloat16):
    factor_of = steps_of(own_key, extent, cuts, -0.22, 0.18) if cuts else 1.0
    result = jax.random.normal(own_key, extent, jnp.float32) * scale * factor_of
    return jnp.minimum(jnp.maximum(result, -limit), limit).astype(kind)


def setup_inputs(seed: int = 0) -> dict:
    seeds = jax.random.split(jax.random.key(seed), 8)
    return {
        "hidden": gaussian(seeds[0], (TOKENS, D), 1.0, 6.0, ((0, 32),)),
        "lengths": draw_lengths(jax.random.fold_in(seeds[7], 71), 0),
        "learner": draw_learner(jax.random.fold_in(seeds[7], 71), 0),
        "slot_offset": draw_slot_offset(jax.random.fold_in(seeds[7], 71), 0),
        "norm_gain": jnp.clip(1.0 + 0.18 * jax.random.normal(seeds[4], (D,), jnp.float32), 0.099609375, 1.8984375).astype(jnp.bfloat16),
        "query_weight": draw_query_weight(jax.random.fold_in(seeds[7], 71), 0),
        "keyval_weight": draw_keyval_weight(jax.random.fold_in(seeds[7], 71), 0),
    }


rope_base = 500000.0
norm_eps = 1e-05

def rotate(values, positions):
    midpoint = values.shape[-1] // 2
    frequency = rope_base ** (-jnp.arange(midpoint, dtype=jnp.float32) * 2.0 / values.shape[-1])
    angles = positions.astype(jnp.float32)[:, None] * frequency[None, :]
    cosine = jnp.cos(angles)[:, None, :]
    sines = jnp.sin(angles)[:, None, :]
    leading = values[..., :midpoint]
    trailing = values[..., midpoint:]
    return jnp.concatenate([leading * cosine - trailing * sines, trailing * cosine + leading * sines], -1)

def project_block(rows, positions, norm_gain, query_weight, keyval_weight):
    inverse = lax.rsqrt(lax.optimization_barrier(jnp.mean(jnp.square(rows.astype(jnp.float32)), axis=1, keepdims=True)) + norm_eps)
    normed = (rows.astype(jnp.float32) * inverse * norm_gain.astype(jnp.float32)[None, :]).astype(jnp.bfloat16)
    query = jnp.dot(normed, query_weight, preferred_element_type=jnp.float32)
    key_value = jnp.dot(normed, keyval_weight, preferred_element_type=jnp.float32)
    query = rotate(query.reshape(-1, QH, HD), positions).reshape(-1, QH * HD)
    key_part = rotate(key_value[:, :HD].reshape(-1, 1, HD), positions).reshape(-1, HD)
    return jnp.concatenate([query, key_part, key_value[:, HD:]], axis=1).astype(jnp.bfloat16)

def attend_block(packed, segment, position):
    query = packed[:, :QH * HD].reshape(-1, QH, HD).astype(jnp.float32)
    key_part = packed[:, QH * HD:QH * HD + HD].astype(jnp.float32)
    value_part = packed[:, QH * HD + HD:].astype(jnp.float32)
    scores = jnp.einsum('qhd,kd->hqk', query, key_part) * HD ** (-0.5)
    allowed = (segment[:, None] == segment[None, :]) & (position[None, :] <= position[:, None])
    scores = jnp.where(allowed[None], scores, -1e+30)
    row_max = lax.optimization_barrier(jnp.max(scores, axis=2, keepdims=True))
    weights = jnp.exp(scores - row_max)
    row_total = lax.optimization_barrier(jnp.sum(weights, axis=2, keepdims=True))
    probability = (weights / row_total).astype(jnp.bfloat16).astype(jnp.float32)
    mixed = jnp.einsum('hqk,kd->qhd', probability, value_part)
    return mixed.reshape(-1, QH * HD).astype(jnp.bfloat16)

def reference(hidden, lengths, learner, slot_offset, norm_gain, query_weight, keyval_weight):
    devices = N_DP * N_FSDP
    lengths_dev = lengths.reshape(devices, ROWS_DEV)
    starts = jnp.cumsum(lengths_dev, axis=1) - lengths_dev
    places = jnp.arange(CAP, dtype=jnp.int32)
    relative = places[None, :, None] - starts[:, None, :]
    inside = (relative >= 0) & (relative < lengths_dev[:, None, :])
    position = lax.optimization_barrier(jnp.sum(jnp.where(inside, relative, 0), axis=2)).astype(jnp.int32)
    row_local = lax.optimization_barrier(jnp.sum(jnp.where(inside, jnp.arange(ROWS_DEV, dtype=jnp.int32)[None, None, :], 0), axis=2)).astype(jnp.int32)
    row_global = row_local + (jnp.arange(devices, dtype=jnp.int32) * ROWS_DEV)[:, None]
    column = jnp.arange(devices, dtype=jnp.int32) % N_FSDP
    target_dev = learner.reshape(devices, ROWS_DEV) * N_FSDP + column[:, None]
    target_start = target_dev * CAP + slot_offset.reshape(devices, ROWS_DEV)
    target = jnp.take_along_axis(target_start, row_local, axis=1) + position
    source = jnp.zeros((TOKENS,), jnp.int32).at[target.reshape(-1)].set(jnp.arange(TOKENS, dtype=jnp.int32))

    def project_one(operands):
        rows, positions = operands
        return project_block(rows, positions, norm_gain, query_weight, keyval_weight)
    packed = lax.map(project_one, (hidden.reshape(devices, CAP, D), position))
    packed = packed.reshape(TOKENS, (QH + 2) * HD)[source]
    segment = row_global.reshape(-1)[source]
    learner_position = position.reshape(-1)[source]

    def attend_one(operands):
        block, seg_block, pos_block = operands
        return attend_block(block, seg_block, pos_block)
    attended = lax.map(attend_one, (packed.reshape(devices, CAP, -1), segment.reshape(devices, CAP), learner_position.reshape(devices, CAP)))
    return attended.reshape(TOKENS, QH * HD)
```

```python
import functools
import math

import jax
import jax.numpy as jnp
from jax import lax
from jax.experimental import pallas as pl
from jax.experimental.pallas import tpu as pltpu
from jax.sharding import PartitionSpec as P

HD = 128
QH = 4
ROPE_BASE = 500000.0
NORM_EPS = 1e-05
MESH = pl.DeviceIdType.MESH
PIECES = 4


def kernel(
    n_dp,
    n_fsdp,
    lengths_ref,
    learner_ref,
    offset_ref,
    hidden_ref,
    gain_ref,
    query_ref,
    keyval_ref,
    out_ref,
    weights,
    gains,
    own_rows,
    mate_rows,
    own_inv,
    mate_inv,
    total,
    mate_total,
    cosine,
    sine,
    masked,
    place_here,
    place_there,
    sent_heads,
    got_heads,
    local_sem,
    part_recv,
    z_send,
    y_send,
    x_send,
    gain_send,
    gain_recv,
    rows_send,
    rows_recv,
    inv_sem,
    sum_send,
    sum_recv,
    head_send,
    head_recv,
):
    dp = lax.axis_index("dp")
    fs = lax.axis_index("fsdp")
    core = lax.rem(fs, 2)
    y = lax.rem(fs // 2, 2)
    z = fs // 4
    n_z = n_fsdp // 4
    x = lax.rem(dp, 2)
    x_peer = {"dp": dp + 1 - 2 * x}
    mate = {"fsdp": fs + 1 - 2 * core}
    y_peer = {"fsdp": fs + 2 - 4 * y}
    tokens = own_rows.shape[0]
    depth = query_ref.shape[0]
    n_cols = weights.shape[2]
    q_cols = QH * HD
    part = depth // PIECES
    own = z * 2 + y
    n_shards = 2 * n_z
    role_a = 3 * x
    role_b = 1 + x
    role_c = 2 - x
    role_d = 3 - 3 * x

    load_q = pltpu.make_async_copy(query_ref, weights.at[own, :, pl.ds(0, q_cols)], local_sem.at[0])
    load_kv = pltpu.make_async_copy(
        keyval_ref, weights.at[own, :, pl.ds(q_cols, n_cols - q_cols)], local_sem.at[1]
    )
    load_rows = pltpu.make_async_copy(hidden_ref, own_rows, local_sem.at[2])
    load_q.start()
    load_kv.start()
    load_rows.start()
    gains[own] = jnp.broadcast_to(gain_ref[...].astype(jnp.float32), (8, depth))

    barrier = pltpu.get_barrier_semaphore()
    pl.semaphore_signal(barrier, inc=1, device_id=x_peer, device_id_type=MESH)
    pl.semaphore_signal(barrier, inc=1, device_id=mate, device_id_type=MESH)
    for step in range(1, n_shards):
        peer = lax.rem(own + step, n_shards)
        pl.semaphore_signal(
            barrier, inc=1, device_id={"fsdp": peer * 2 + core}, device_id_type=MESH
        )
    pl.semaphore_wait(barrier, n_shards + 1)

    def piece(slot, q):
        return weights.at[slot, pl.ds(pl.multiple_of(q * part, part), part), :]

    def send_z(zz, q, up):
        slot = zz * 2 + y
        step = 1 if up else -1
        return pltpu.make_async_remote_copy(
            src_ref=piece(slot, q),
            dst_ref=piece(slot, q),
            send_sem=z_send.at[1 if up else 0, zz, q],
            recv_sem=part_recv.at[slot, q],
            device_id={"fsdp": fs + 4 * step},
            device_id_type=MESH,
        )

    def send_y(zz, q):
        slot = zz * 2 + y
        return pltpu.make_async_remote_copy(
            src_ref=piece(slot, q),
            dst_ref=piece(slot, q),
            send_sem=y_send.at[zz, q],
            recv_sem=part_recv.at[slot, q],
            device_id=y_peer,
            device_id_type=MESH,
        )

    def send_x(slot, q):
        return pltpu.make_async_remote_copy(
            src_ref=piece(slot, q),
            dst_ref=piece(slot, q),
            send_sem=x_send.at[slot, q],
            recv_sem=part_recv.at[slot, q],
            device_id=x_peer,
            device_id_type=MESH,
        )

    def arrived(slot, q):
        send_x(slot, q).wait_recv()

    def send_gain(step):
        peer = lax.rem(own + step, n_shards)
        return pltpu.make_async_remote_copy(
            src_ref=gains.at[own],
            dst_ref=gains.at[own],
            send_sem=gain_send.at[step],
            recv_sem=gain_recv.at[own],
            device_id={"fsdp": peer * 2 + core},
            device_id_type=MESH,
        )

    def send_rows(s):
        start = pl.multiple_of((s * 2 + 1 - core) * depth, depth)
        return pltpu.make_async_remote_copy(
            src_ref=hidden_ref.at[:, pl.ds(start, depth)],
            dst_ref=mate_rows.at[s],
            send_sem=rows_send.at[s],
            recv_sem=rows_recv.at[s],
            device_id=mate,
            device_id_type=MESH,
        )

    send_inv = pltpu.make_async_remote_copy(
        src_ref=own_inv,
        dst_ref=mate_inv,
        send_sem=inv_sem.at[0],
        recv_sem=inv_sem.at[1],
        device_id=mate,
        device_id_type=MESH,
    )

    load_q.wait()
    load_kv.wait()
    for q in (role_a, role_b, role_c):
        pl.when(z < n_z - 1)(lambda q=q: send_z(z, q, True).start())
        pl.when(z > 0)(lambda q=q: send_z(z, q, False).start())
        send_y(z, q).start()
    send_y(z, role_d).start()
    for step in range(1, n_shards):
        send_gain(step).start()
    for s in range(n_shards):
        send_rows(s).start()

    load_rows.wait()
    width = own_rows.shape[1]

    def square(i, carry):
        rows = pl.ds(pl.multiple_of(i * 32, 32), 32)
        values = own_rows[rows, :].astype(jnp.float32)
        mean = jnp.sum(values * values, axis=1, keepdims=True) / width
        own_inv[rows, :] = jnp.broadcast_to(lax.rsqrt(mean + NORM_EPS), (32, 128))
        return carry

    lax.fori_loop(0, tokens // 32, square, 0)
    send_inv.start()

    n_rows = lengths_ref.shape[0]
    across = lax.broadcasted_iota(jnp.int32, (1, tokens), 1)
    down = lax.broadcasted_iota(jnp.int32, (tokens, 1), 0)
    row_across = jnp.zeros_like(across)
    row_down = jnp.zeros_like(down)
    start_down = jnp.zeros_like(down)
    target = jnp.zeros_like(across)
    goes_to = jnp.zeros_like(across)
    start = jnp.int32(0)
    for r in range(n_rows):
        in_across = across >= start
        in_down = down >= start
        row_across = jnp.where(in_across, r, row_across)
        row_down = jnp.where(in_down, r, row_down)
        start_down = jnp.where(in_down, start, start_down)
        target = jnp.where(in_across, offset_ref[r] + across - start, target)
        goes_to = jnp.where(in_across, learner_ref[r], goes_to)
        start = start + lengths_ref[r]
    position = (down - start_down).astype(jnp.float32)
    lane = lax.broadcasted_iota(jnp.int32, (1, HD), 1)
    half = HD // 2
    index = jnp.where(lane < half, lane, lane - half).astype(jnp.float32)
    angle = position * jnp.exp(index * (-2.0 * math.log(ROPE_BASE) / HD))
    cosine[...] = jnp.cos(angle)
    sine[...] = jnp.where(lane < half, -jnp.sin(angle), jnp.sin(angle))
    allowed = (row_across == row_down) & (across <= down)
    masked[...] = jnp.where(allowed, 0.0, 1.0)
    if n_dp == 2:
        slot_iota = lax.broadcasted_iota(jnp.int32, (tokens, tokens), 0)
        place_here[...] = jnp.where(
            slot_iota == jnp.where(goes_to == dp, target, -1), 1.0, 0.0
        ).astype(jnp.bfloat16)
        place_there[...] = jnp.where(
            slot_iota == jnp.where(goes_to == 1 - dp, target, -1), 1.0, 0.0
        ).astype(jnp.bfloat16)

    def project(slot, first=False):
        gain = gains[slot][0:1, :]
        column = pl.multiple_of((slot * 2 + core) * depth, depth)
        mine = own_rows[:, pl.ds(column, depth)].astype(jnp.float32)
        normed = (mine * own_inv[:, 0:1] * gain).astype(jnp.bfloat16)
        result = jnp.dot(normed, weights[slot], preferred_element_type=jnp.float32)
        total[0] = result if first else total[0] + result
        theirs = mate_rows[slot].astype(jnp.float32)
        normed = (theirs * mate_inv[:, 0:1] * gain).astype(jnp.bfloat16)
        result = jnp.dot(normed, weights[slot], preferred_element_type=jnp.float32)
        total[1] = result if first else total[1] + result

    def sides(d):
        return ((z + d < n_z, z + d, False), (z - d >= 0, z - d, True))

    def along_z(d, q, to_y, to_x):
        for valid, zz, up in sides(d):

            @pl.when(valid)
            def _(zz=zz, up=up):
                arrived(zz * 2 + y, q)
                pl.when(z < n_z - 1 if up else z > 0)(lambda: send_z(zz, q, up).start())
                if to_y:
                    send_y(zz, q).start()
                if to_x:
                    send_x(zz * 2 + y, q).start()

    def along_y(d, q):
        for valid, zz, _ in sides(d):

            @pl.when(valid)
            def _(zz=zz):
                slot = zz * 2 + 1 - y
                arrived(slot, q)
                send_x(slot, q).start()

    def finish(d):
        for valid, zz, _ in sides(d):

            @pl.when(valid)
            def _(zz=zz):
                arrived(zz * 2 + y, role_d)
                arrived(zz * 2 + 1 - y, role_d)
                arrived(zz * 2 + 1 - y, role_c)

                def one(i, carry):
                    project(zz * 2 + i)
                    return carry

                lax.fori_loop(0, 2, one, 0)

    for step in range(1, n_shards):
        peer = lax.rem(own + step, n_shards)
        pltpu.make_async_remote_copy(
            src_ref=gains.at[peer],
            dst_ref=gains.at[peer],
            send_sem=gain_send.at[step],
            recv_sem=gain_recv.at[peer],
            device_id=mate,
            device_id_type=MESH,
        ).wait_recv()
    send_inv.wait_recv()
    for s in range(n_shards):
        send_rows(s).wait_recv()

    along_z(1, role_a, True, True)
    project(own, first=True)
    along_z(1, role_b, True, False)
    along_z(1, role_c, False, False)
    for q in range(PIECES):
        arrived(z * 2 + 1 - y, q)
    project(z * 2 + 1 - y)
    for d in range(2, n_z):
        along_z(d, role_a, True, True)
        along_y(d - 1, role_a)
        along_z(d, role_b, True, False)
        along_y(d - 1, role_b)
        along_z(d, role_c, False, False)
        if d > 2:
            finish(d - 2)
    along_y(n_z - 1, role_a)
    along_y(n_z - 1, role_b)
    for d in range(max(1, n_z - 2), n_z):
        finish(d)

    def send_sum(c):
        cols = pl.ds(c * 256, 256)
        return pltpu.make_async_remote_copy(
            src_ref=total.at[1, :, cols],
            dst_ref=mate_total.at[:, cols],
            send_sem=sum_send.at[c],
            recv_sem=sum_recv.at[c],
            device_id=mate,
            device_id_type=MESH,
        )

    n_sums = n_cols // 256
    order = [n_sums - 1] + list(range(n_sums - 1))
    for c in order:
        send_sum(c).start()

    def rotated(values):
        return (values * cosine[...] + pltpu.roll(values, half, 1) * sine[...]).astype(jnp.bfloat16)

    def summed(col):
        return total[0, :, col : col + HD] + mate_total[:, col : col + HD]

    send_sum(n_sums - 1).wait_recv()
    key = rotated(summed(q_cols))
    value = summed(q_cols + HD).astype(jnp.bfloat16)

    def send_head(h):
        return pltpu.make_async_remote_copy(
            src_ref=sent_heads.at[h],
            dst_ref=got_heads.at[h],
            send_sem=head_send.at[h],
            recv_sem=head_recv.at[h],
            device_id=x_peer,
            device_id_type=MESH,
        )

    for h in range(QH):
        if h % 2 == 0:
            send_sum(h // 2).wait_recv()
        query = rotated(summed(h * HD))
        scores = lax.dot_general(
            query, key, (((1,), (1,)), ((), ())), preferred_element_type=jnp.float32
        ) * HD ** (-0.5)
        scores = jnp.where(masked[...] > 0.5, -1e30, scores)
        exped = jnp.exp(scores - jnp.max(scores, axis=1, keepdims=True))
        chance = (exped / jnp.sum(exped, axis=1, keepdims=True)).astype(jnp.bfloat16)
        mixed = jnp.dot(chance, value, preferred_element_type=jnp.float32).astype(jnp.bfloat16)
        cols = pl.ds(h * HD, HD)
        if n_dp == 2:
            sent_heads[h] = jnp.dot(
                place_there[...], mixed, preferred_element_type=jnp.float32
            ).astype(jnp.bfloat16)
            send_head(h).start()
            out_ref[:, cols] = jnp.dot(
                place_here[...], mixed, preferred_element_type=jnp.float32
            ).astype(jnp.bfloat16)
        else:
            out_ref[:, cols] = mixed

    for q in (role_a, role_b, role_c):
        pl.when(z < n_z - 1)(lambda q=q: send_z(z, q, True).wait_send())
        pl.when(z > 0)(lambda q=q: send_z(z, q, False).wait_send())
        send_y(z, q).wait_send()
    send_y(z, role_d).wait_send()
    for step in range(1, n_shards):
        send_gain(step).wait_send()
    for s in range(n_shards):
        send_rows(s).wait_send()
    send_inv.wait_send()
    for d in range(1, n_z):
        for valid, zz, up in sides(d):

            @pl.when(valid)
            def _(zz=zz, up=up):
                for q in (role_a, role_b, role_c):
                    pl.when(z < n_z - 1 if up else z > 0)(
                        lambda q=q: send_z(zz, q, up).wait_send()
                    )
                send_y(zz, role_a).wait_send()
                send_y(zz, role_b).wait_send()
                send_x(zz * 2 + y, role_a).wait_send()
                send_x(zz * 2 + 1 - y, role_a).wait_send()
                send_x(zz * 2 + 1 - y, role_b).wait_send()

    for c in order:
        send_sum(c).wait_send()
    if n_dp == 2:
        for h in range(QH):
            cols = pl.ds(h * HD, HD)
            send_head(h).wait_recv()
            out_ref[:, cols] = out_ref[:, cols] + got_heads[h]
        for h in range(QH):
            send_head(h).wait_send()


def fused(n_dp, n_fsdp, hidden, lengths, learner, slot_offset, norm_gain, query_weight, keyval_weight):
    tokens, width = hidden.shape
    depth, q_cols = query_weight.shape
    n_cols = q_cols + keyval_weight.shape[1]
    n_z = n_fsdp // 4
    n_shards = 2 * n_z
    bf16, f32 = jnp.bfloat16, jnp.float32
    dma = pltpu.SemaphoreType.DMA
    smem = pl.BlockSpec(memory_space=pltpu.SMEM)
    vmem = pl.BlockSpec(memory_space=pltpu.VMEM)
    anywhere = pl.BlockSpec(memory_space=pl.ANY)
    return pl.pallas_call(
        functools.partial(kernel, n_dp, n_fsdp),
        out_shape=jax.ShapeDtypeStruct((tokens, q_cols), bf16),
        in_specs=[smem, smem, smem, anywhere, vmem, anywhere, anywhere],
        out_specs=vmem,
        scratch_shapes=[
            pltpu.VMEM((n_shards, depth, n_cols), bf16),
            pltpu.VMEM((n_shards, 8, depth), f32),
            pltpu.VMEM((tokens, width), bf16),
            pltpu.VMEM((n_shards, tokens, depth), bf16),
            pltpu.VMEM((tokens, 128), f32),
            pltpu.VMEM((tokens, 128), f32),
            pltpu.VMEM((2, tokens, n_cols), f32),
            pltpu.VMEM((tokens, n_cols), f32),
            pltpu.VMEM((tokens, HD), f32),
            pltpu.VMEM((tokens, HD), f32),
            pltpu.VMEM((tokens, tokens), f32),
            pltpu.VMEM((tokens, tokens), bf16),
            pltpu.VMEM((tokens, tokens), bf16),
            pltpu.VMEM((QH, tokens, HD), bf16),
            pltpu.VMEM((QH, tokens, HD), bf16),
            dma((3,)),
            dma((n_shards, PIECES)),
            dma((2, n_z, PIECES)),
            dma((n_z, PIECES)),
            dma((n_shards, PIECES)),
            dma((n_shards,)),
            dma((n_shards,)),
            dma((n_shards,)),
            dma((n_shards,)),
            dma((2,)),
            dma((n_cols // 256,)),
            dma((n_cols // 256,)),
            dma((QH,)),
            dma((QH,)),
        ],
        compiler_params=pltpu.CompilerParams(
            collective_id=0, has_side_effects=True, vmem_limit_bytes=48 * 1024 * 1024
        ),
    )(lengths, learner, slot_offset, hidden, norm_gain.reshape(1, -1), query_weight, keyval_weight)


def route(buffer, tables):
    channels = buffer.shape[1]
    peer_count = lax.axis_size("dp")
    pair_count = tables.shape[1] // (2 * peer_count)
    block_len = buffer.shape[0] // pair_count
    slice_len = block_len // peer_count
    blocks = buffer.reshape(pair_count, peer_count, slice_len, channels)
    spread = lax.all_to_all(blocks, "dp", split_axis=1, concat_axis=0, tiled=True)
    lengths_all = tables[0].reshape(peer_count * pair_count, 2)
    targets = tables[1].reshape(peer_count * pair_count, 2)[:, 0]
    offsets_all = tables[2].reshape(peer_count * pair_count, 2)
    ordering = jnp.argsort(targets, stable=True)
    arranged = jnp.take(spread, ordering, axis=0).reshape(
        peer_count, pair_count, 1, slice_len, channels
    )
    received = lax.all_to_all(arranged, "dp", split_axis=0, concat_axis=2, tiled=True)
    received = received.reshape(pair_count * block_len, channels)
    own_blocks = lax.dynamic_slice_in_dim(ordering, lax.axis_index("dp") * pair_count, pair_count)
    pair_lengths = jnp.take(lengths_all, own_blocks, axis=0)
    sources = jnp.stack([jnp.zeros_like(pair_lengths[:, 0]), pair_lengths[:, 0]], axis=1)
    sources = (sources + (jnp.arange(pair_count, dtype=jnp.int32) * block_len)[:, None]).reshape(-1)
    row_lengths = pair_lengths.reshape(-1)
    row_offsets = jnp.take(offsets_all, own_blocks, axis=0).reshape(-1)
    places = jnp.arange(pair_count * block_len, dtype=jnp.int32)
    relative = places[:, None] - row_offsets[None, :]
    inside = (relative >= 0) & (relative < row_lengths[None, :])
    take_index = jnp.sum(jnp.where(inside, sources[None, :] + relative, 0), axis=1)
    return jnp.take(received, take_index, axis=0)


def solution(mesh):
    n_dp, n_fsdp = mesh.shape["dp"], mesh.shape["fsdp"]

    def shards(hidden, lengths, learner, slot_offset, norm_gain, query_weight, keyval_weight):
        attended = fused(
            n_dp, n_fsdp, hidden, lengths, learner, slot_offset, norm_gain, query_weight, keyval_weight
        )
        if n_dp == 2:
            return attended
        tables = lax.all_gather(
            jnp.stack([lengths, learner, slot_offset]), "dp", axis=1, tiled=True
        )
        return route(attended, tables)

    placed = (
        P(("dp", "fsdp"), None),
        P(("dp", "fsdp")),
        P(("dp", "fsdp")),
        P(("dp", "fsdp")),
        P("fsdp"),
        P("fsdp", None),
        P("fsdp", None),
    )
    return jax.shard_map(
        shards, mesh=mesh, in_specs=placed, out_specs=P(("dp", "fsdp"), None), check_vma=False
    )
```

```python
import functools
import math

import jax
import jax.numpy as jnp
from jax import lax
from jax.experimental import pallas as pl
from jax.experimental.pallas import tpu as pltpu
from jax.sharding import PartitionSpec as P

HD = 128
QH = 4
ROPE_BASE = 500000.0
NORM_EPS = 1e-05
MESH = pl.DeviceIdType.MESH
SUBS = 2


def kernel(
    n_dp,
    n_fsdp,
    lengths_hbm,
    learner_hbm,
    offset_hbm,
    hidden_ref,
    gain_ref,
    query_ref,
    keyval_ref,
    out_ref,
    lengths_ref,
    learner_ref,
    offset_ref,
    weights,
    gains,
    own_rows,
    mate_rows,
    own_inv,
    mate_inv,
    total,
    mate_total,
    cosine,
    sine,
    masked,
    place_here,
    place_there,
    sent_heads,
    got_heads,
    local_sem,
    part_recv,
    z_send,
    y_send,
    x_send,
    gain_send,
    gain_recv,
    rows_send,
    rows_recv,
    inv_sem,
    sum_send,
    sum_recv,
    head_send,
    head_recv,
):
    dp = lax.axis_index("dp")
    fs = lax.axis_index("fsdp")
    core = lax.rem(fs, 2)
    y = lax.rem(fs // 2, 2)
    z = fs // 4
    n_z = n_fsdp // 4
    x = lax.rem(dp, 2)
    x_peer = {"dp": dp + 1 - 2 * x}
    mate = {"fsdp": fs + 1 - 2 * core}
    y_peer = {"fsdp": fs + 2 - 4 * y}
    tokens = own_rows.shape[0]
    depth = query_ref.shape[0]
    n_cols = weights.shape[2]
    q_cols = QH * HD
    part = depth // (4 * SUBS)
    own = z * 2 + y
    other = z * 2 + 1 - y
    n_shards = 2 * n_z
    role_a = 3 * x
    role_b = 1 + x
    role_c = 2 - x
    role_d = 3 - 3 * x

    load_q = pltpu.make_async_copy(query_ref, weights.at[own, :, pl.ds(0, q_cols)], local_sem.at[0])
    load_kv = pltpu.make_async_copy(
        keyval_ref, weights.at[own, :, pl.ds(q_cols, n_cols - q_cols)], local_sem.at[1]
    )
    load_rows = pltpu.make_async_copy(hidden_ref, own_rows, local_sem.at[2])
    load_tables = [
        pltpu.make_async_copy(src, dst, local_sem.at[3 + i])
        for i, (src, dst) in enumerate(
            ((lengths_hbm, lengths_ref), (learner_hbm, learner_ref), (offset_hbm, offset_ref))
        )
    ]
    load_q.start()
    load_kv.start()
    load_rows.start()
    for load in load_tables:
        load.start()

    barrier = pltpu.get_barrier_semaphore()
    pl.semaphore_signal(barrier, inc=1, device_id=x_peer, device_id_type=MESH)
    pl.semaphore_signal(barrier, inc=1, device_id=mate, device_id_type=MESH)
    for step in range(1, n_shards):
        peer = lax.rem(own + step, n_shards)
        pl.semaphore_signal(
            barrier, inc=1, device_id={"fsdp": peer * 2 + core}, device_id_type=MESH
        )
    gains[own] = jnp.broadcast_to(gain_ref[...].astype(jnp.float32).reshape(1, depth), (8, depth))
    pl.semaphore_wait(barrier, n_shards + 1)

    def piece(slot, p):
        return weights.at[slot, pl.ds(pl.multiple_of(p * part, part), part), :]

    def send_z(zz, p, up):
        slot = zz * 2 + y
        return pltpu.make_async_remote_copy(
            src_ref=piece(slot, p),
            dst_ref=piece(slot, p),
            send_sem=z_send.at[up, zz, p],
            recv_sem=part_recv.at[slot, p],
            device_id={"fsdp": fs + 8 * up - 4},
            device_id_type=MESH,
        )

    def can_send(up):
        return (z + 2 * up - 1 >= 0) & (z + 2 * up - 1 < n_z)

    def send_y(zz, p):
        slot = zz * 2 + y
        return pltpu.make_async_remote_copy(
            src_ref=piece(slot, p),
            dst_ref=piece(slot, p),
            send_sem=y_send.at[zz, p],
            recv_sem=part_recv.at[slot, p],
            device_id=y_peer,
            device_id_type=MESH,
        )

    def send_x(slot, p):
        return pltpu.make_async_remote_copy(
            src_ref=piece(slot, p),
            dst_ref=piece(slot, p),
            send_sem=x_send.at[slot, p],
            recv_sem=part_recv.at[slot, p],
            device_id=x_peer,
            device_id_type=MESH,
        )

    def arrived(slot, p):
        send_x(slot, p).wait_recv()

    def send_gain(step):
        peer = lax.rem(own + step, n_shards)
        return pltpu.make_async_remote_copy(
            src_ref=gains.at[own],
            dst_ref=gains.at[own],
            send_sem=gain_send.at[step],
            recv_sem=gain_recv.at[own],
            device_id={"fsdp": peer * 2 + core},
            device_id_type=MESH,
        )

    def send_rows(s):
        start = pl.multiple_of((s * 2 + 1 - core) * depth, depth)
        return pltpu.make_async_remote_copy(
            src_ref=hidden_ref.at[:, pl.ds(start, depth)],
            dst_ref=mate_rows.at[s],
            send_sem=rows_send.at[s],
            recv_sem=rows_recv.at[s],
            device_id=mate,
            device_id_type=MESH,
        )

    send_inv = pltpu.make_async_remote_copy(
        src_ref=own_inv,
        dst_ref=mate_inv,
        send_sem=inv_sem.at[0],
        recv_sem=inv_sem.at[1],
        device_id=mate,
        device_id_type=MESH,
    )

    def each(count, body):
        def step(i, carry):
            body(i)
            return carry

        lax.fori_loop(0, count, step, 0)

    def own_z(q, act):
        def body(j):
            up = lax.rem(j, 2)
            pl.when(can_send(up))(lambda: act(send_z(z, q * SUBS + j // 2, up)))

        each(2 * SUBS, body)

    def own_y(q, act):
        each(SUBS, lambda j: act(send_y(z, q * SUBS + j)))

    def start(copy):
        copy.start()

    def sent(copy):
        copy.wait_send()

    def remote(d, body):
        def step(j):
            up = lax.rem(j, 2)
            zz = z + d - 2 * d * up
            pl.when((zz >= 0) & (zz < n_z))(lambda: body(j // 2, zz, up))

        each(2 * SUBS, step)

    def along_z(d, q, to_y, to_x):
        def body(sub, zz, up):
            p = q * SUBS + sub
            arrived(zz * 2 + y, p)
            pl.when(can_send(up))(lambda: send_z(zz, p, up).start())
            if to_y:
                send_y(zz, p).start()
            if to_x:
                send_x(zz * 2 + y, p).start()

        remote(d, body)

    def along_y(d, q):
        def body(sub, zz, up):
            p = q * SUBS + sub
            arrived(zz * 2 + 1 - y, p)
            send_x(zz * 2 + 1 - y, p).start()

        remote(d, body)

    load_q.wait()
    load_kv.wait()
    own_z(role_a, start)
    own_y(role_a, start)
    own_z(role_b, start)
    for step in range(1, n_shards):
        send_gain(step).start()
    for s in range(n_shards):
        send_rows(s).start()

    load_rows.wait()
    width = own_rows.shape[1]

    def square(i):
        rows = pl.ds(pl.multiple_of(i * 32, 32), 32)
        values = own_rows[rows, :].astype(jnp.float32)
        mean = jnp.sum(values * values, axis=1, keepdims=True) / width
        own_inv[rows, :] = jnp.broadcast_to(lax.rsqrt(mean + NORM_EPS), (32, 128))

    each(tokens // 32, square)
    send_inv.start()
    along_z(1, role_a, True, True)

    for load in load_tables:
        load.wait()
    n_rows = lengths_ref.shape[0]
    across = lax.broadcasted_iota(jnp.int32, (1, tokens), 1)
    down = lax.broadcasted_iota(jnp.int32, (tokens, 1), 0)
    row_across = jnp.zeros_like(across)
    row_down = jnp.zeros_like(down)
    start_down = jnp.zeros_like(down)
    target = jnp.zeros_like(across)
    goes_to = jnp.zeros_like(across)
    first = jnp.int32(0)
    for r in range(n_rows):
        in_across = across >= first
        in_down = down >= first
        row_across = jnp.where(in_across, r, row_across)
        row_down = jnp.where(in_down, r, row_down)
        start_down = jnp.where(in_down, first, start_down)
        target = jnp.where(in_across, offset_ref[r] + across - first, target)
        goes_to = jnp.where(in_across, learner_ref[r], goes_to)
        first = first + lengths_ref[r]
    position = (down - start_down).astype(jnp.float32)
    lane = lax.broadcasted_iota(jnp.int32, (1, HD), 1)
    half = HD // 2
    index = jnp.where(lane < half, lane, lane - half).astype(jnp.float32)
    angle = position * jnp.exp(index * (-2.0 * math.log(ROPE_BASE) / HD))
    cosine[...] = jnp.cos(angle)
    sine[...] = jnp.where(lane < half, -jnp.sin(angle), jnp.sin(angle))

    along_z(1, role_b, True, False)
    own_y(role_b, start)
    along_y(1, role_a)

    allowed = (row_across == row_down) & (across <= down)
    masked[...] = jnp.where(allowed, 0.0, 1.0)
    if n_dp == 2:
        slot_iota = lax.broadcasted_iota(jnp.int32, (tokens, tokens), 0)
        place_here[...] = jnp.where(
            slot_iota == jnp.where(goes_to == dp, target, -1), 1.0, 0.0
        ).astype(jnp.bfloat16)
        place_there[...] = jnp.where(
            slot_iota == jnp.where(goes_to == 1 - dp, target, -1), 1.0, 0.0
        ).astype(jnp.bfloat16)

    block = depth // 2

    def project(slot, h, whose):
        inner = pl.ds(pl.multiple_of(h * block, block), block)
        gain = gains[slot, 0:1, inner]
        if whose == 0:
            column = pl.multiple_of((slot * 2 + core) * depth + h * block, block)
            rows, inverse = own_rows[:, pl.ds(column, block)], own_inv[:, 0:1]
        else:
            rows, inverse = mate_rows[slot, :, inner], mate_inv[:, 0:1]
        normed = (rows.astype(jnp.float32) * inverse * gain).astype(jnp.bfloat16)
        total[whose] += jnp.dot(normed, weights[slot, inner, :], preferred_element_type=jnp.float32)

    def project_both(slot, h):
        project(slot, h, 1)
        project(slot, h, 0)

    def project_remote(d, column, h, quarters):
        def step(up):
            zz = z + d - 2 * d * up

            @pl.when((zz >= 0) & (zz < n_z))
            def _():
                slot = zz * 2 + (y if column == 0 else 1 - y)
                for q in quarters:
                    each(SUBS, lambda j: arrived(slot, q * SUBS + j))
                project_both(slot, h)

        each(2, step)

    for step in range(1, n_shards):
        peer = lax.rem(own + step, n_shards)
        pltpu.make_async_remote_copy(
            src_ref=gains.at[peer],
            dst_ref=gains.at[peer],
            send_sem=gain_send.at[step],
            recv_sem=gain_recv.at[peer],
            device_id=mate,
            device_id_type=MESH,
        ).wait_recv()
    along_z(2, role_a, True, True)
    along_y(1, role_b)
    send_inv.wait_recv()
    for s in range(n_shards):
        send_rows(s).wait_recv()
    total[...] = jnp.zeros_like(total)
    each(2, lambda h: project_both(own, h))
    along_z(2, role_b, True, False)
    own_y(role_c, start)
    own_z(role_c, start)
    along_y(2, role_a)
    for d in range(3, n_z):
        along_z(d, role_a, True, True)
        along_y(d - 1, role_b)
        along_z(d, role_b, True, False)
        along_y(d, role_a)
    own_y(role_d, start)
    project_remote(1, 0, x, ())
    along_z(1, role_c, False, False)
    project_remote(1, 1, x, ())
    along_y(n_z - 1, role_b)
    project_remote(2, 0, x, ())
    along_z(2, role_c, False, False)
    project_remote(2, 1, x, ())
    project_remote(1, 1, 1 - x, (role_d, role_c))
    for d in range(3, n_z):
        along_z(d, role_c, False, False)
    project_remote(1, 0, 1 - x, (role_d,))
    project_remote(2, 0, 1 - x, (role_d,))
    project_remote(2, 1, 1 - x, (role_d, role_c))
    for d in range(3, n_z):
        project_remote(d, 0, x, ())
        project_remote(d, 1, x, ())
        project_remote(d, 0, 1 - x, (role_d,))
    for q in (role_a, role_b):
        each(SUBS, lambda j: arrived(other, q * SUBS + j))
    project_both(other, x)
    for d in range(3, n_z):
        project_remote(d, 1, 1 - x, (role_d, role_c))
    for q in (role_c, role_d):
        each(SUBS, lambda j: arrived(other, q * SUBS + j))
    project(other, 1 - x, 1)

    def send_sum(c):
        cols = pl.ds(c * 256, 256)
        return pltpu.make_async_remote_copy(
            src_ref=total.at[1, :, cols],
            dst_ref=mate_total.at[:, cols],
            send_sem=sum_send.at[c],
            recv_sem=sum_recv.at[c],
            device_id=mate,
            device_id_type=MESH,
        )

    n_sums = n_cols // 256
    order = [n_sums - 1] + list(range(n_sums - 1))
    for c in order:
        send_sum(c).start()
    project(other, 1 - x, 0)

    def rotated(values):
        return (values * cosine[...] + pltpu.roll(values, half, 1) * sine[...]).astype(jnp.bfloat16)

    def summed(col):
        return total[0, :, col : col + HD] + mate_total[:, col : col + HD]

    send_sum(n_sums - 1).wait_recv()
    key = rotated(summed(q_cols))
    value = summed(q_cols + HD).astype(jnp.bfloat16)

    def send_head(h):
        return pltpu.make_async_remote_copy(
            src_ref=sent_heads.at[h],
            dst_ref=got_heads.at[h],
            send_sem=head_send.at[h],
            recv_sem=head_recv.at[h],
            device_id=x_peer,
            device_id_type=MESH,
        )

    for h in range(QH):
        if h % 2 == 0:
            send_sum(h // 2).wait_recv()
        query = rotated(summed(h * HD))
        scores = lax.dot_general(
            query, key, (((1,), (1,)), ((), ())), preferred_element_type=jnp.float32
        ) * HD ** (-0.5)
        scores = jnp.where(masked[...] > 0.5, -1e30, scores)
        exped = jnp.exp(scores - jnp.max(scores, axis=1, keepdims=True))
        chance = (exped / jnp.sum(exped, axis=1, keepdims=True)).astype(jnp.bfloat16)
        mixed = jnp.dot(chance, value, preferred_element_type=jnp.float32).astype(jnp.bfloat16)
        cols = pl.ds(h * HD, HD)
        if n_dp == 2:
            sent_heads[h] = jnp.dot(
                place_there[...], mixed, preferred_element_type=jnp.float32
            ).astype(jnp.bfloat16)
            send_head(h).start()
            out_ref[:, cols] = jnp.dot(
                place_here[...], mixed, preferred_element_type=jnp.float32
            ).astype(jnp.bfloat16)
        else:
            out_ref[:, cols] = mixed

    for q in (role_a, role_b, role_c):
        own_z(q, sent)
    for q in (role_a, role_b, role_c, role_d):
        own_y(q, sent)
    for step in range(1, n_shards):
        send_gain(step).wait_send()
    for s in range(n_shards):
        send_rows(s).wait_send()
    send_inv.wait_send()

    def relayed(sub, zz, up):
        a, b, c = (q * SUBS + sub for q in (role_a, role_b, role_c))
        for p in (a, b, c):
            pl.when(can_send(up))(lambda p=p: send_z(zz, p, up).wait_send())
        send_y(zz, a).wait_send()
        send_y(zz, b).wait_send()
        send_x(zz * 2 + y, a).wait_send()
        send_x(zz * 2 + 1 - y, a).wait_send()
        send_x(zz * 2 + 1 - y, b).wait_send()

    for d in range(1, n_z):
        remote(d, relayed)

    for c in order:
        send_sum(c).wait_send()
    if n_dp == 2:
        for h in range(QH):
            cols = pl.ds(h * HD, HD)
            send_head(h).wait_recv()
            out_ref[:, cols] = out_ref[:, cols] + got_heads[h]
        for h in range(QH):
            send_head(h).wait_send()


def fused(n_dp, n_fsdp, hidden, lengths, learner, slot_offset, norm_gain, query_weight, keyval_weight):
    tokens, width = hidden.shape
    depth, q_cols = query_weight.shape
    n_cols = q_cols + keyval_weight.shape[1]
    n_z = n_fsdp // 4
    n_shards = 2 * n_z
    bf16, f32 = jnp.bfloat16, jnp.float32
    dma = pltpu.SemaphoreType.DMA
    vmem = pl.BlockSpec(memory_space=pltpu.VMEM)
    anywhere = pl.BlockSpec(memory_space=pl.ANY)
    return pl.pallas_call(
        functools.partial(kernel, n_dp, n_fsdp),
        out_shape=jax.ShapeDtypeStruct((tokens, q_cols), bf16),
        in_specs=[anywhere, anywhere, anywhere, anywhere, vmem, anywhere, anywhere],
        out_specs=vmem,
        scratch_shapes=[
            pltpu.SMEM(lengths.shape, jnp.int32),
            pltpu.SMEM(lengths.shape, jnp.int32),
            pltpu.SMEM(lengths.shape, jnp.int32),
            pltpu.VMEM((n_shards, depth, n_cols), bf16),
            pltpu.VMEM((n_shards, 8, depth), f32),
            pltpu.VMEM((tokens, width), bf16),
            pltpu.VMEM((n_shards, tokens, depth), bf16),
            pltpu.VMEM((tokens, 128), f32),
            pltpu.VMEM((tokens, 128), f32),
            pltpu.VMEM((2, tokens, n_cols), f32),
            pltpu.VMEM((tokens, n_cols), f32),
            pltpu.VMEM((tokens, HD), f32),
            pltpu.VMEM((tokens, HD), f32),
            pltpu.VMEM((tokens, tokens), f32),
            pltpu.VMEM((tokens, tokens), bf16),
            pltpu.VMEM((tokens, tokens), bf16),
            pltpu.VMEM((QH, tokens, HD), bf16),
            pltpu.VMEM((QH, tokens, HD), bf16),
            dma((6,)),
            dma((n_shards, 4 * SUBS)),
            dma((2, n_z, 4 * SUBS)),
            dma((n_z, 4 * SUBS)),
            dma((n_shards, 4 * SUBS)),
            dma((n_shards,)),
            dma((n_shards,)),
            dma((n_shards,)),
            dma((n_shards,)),
            dma((2,)),
            dma((n_cols // 256,)),
            dma((n_cols // 256,)),
            dma((QH,)),
            dma((QH,)),
        ],
        compiler_params=pltpu.CompilerParams(
            collective_id=0, has_side_effects=True, vmem_limit_bytes=60 * 1024 * 1024
        ),
    )(lengths, learner, slot_offset, hidden, norm_gain, query_weight, keyval_weight)


def route(buffer, tables):
    channels = buffer.shape[1]
    peer_count = lax.axis_size("dp")
    pair_count = tables.shape[1] // (2 * peer_count)
    block_len = buffer.shape[0] // pair_count
    slice_len = block_len // peer_count
    blocks = buffer.reshape(pair_count, peer_count, slice_len, channels)
    spread = lax.all_to_all(blocks, "dp", split_axis=1, concat_axis=0, tiled=True)
    lengths_all = tables[0].reshape(peer_count * pair_count, 2)
    targets = tables[1].reshape(peer_count * pair_count, 2)[:, 0]
    offsets_all = tables[2].reshape(peer_count * pair_count, 2)
    ordering = jnp.argsort(targets, stable=True)
    arranged = jnp.take(spread, ordering, axis=0).reshape(
        peer_count, pair_count, 1, slice_len, channels
    )
    received = lax.all_to_all(arranged, "dp", split_axis=0, concat_axis=2, tiled=True)
    received = received.reshape(pair_count * block_len, channels)
    own_blocks = lax.dynamic_slice_in_dim(ordering, lax.axis_index("dp") * pair_count, pair_count)
    pair_lengths = jnp.take(lengths_all, own_blocks, axis=0)
    sources = jnp.stack([jnp.zeros_like(pair_lengths[:, 0]), pair_lengths[:, 0]], axis=1)
    sources = (sources + (jnp.arange(pair_count, dtype=jnp.int32) * block_len)[:, None]).reshape(-1)
    row_lengths = pair_lengths.reshape(-1)
    row_offsets = jnp.take(offsets_all, own_blocks, axis=0).reshape(-1)
    places = jnp.arange(pair_count * block_len, dtype=jnp.int32)
    relative = places[:, None] - row_offsets[None, :]
    inside = (relative >= 0) & (relative < row_lengths[None, :])
    take_index = jnp.sum(jnp.where(inside, sources[None, :] + relative, 0), axis=1)
    return jnp.take(received, take_index, axis=0)


def solution(mesh):
    n_dp, n_fsdp = mesh.shape["dp"], mesh.shape["fsdp"]

    def shards(hidden, lengths, learner, slot_offset, norm_gain, query_weight, keyval_weight):
        attended = fused(
            n_dp, n_fsdp, hidden, lengths, learner, slot_offset, norm_gain, query_weight, keyval_weight
        )
        if n_dp == 2:
            return attended
        tables = lax.all_gather(
            jnp.stack([lengths, learner, slot_offset]), "dp", axis=1, tiled=True
        )
        return route(attended, tables)

    placed = (
        P(("dp", "fsdp"), None),
        P(("dp", "fsdp")),
        P(("dp", "fsdp")),
        P(("dp", "fsdp")),
        P("fsdp"),
        P("fsdp", None),
        P("fsdp", None),
    )
    return jax.shard_map(
        shards, mesh=mesh, in_specs=placed, out_specs=P(("dp", "fsdp"), None), check_vma=False
    )
```

```python
import functools
import math

import jax
import jax.numpy as jnp
from jax import lax
from jax.experimental import pallas as pl
from jax.experimental.pallas import tpu as pltpu
from jax.sharding import PartitionSpec as P

HD = 128
QH = 4
ROPE_BASE = 500000.0
NORM_EPS = 1e-05
MESH = pl.DeviceIdType.MESH
SUBS = 2


def kernel(
    n_dp,
    n_fsdp,
    lengths_hbm,
    learner_hbm,
    offset_hbm,
    hidden_ref,
    gain_ref,
    query_ref,
    keyval_ref,
    out_ref,
    lengths_ref,
    learner_ref,
    offset_ref,
    weights,
    gains,
    own_rows,
    mate_rows,
    own_inv,
    mate_inv,
    total,
    mate_total,
    cosine,
    sine,
    masked,
    place_here,
    place_there,
    sent_heads,
    got_heads,
    local_sem,
    part_recv,
    z_send,
    y_send,
    x_send,
    gain_send,
    gain_recv,
    rows_send,
    rows_recv,
    inv_sem,
    sum_send,
    sum_recv,
    head_send,
    head_recv,
):
    dp = lax.axis_index("dp")
    fs = lax.axis_index("fsdp")
    core = lax.rem(fs, 2)
    y = lax.rem(fs // 2, 2)
    z = fs // 4
    n_z = n_fsdp // 4
    x = lax.rem(dp, 2)
    x_peer = {"dp": dp + 1 - 2 * x}
    mate = {"fsdp": fs + 1 - 2 * core}
    y_peer = {"fsdp": fs + 2 - 4 * y}
    tokens = own_rows.shape[0]
    depth = query_ref.shape[0]
    n_cols = weights.shape[2]
    q_cols = QH * HD
    part = depth // (4 * SUBS)
    own = z * 2 + y
    other = z * 2 + 1 - y
    n_shards = 2 * n_z
    role_a = 3 * x
    role_b = 1 + x
    role_c = 2 - x
    role_d = 3 - 3 * x

    def can_send(up):
        return (z + 2 * up - 1 >= 0) & (z + 2 * up - 1 < n_z)

    load_q = pltpu.make_async_copy(query_ref, weights.at[own, :, pl.ds(0, q_cols)], local_sem.at[0])
    load_kv = pltpu.make_async_copy(
        keyval_ref, weights.at[own, :, pl.ds(q_cols, n_cols - q_cols)], local_sem.at[1]
    )
    load_rows = pltpu.make_async_copy(hidden_ref, own_rows, local_sem.at[2])
    load_tables = [
        pltpu.make_async_copy(src, dst, local_sem.at[3 + i])
        for i, (src, dst) in enumerate(
            ((lengths_hbm, lengths_ref), (learner_hbm, learner_ref), (offset_hbm, offset_ref))
        )
    ]
    load_q.start()
    load_kv.start()
    load_rows.start()
    for load in load_tables:
        load.start()

    barrier = pltpu.get_barrier_semaphore()
    pl.semaphore_signal(barrier, inc=1, device_id=x_peer, device_id_type=MESH)
    pl.semaphore_signal(barrier, inc=1, device_id=mate, device_id_type=MESH)
    pl.semaphore_signal(barrier, inc=1, device_id=y_peer, device_id_type=MESH)
    for up in (0, 1):

        @pl.when(can_send(up))
        def _(up=up):
            pl.semaphore_signal(
                barrier, inc=1, device_id={"fsdp": fs + 8 * up - 4}, device_id_type=MESH
            )

    gains[own] = jnp.broadcast_to(gain_ref[...].astype(jnp.float32).reshape(1, depth), (8, depth))
    inner = (z > 0) & (z < n_z - 1)
    pl.semaphore_wait(barrier, jnp.where(inner, 5, 4))

    def piece(slot, p):
        return weights.at[slot, pl.ds(pl.multiple_of(p * part, part), part), :]

    def send_z(zz, p, up):
        slot = zz * 2 + y
        return pltpu.make_async_remote_copy(
            src_ref=piece(slot, p),
            dst_ref=piece(slot, p),
            send_sem=z_send.at[up, zz, p],
            recv_sem=part_recv.at[slot, p],
            device_id={"fsdp": fs + 8 * up - 4},
            device_id_type=MESH,
        )

    def send_y(zz, p):
        slot = zz * 2 + y
        return pltpu.make_async_remote_copy(
            src_ref=piece(slot, p),
            dst_ref=piece(slot, p),
            send_sem=y_send.at[zz, p],
            recv_sem=part_recv.at[slot, p],
            device_id=y_peer,
            device_id_type=MESH,
        )

    def send_x(slot, p):
        return pltpu.make_async_remote_copy(
            src_ref=piece(slot, p),
            dst_ref=piece(slot, p),
            send_sem=x_send.at[slot, p],
            recv_sem=part_recv.at[slot, p],
            device_id=x_peer,
            device_id_type=MESH,
        )

    def arrived(slot, p):
        send_x(slot, p).wait_recv()

    def send_gain(zz, device, sem):
        slot = zz * 2 + y
        return pltpu.make_async_remote_copy(
            src_ref=gains.at[slot],
            dst_ref=gains.at[slot],
            send_sem=sem,
            recv_sem=gain_recv.at[slot],
            device_id=device,
            device_id_type=MESH,
        )

    def gain_z(zz, up):
        return send_gain(zz, {"fsdp": fs + 8 * up - 4}, gain_send.at[up, zz])

    def gain_y(zz):
        return send_gain(zz, y_peer, gain_send.at[2, zz])

    def gain_arrived(slot):
        pltpu.make_async_remote_copy(
            src_ref=gains.at[slot],
            dst_ref=gains.at[slot],
            send_sem=gain_send.at[2, 0],
            recv_sem=gain_recv.at[slot],
            device_id=y_peer,
            device_id_type=MESH,
        ).wait_recv()

    def send_rows(s):
        start = pl.multiple_of((s * 2 + 1 - core) * depth, depth)
        return pltpu.make_async_remote_copy(
            src_ref=hidden_ref.at[:, pl.ds(start, depth)],
            dst_ref=mate_rows.at[s],
            send_sem=rows_send.at[s],
            recv_sem=rows_recv.at[s],
            device_id=mate,
            device_id_type=MESH,
        )

    send_inv = pltpu.make_async_remote_copy(
        src_ref=own_inv,
        dst_ref=mate_inv,
        send_sem=inv_sem.at[0],
        recv_sem=inv_sem.at[1],
        device_id=mate,
        device_id_type=MESH,
    )

    def each(count, body):
        def step(i, carry):
            body(i)
            return carry

        lax.fori_loop(0, count, step, 0)

    def own_z(q, act):
        def body(j):
            up = lax.rem(j, 2)
            pl.when(can_send(up))(lambda: act(send_z(z, q * SUBS + j // 2, up)))

        each(2 * SUBS, body)

    def own_y(q, act):
        each(SUBS, lambda j: act(send_y(z, q * SUBS + j)))

    def start(copy):
        copy.start()

    def sent(copy):
        copy.wait_send()

    def remote(d, body):
        def step(j):
            up = lax.rem(j, 2)
            zz = z + d - 2 * d * up
            pl.when((zz >= 0) & (zz < n_z))(lambda: body(j // 2, zz, up))

        each(2 * SUBS, step)

    def along_z(d, q, to_y, to_x):
        def body(sub, zz, up):
            p = q * SUBS + sub
            arrived(zz * 2 + y, p)
            pl.when(can_send(up))(lambda: send_z(zz, p, up).start())
            if to_y:
                send_y(zz, p).start()
            if to_x:
                send_x(zz * 2 + y, p).start()

        remote(d, body)

    def gain_along_z(d):
        def step(up):
            zz = z + d - 2 * d * up

            @pl.when((zz >= 0) & (zz < n_z))
            def _():
                gain_arrived(zz * 2 + y)
                pl.when(can_send(up))(lambda: gain_z(zz, up).start())
                gain_y(zz).start()

        each(2, step)

    def along_y(d, q):
        def body(sub, zz, up):
            p = q * SUBS + sub
            arrived(zz * 2 + 1 - y, p)
            send_x(zz * 2 + 1 - y, p).start()

        remote(d, body)

    load_q.wait()
    load_kv.wait()
    own_z(role_a, start)
    own_y(role_a, start)
    own_z(role_b, start)
    for up in (0, 1):
        pl.when(can_send(up))(lambda up=up: gain_z(z, up).start())
    gain_y(z).start()

    def rows_out(i):
        for k in (2 * i, 2 * i + 1):
            send_rows(lax.rem(own + k, n_shards)).start()

    rows_out(0)

    load_rows.wait()
    width = own_rows.shape[1]

    def square(i):
        rows = pl.ds(pl.multiple_of(i * 32, 32), 32)
        values = own_rows[rows, :].astype(jnp.float32)
        mean = jnp.sum(values * values, axis=1, keepdims=True) / width
        own_inv[rows, :] = jnp.broadcast_to(lax.rsqrt(mean + NORM_EPS), (32, 128))

    each(tokens // 32, square)
    send_inv.start()
    along_z(1, role_a, True, True)
    gain_along_z(1)
    rows_out(1)

    for load in load_tables:
        load.wait()
    n_rows = lengths_ref.shape[0]
    across = lax.broadcasted_iota(jnp.int32, (1, tokens), 1)
    down = lax.broadcasted_iota(jnp.int32, (tokens, 1), 0)
    row_across = jnp.zeros_like(across)
    row_down = jnp.zeros_like(down)
    start_down = jnp.zeros_like(down)
    target = jnp.zeros_like(across)
    goes_to = jnp.zeros_like(across)
    first = jnp.int32(0)
    for r in range(n_rows):
        in_across = across >= first
        in_down = down >= first
        row_across = jnp.where(in_across, r, row_across)
        row_down = jnp.where(in_down, r, row_down)
        start_down = jnp.where(in_down, first, start_down)
        target = jnp.where(in_across, offset_ref[r] + across - first, target)
        goes_to = jnp.where(in_across, learner_ref[r], goes_to)
        first = first + lengths_ref[r]
    position = (down - start_down).astype(jnp.float32)
    lane = lax.broadcasted_iota(jnp.int32, (1, HD), 1)
    half = HD // 2
    index = jnp.where(lane < half, lane, lane - half).astype(jnp.float32)
    angle = position * jnp.exp(index * (-2.0 * math.log(ROPE_BASE) / HD))
    cosine[...] = jnp.cos(angle)
    sine[...] = jnp.where(lane < half, -jnp.sin(angle), jnp.sin(angle))

    along_z(1, role_b, True, False)
    own_y(role_b, start)
    rows_out(2)
    along_y(1, role_a)
    for i in range(3, n_shards // 2):
        rows_out(i)

    allowed = (row_across == row_down) & (across <= down)
    masked[...] = jnp.where(allowed, 0.0, 1.0)
    if n_dp == 2:
        slot_iota = lax.broadcasted_iota(jnp.int32, (tokens, tokens), 0)
        place_here[...] = jnp.where(
            slot_iota == jnp.where(goes_to == dp, target, -1), 1.0, 0.0
        ).astype(jnp.bfloat16)
        place_there[...] = jnp.where(
            slot_iota == jnp.where(goes_to == 1 - dp, target, -1), 1.0, 0.0
        ).astype(jnp.bfloat16)

    block = depth // 2

    def project(slot, h, whose):
        inner = pl.ds(pl.multiple_of(h * block, block), block)
        gain = gains[slot, 0:1, inner]
        if whose == 0:
            column = pl.multiple_of((slot * 2 + core) * depth + h * block, block)
            rows, inverse = own_rows[:, pl.ds(column, block)], own_inv[:, 0:1]
        else:
            rows, inverse = mate_rows[slot, :, inner], mate_inv[:, 0:1]
        normed = (rows.astype(jnp.float32) * inverse * gain).astype(jnp.bfloat16)
        total[whose] += jnp.dot(normed, weights[slot, inner, :], preferred_element_type=jnp.float32)

    def project_both(slot, h):
        project(slot, h, 1)
        project(slot, h, 0)

    def project_remote(d, column, h, quarters):
        def step(up):
            zz = z + d - 2 * d * up

            @pl.when((zz >= 0) & (zz < n_z))
            def _():
                slot = zz * 2 + (y if column == 0 else 1 - y)
                for q in quarters:
                    each(SUBS, lambda j: arrived(slot, q * SUBS + j))
                project_both(slot, h)

        each(2, step)

    along_z(2, role_a, True, True)
    gain_along_z(2)
    along_y(1, role_b)
    along_z(2, role_b, True, False)
    own_y(role_c, start)
    own_z(role_c, start)
    send_inv.wait_recv()
    for s in range(n_shards):
        send_rows(s).wait_recv()
    total[...] = jnp.zeros_like(total)
    each(2, lambda h: project_both(own, h))
    along_y(2, role_a)
    for d in range(3, n_z):
        along_z(d, role_a, True, True)
        gain_along_z(d)
        along_y(d - 1, role_b)
        along_z(d, role_b, True, False)
        along_y(d, role_a)
    own_y(role_d, start)
    for zz in range(n_z):
        gain_arrived(zz * 2 + 1 - y)
    project_remote(1, 0, x, ())
    along_z(1, role_c, False, False)
    project_remote(1, 1, x, ())
    along_y(n_z - 1, role_b)
    project_remote(2, 0, x, ())
    along_z(2, role_c, False, False)
    project_remote(2, 1, x, ())
    project_remote(1, 1, 1 - x, (role_d, role_c))
    for d in range(3, n_z):
        along_z(d, role_c, False, False)
    project_remote(1, 0, 1 - x, (role_d,))
    project_remote(2, 0, 1 - x, (role_d,))
    project_remote(2, 1, 1 - x, (role_d, role_c))
    for d in range(3, n_z):
        project_remote(d, 0, x, ())
        project_remote(d, 1, x, ())
        project_remote(d, 0, 1 - x, (role_d,))
    for q in (role_a, role_b):
        each(SUBS, lambda j: arrived(other, q * SUBS + j))
    project_both(other, x)
    for d in range(3, n_z):
        project_remote(d, 1, 1 - x, (role_d, role_c))
    for q in (role_c, role_d):
        each(SUBS, lambda j: arrived(other, q * SUBS + j))
    project(other, 1 - x, 1)

    def send_sum(c):
        cols = pl.ds(c * 256, 256)
        return pltpu.make_async_remote_copy(
            src_ref=total.at[1, :, cols],
            dst_ref=mate_total.at[:, cols],
            send_sem=sum_send.at[c],
            recv_sem=sum_recv.at[c],
            device_id=mate,
            device_id_type=MESH,
        )

    n_sums = n_cols // 256
    order = [n_sums - 1] + list(range(n_sums - 1))
    for c in order:
        send_sum(c).start()
    project(other, 1 - x, 0)

    def rotated(values):
        return (values * cosine[...] + pltpu.roll(values, half, 1) * sine[...]).astype(jnp.bfloat16)

    def summed(col):
        return total[0, :, col : col + HD] + mate_total[:, col : col + HD]

    send_sum(n_sums - 1).wait_recv()
    key = rotated(summed(q_cols))
    value = summed(q_cols + HD).astype(jnp.bfloat16)

    def send_head(h):
        return pltpu.make_async_remote_copy(
            src_ref=sent_heads.at[h],
            dst_ref=got_heads.at[h],
            send_sem=head_send.at[h],
            recv_sem=head_recv.at[h],
            device_id=x_peer,
            device_id_type=MESH,
        )

    for h in range(QH):
        if h % 2 == 0:
            send_sum(h // 2).wait_recv()
        query = rotated(summed(h * HD))
        scores = lax.dot_general(
            query, key, (((1,), (1,)), ((), ())), preferred_element_type=jnp.float32
        ) * HD ** (-0.5)
        scores = jnp.where(masked[...] > 0.5, -1e30, scores)
        exped = jnp.exp(scores - jnp.max(scores, axis=1, keepdims=True))
        chance = (exped / jnp.sum(exped, axis=1, keepdims=True)).astype(jnp.bfloat16)
        mixed = jnp.dot(chance, value, preferred_element_type=jnp.float32).astype(jnp.bfloat16)
        cols = pl.ds(h * HD, HD)
        if n_dp == 2:
            sent_heads[h] = jnp.dot(
                place_there[...], mixed, preferred_element_type=jnp.float32
            ).astype(jnp.bfloat16)
            send_head(h).start()
            out_ref[:, cols] = jnp.dot(
                place_here[...], mixed, preferred_element_type=jnp.float32
            ).astype(jnp.bfloat16)
        else:
            out_ref[:, cols] = mixed

    for q in (role_a, role_b, role_c):
        own_z(q, sent)
    for q in (role_a, role_b, role_c, role_d):
        own_y(q, sent)
    for zz in range(n_z):
        pl.when(can_send(0) & (zz >= z))(lambda zz=zz: gain_z(zz, 0).wait_send())
        pl.when(can_send(1) & (zz <= z))(lambda zz=zz: gain_z(zz, 1).wait_send())
        gain_y(zz).wait_send()
    for s in range(n_shards):
        send_rows(s).wait_send()
    send_inv.wait_send()

    def relayed(sub, zz, up):
        a, b, c = (q * SUBS + sub for q in (role_a, role_b, role_c))
        for p in (a, b, c):
            pl.when(can_send(up))(lambda p=p: send_z(zz, p, up).wait_send())
        send_y(zz, a).wait_send()
        send_y(zz, b).wait_send()
        send_x(zz * 2 + y, a).wait_send()
        send_x(zz * 2 + 1 - y, a).wait_send()
        send_x(zz * 2 + 1 - y, b).wait_send()

    for d in range(1, n_z):
        remote(d, relayed)

    for c in order:
        send_sum(c).wait_send()
    if n_dp == 2:
        for h in range(QH):
            cols = pl.ds(h * HD, HD)
            send_head(h).wait_recv()
            out_ref[:, cols] = out_ref[:, cols] + got_heads[h]
        for h in range(QH):
            send_head(h).wait_send()


def fused(n_dp, n_fsdp, hidden, lengths, learner, slot_offset, norm_gain, query_weight, keyval_weight):
    tokens, width = hidden.shape
    depth, q_cols = query_weight.shape
    n_cols = q_cols + keyval_weight.shape[1]
    n_z = n_fsdp // 4
    n_shards = 2 * n_z
    bf16, f32 = jnp.bfloat16, jnp.float32
    dma = pltpu.SemaphoreType.DMA
    vmem = pl.BlockSpec(memory_space=pltpu.VMEM)
    hbm = pl.BlockSpec(memory_space=pl.ANY)
    return pl.pallas_call(
        functools.partial(kernel, n_dp, n_fsdp),
        out_shape=jax.ShapeDtypeStruct((tokens, q_cols), bf16),
        in_specs=[hbm, hbm, hbm, hbm, vmem, hbm, hbm],
        out_specs=vmem,
        scratch_shapes=[
            pltpu.SMEM(lengths.shape, jnp.int32),
            pltpu.SMEM(lengths.shape, jnp.int32),
            pltpu.SMEM(lengths.shape, jnp.int32),
            pltpu.VMEM((n_shards, depth, n_cols), bf16),
            pltpu.VMEM((n_shards, 8, depth), f32),
            pltpu.VMEM((tokens, width), bf16),
            pltpu.VMEM((n_shards, tokens, depth), bf16),
            pltpu.VMEM((tokens, 128), f32),
            pltpu.VMEM((tokens, 128), f32),
            pltpu.VMEM((2, tokens, n_cols), f32),
            pltpu.VMEM((tokens, n_cols), f32),
            pltpu.VMEM((tokens, HD), f32),
            pltpu.VMEM((tokens, HD), f32),
            pltpu.VMEM((tokens, tokens), f32),
            pltpu.VMEM((tokens, tokens), bf16),
            pltpu.VMEM((tokens, tokens), bf16),
            pltpu.VMEM((QH, tokens, HD), bf16),
            pltpu.VMEM((QH, tokens, HD), bf16),
            dma((6,)),
            dma((n_shards, 4 * SUBS)),
            dma((2, n_z, 4 * SUBS)),
            dma((n_z, 4 * SUBS)),
            dma((n_shards, 4 * SUBS)),
            dma((3, n_z)),
            dma((n_shards,)),
            dma((n_shards,)),
            dma((n_shards,)),
            dma((2,)),
            dma((n_cols // 256,)),
            dma((n_cols // 256,)),
            dma((QH,)),
            dma((QH,)),
        ],
        compiler_params=pltpu.CompilerParams(
            collective_id=0, has_side_effects=True, vmem_limit_bytes=60 * 1024 * 1024
        ),
    )(lengths, learner, slot_offset, hidden, norm_gain, query_weight, keyval_weight)


def route(buffer, tables):
    channels = buffer.shape[1]
    peer_count = lax.axis_size("dp")
    pair_count = tables.shape[1] // (2 * peer_count)
    block_len = buffer.shape[0] // pair_count
    slice_len = block_len // peer_count
    blocks = buffer.reshape(pair_count, peer_count, slice_len, channels)
    spread = lax.all_to_all(blocks, "dp", split_axis=1, concat_axis=0, tiled=True)
    lengths_all = tables[0].reshape(peer_count * pair_count, 2)
    targets = tables[1].reshape(peer_count * pair_count, 2)[:, 0]
    offsets_all = tables[2].reshape(peer_count * pair_count, 2)
    ordering = jnp.argsort(targets, stable=True)
    arranged = jnp.take(spread, ordering, axis=0).reshape(
        peer_count, pair_count, 1, slice_len, channels
    )
    received = lax.all_to_all(arranged, "dp", split_axis=0, concat_axis=2, tiled=True)
    received = received.reshape(pair_count * block_len, channels)
    own_blocks = lax.dynamic_slice_in_dim(ordering, lax.axis_index("dp") * pair_count, pair_count)
    pair_lengths = jnp.take(lengths_all, own_blocks, axis=0)
    sources = jnp.stack([jnp.zeros_like(pair_lengths[:, 0]), pair_lengths[:, 0]], axis=1)
    sources = (sources + (jnp.arange(pair_count, dtype=jnp.int32) * block_len)[:, None]).reshape(-1)
    row_lengths = pair_lengths.reshape(-1)
    row_offsets = jnp.take(offsets_all, own_blocks, axis=0).reshape(-1)
    places = jnp.arange(pair_count * block_len, dtype=jnp.int32)
    relative = places[:, None] - row_offsets[None, :]
    inside = (relative >= 0) & (relative < row_lengths[None, :])
    take_index = jnp.sum(jnp.where(inside, sources[None, :] + relative, 0), axis=1)
    return jnp.take(received, take_index, axis=0)


def solution(mesh):
    n_dp, n_fsdp = mesh.shape["dp"], mesh.shape["fsdp"]

    def shards(hidden, lengths, learner, slot_offset, norm_gain, query_weight, keyval_weight):
        attended = fused(
            n_dp, n_fsdp, hidden, lengths, learner, slot_offset, norm_gain, query_weight, keyval_weight
        )
        if n_dp == 2:
            return attended
        tables = lax.all_gather(
            jnp.stack([lengths, learner, slot_offset]), "dp", axis=1, tiled=True
        )
        return route(attended, tables)

    placed = (
        P(("dp", "fsdp"), None),
        P(("dp", "fsdp")),
        P(("dp", "fsdp")),
        P(("dp", "fsdp")),
        P("fsdp"),
        P("fsdp", None),
        P("fsdp", None),
    )
    return jax.shard_map(
        shards, mesh=mesh, in_specs=placed, out_specs=P(("dp", "fsdp"), None), check_vma=False
    )
```

```python
import functools
import math

import jax
import jax.numpy as jnp
from jax import lax
from jax.experimental import pallas as pl
from jax.experimental.pallas import tpu as pltpu
from jax.sharding import PartitionSpec as P

HD = 128
QH = 4
ROPE_BASE = 500000.0
NORM_EPS = 1e-05
MESH = pl.DeviceIdType.MESH
SUBS = 2


def kernel(
    n_dp,
    n_fsdp,
    lengths_hbm,
    learner_hbm,
    offset_hbm,
    hidden_ref,
    gain_ref,
    query_ref,
    keyval_ref,
    out_ref,
    lengths_ref,
    learner_ref,
    offset_ref,
    weights,
    gains,
    own_rows,
    mate_rows,
    own_inv,
    mate_inv,
    total,
    mate_total,
    cosine,
    sine,
    masked,
    place_here,
    place_there,
    sent_heads,
    got_heads,
    local_sem,
    part_recv,
    z_send,
    y_send,
    x_send,
    gain_send,
    gain_recv,
    rows_send,
    rows_recv,
    inv_sem,
    sum_send,
    sum_recv,
    head_send,
    head_recv,
):
    dp = lax.axis_index("dp")
    fs = lax.axis_index("fsdp")
    core = lax.rem(fs, 2)
    y = lax.rem(fs // 2, 2)
    z = fs // 4
    n_z = n_fsdp // 4
    x = lax.rem(dp, 2)
    x_peer = {"dp": dp + 1 - 2 * x}
    mate = {"fsdp": fs + 1 - 2 * core}
    y_peer = {"fsdp": fs + 2 - 4 * y}
    tokens = own_rows.shape[0]
    depth = query_ref.shape[0]
    n_cols = weights.shape[2]
    q_cols = QH * HD
    part = depth // (4 * SUBS)
    own = z * 2 + y
    other = z * 2 + 1 - y
    n_shards = 2 * n_z
    role_a = 3 * x
    role_b = 1 + x
    role_c = 2 - x
    role_d = 3 - 3 * x

    def can_send(up):
        return (z + 2 * up - 1 >= 0) & (z + 2 * up - 1 < n_z)

    load_q = pltpu.make_async_copy(query_ref, weights.at[own, :, pl.ds(0, q_cols)], local_sem.at[0])
    load_kv = pltpu.make_async_copy(
        keyval_ref, weights.at[own, :, pl.ds(q_cols, n_cols - q_cols)], local_sem.at[1]
    )
    load_rows = pltpu.make_async_copy(hidden_ref, own_rows, local_sem.at[2])
    load_tables = [
        pltpu.make_async_copy(src, dst, local_sem.at[3 + i])
        for i, (src, dst) in enumerate(
            ((lengths_hbm, lengths_ref), (learner_hbm, learner_ref), (offset_hbm, offset_ref))
        )
    ]
    load_q.start()
    load_kv.start()
    load_rows.start()
    for load in load_tables:
        load.start()

    barrier = pltpu.get_barrier_semaphore()
    pl.semaphore_signal(barrier, inc=1, device_id=x_peer, device_id_type=MESH)
    pl.semaphore_signal(barrier, inc=1, device_id=mate, device_id_type=MESH)
    pl.semaphore_signal(barrier, inc=1, device_id=y_peer, device_id_type=MESH)
    for up in (0, 1):

        @pl.when(can_send(up))
        def _(up=up):
            pl.semaphore_signal(
                barrier, inc=1, device_id={"fsdp": fs + 8 * up - 4}, device_id_type=MESH
            )

    gains[own] = jnp.broadcast_to(gain_ref[...].astype(jnp.float32).reshape(1, depth), (8, depth))
    inner = (z > 0) & (z < n_z - 1)
    pl.semaphore_wait(barrier, jnp.where(inner, 5, 4))

    def piece(slot, p):
        return weights.at[slot, pl.ds(pl.multiple_of(p * part, part), part), :]

    def send_z(zz, p, up):
        slot = zz * 2 + y
        return pltpu.make_async_remote_copy(
            src_ref=piece(slot, p),
            dst_ref=piece(slot, p),
            send_sem=z_send.at[up, zz, p],
            recv_sem=part_recv.at[slot, p],
            device_id={"fsdp": fs + 8 * up - 4},
            device_id_type=MESH,
        )

    def send_y(zz, p):
        slot = zz * 2 + y
        return pltpu.make_async_remote_copy(
            src_ref=piece(slot, p),
            dst_ref=piece(slot, p),
            send_sem=y_send.at[zz, p],
            recv_sem=part_recv.at[slot, p],
            device_id=y_peer,
            device_id_type=MESH,
        )

    def send_x(slot, p):
        return pltpu.make_async_remote_copy(
            src_ref=piece(slot, p),
            dst_ref=piece(slot, p),
            send_sem=x_send.at[slot, p],
            recv_sem=part_recv.at[slot, p],
            device_id=x_peer,
            device_id_type=MESH,
        )

    def arrived(slot, p):
        send_x(slot, p).wait_recv()

    def send_gain(zz, device, sem):
        slot = zz * 2 + y
        return pltpu.make_async_remote_copy(
            src_ref=gains.at[slot],
            dst_ref=gains.at[slot],
            send_sem=sem,
            recv_sem=gain_recv.at[slot],
            device_id=device,
            device_id_type=MESH,
        )

    def gain_z(zz, up):
        return send_gain(zz, {"fsdp": fs + 8 * up - 4}, gain_send.at[up, zz])

    def gain_y(zz):
        return send_gain(zz, y_peer, gain_send.at[2, zz])

    def gain_arrived(slot):
        pltpu.make_async_remote_copy(
            src_ref=gains.at[slot],
            dst_ref=gains.at[slot],
            send_sem=gain_send.at[2, 0],
            recv_sem=gain_recv.at[slot],
            device_id=y_peer,
            device_id_type=MESH,
        ).wait_recv()

    def send_rows(s):
        start = pl.multiple_of((s * 2 + 1 - core) * depth, depth)
        return pltpu.make_async_remote_copy(
            src_ref=hidden_ref.at[:, pl.ds(start, depth)],
            dst_ref=mate_rows.at[s],
            send_sem=rows_send.at[s],
            recv_sem=rows_recv.at[s],
            device_id=mate,
            device_id_type=MESH,
        )

    send_inv = pltpu.make_async_remote_copy(
        src_ref=own_inv,
        dst_ref=mate_inv,
        send_sem=inv_sem.at[0],
        recv_sem=inv_sem.at[1],
        device_id=mate,
        device_id_type=MESH,
    )

    def each(count, body):
        def step(i, carry):
            body(i)
            return carry

        lax.fori_loop(0, count, step, 0)

    def own_z(q, act):
        def body(j):
            up = lax.rem(j, 2)
            pl.when(can_send(up))(lambda: act(send_z(z, q * SUBS + j // 2, up)))

        each(2 * SUBS, body)

    def own_y(q, act):
        each(SUBS, lambda j: act(send_y(z, q * SUBS + j)))

    def start(copy):
        copy.start()

    def sent(copy):
        copy.wait_send()

    def remote(d, body):
        def step(j):
            up = lax.rem(j, 2)
            zz = z + d - 2 * d * up
            pl.when((zz >= 0) & (zz < n_z))(lambda: body(j // 2, zz, up))

        each(2 * SUBS, step)

    def along_z(d, q, to_y, to_x):
        def body(sub, zz, up):
            p = q * SUBS + sub
            arrived(zz * 2 + y, p)
            pl.when(can_send(up))(lambda: send_z(zz, p, up).start())
            if to_y:
                send_y(zz, p).start()
            if to_x:
                send_x(zz * 2 + y, p).start()

        remote(d, body)

    def gain_along_z(d):
        def step(up):
            zz = z + d - 2 * d * up

            @pl.when((zz >= 0) & (zz < n_z))
            def _():
                gain_arrived(zz * 2 + y)
                pl.when(can_send(up))(lambda: gain_z(zz, up).start())
                gain_y(zz).start()

        each(2, step)

    def along_y(d, q):
        def body(sub, zz, up):
            p = q * SUBS + sub
            arrived(zz * 2 + 1 - y, p)
            send_x(zz * 2 + 1 - y, p).start()

        remote(d, body)

    load_q.wait()
    load_kv.wait()
    own_z(role_a, start)
    own_y(role_a, start)
    own_z(role_b, start)
    for up in (0, 1):
        pl.when(can_send(up))(lambda up=up: gain_z(z, up).start())
    gain_y(z).start()

    def rows_out(i):
        for k in (2 * i, 2 * i + 1):
            send_rows(lax.rem(own + k, n_shards)).start()

    rows_out(0)

    load_rows.wait()
    width = own_rows.shape[1]

    def square(i):
        rows = pl.ds(pl.multiple_of(i * 32, 32), 32)
        values = own_rows[rows, :].astype(jnp.float32)
        mean = jnp.sum(values * values, axis=1, keepdims=True) / width
        own_inv[rows, :] = jnp.broadcast_to(lax.rsqrt(mean + NORM_EPS), (32, 128))

    each(tokens // 32, square)
    send_inv.start()
    rows_out(1)

    for load in load_tables:
        load.wait()
    n_rows = lengths_ref.shape[0]
    across = lax.broadcasted_iota(jnp.int32, (1, tokens), 1)
    down = lax.broadcasted_iota(jnp.int32, (tokens, 1), 0)
    row_across = jnp.zeros_like(across)
    row_down = jnp.zeros_like(down)
    start_down = jnp.zeros_like(down)
    target = jnp.zeros_like(across)
    goes_to = jnp.zeros_like(across)
    first = jnp.int32(0)
    for r in range(n_rows):
        in_across = across >= first
        in_down = down >= first
        row_across = jnp.where(in_across, r, row_across)
        row_down = jnp.where(in_down, r, row_down)
        start_down = jnp.where(in_down, first, start_down)
        target = jnp.where(in_across, offset_ref[r] + across - first, target)
        goes_to = jnp.where(in_across, learner_ref[r], goes_to)
        first = first + lengths_ref[r]
    position = (down - start_down).astype(jnp.float32)
    lane = lax.broadcasted_iota(jnp.int32, (1, HD), 1)
    half = HD // 2
    index = jnp.where(lane < half, lane, lane - half).astype(jnp.float32)
    angle = position * jnp.exp(index * (-2.0 * math.log(ROPE_BASE) / HD))
    cosine[...] = jnp.cos(angle)
    sine[...] = jnp.where(lane < half, -jnp.sin(angle), jnp.sin(angle))

    along_z(1, role_a, True, True)
    gain_along_z(1)
    rows_out(2)
    for i in range(3, n_shards // 2):
        rows_out(i)

    allowed = (row_across == row_down) & (across <= down)
    masked[...] = jnp.where(allowed, 0.0, 1.0)
    if n_dp == 2:
        slot_iota = lax.broadcasted_iota(jnp.int32, (tokens, tokens), 0)
        place_here[...] = jnp.where(
            slot_iota == jnp.where(goes_to == dp, target, -1), 1.0, 0.0
        ).astype(jnp.bfloat16)
        place_there[...] = jnp.where(
            slot_iota == jnp.where(goes_to == 1 - dp, target, -1), 1.0, 0.0
        ).astype(jnp.bfloat16)

    block = depth // 2

    def project(slot, h, whose):
        inner = pl.ds(pl.multiple_of(h * block, block), block)
        gain = gains[slot, 0:1, inner]
        if whose == 0:
            column = pl.multiple_of((slot * 2 + core) * depth + h * block, block)
            rows, inverse = own_rows[:, pl.ds(column, block)], own_inv[:, 0:1]
        else:
            rows, inverse = mate_rows[slot, :, inner], mate_inv[:, 0:1]
        normed = (rows.astype(jnp.float32) * inverse * gain).astype(jnp.bfloat16)
        total[whose] += jnp.dot(normed, weights[slot, inner, :], preferred_element_type=jnp.float32)

    def project_both(slot, h):
        project(slot, h, 1)
        project(slot, h, 0)

    def project_remote(d, column, h, quarters):
        def step(up):
            zz = z + d - 2 * d * up

            @pl.when((zz >= 0) & (zz < n_z))
            def _():
                slot = zz * 2 + (y if column == 0 else 1 - y)
                for q in quarters:
                    each(SUBS, lambda j: arrived(slot, q * SUBS + j))
                project_both(slot, h)

        each(2, step)

    along_z(1, role_b, True, False)
    own_z(role_c, start)
    own_y(role_b, start)
    along_y(1, role_a)
    along_z(2, role_a, True, True)
    gain_along_z(2)
    along_y(1, role_b)
    total[...] = jnp.zeros_like(total)
    send_inv.wait_recv()
    for s in range(n_shards):
        send_rows(s).wait_recv()
    project_both(own, 0)
    along_z(2, role_b, True, False)
    own_y(role_c, start)
    project_both(own, 1)
    along_y(2, role_a)
    along_z(1, role_c, False, False)
    project_remote(1, 0, x, ())
    for d in range(3, n_z):
        along_z(d, role_a, True, True)
        gain_along_z(d)
        along_y(d - 1, role_b)
        along_z(d, role_b, True, False)
    along_z(2, role_c, False, False)
    own_y(role_d, start)
    for zz in range(n_z):
        gain_arrived(zz * 2 + 1 - y)
    project_remote(1, 1, x, ())
    for d in range(3, n_z):
        along_y(d, role_a)
    project_remote(2, 0, x, ())
    along_y(n_z - 1, role_b)
    project_remote(2, 1, x, ())
    project_remote(1, 1, 1 - x, (role_d, role_c))
    project_remote(1, 0, 1 - x, (role_d,))
    for d in range(3, n_z):
        project_remote(d, 0, x, ())
        project_remote(d, 1, x, ())
        along_z(d, role_c, False, False)
    project_remote(2, 0, 1 - x, (role_d,))
    project_remote(2, 1, 1 - x, (role_d, role_c))
    for q in (role_a, role_b):
        each(SUBS, lambda j: arrived(other, q * SUBS + j))
    project_both(other, x)
    for d in range(3, n_z):
        project_remote(d, 0, 1 - x, (role_d,))
    for d in range(3, n_z):
        project_remote(d, 1, 1 - x, (role_d, role_c))
    for q in (role_c, role_d):
        each(SUBS, lambda j: arrived(other, q * SUBS + j))
    project(other, 1 - x, 1)

    def send_sum(c):
        cols = pl.ds(c * 256, 256)
        return pltpu.make_async_remote_copy(
            src_ref=total.at[1, :, cols],
            dst_ref=mate_total.at[:, cols],
            send_sem=sum_send.at[c],
            recv_sem=sum_recv.at[c],
            device_id=mate,
            device_id_type=MESH,
        )

    n_sums = n_cols // 256
    order = [n_sums - 1] + list(range(n_sums - 1))
    for c in order:
        send_sum(c).start()
    project(other, 1 - x, 0)

    def rotated(values):
        return (values * cosine[...] + pltpu.roll(values, half, 1) * sine[...]).astype(jnp.bfloat16)

    def summed(col):
        return total[0, :, col : col + HD] + mate_total[:, col : col + HD]

    send_sum(n_sums - 1).wait_recv()
    key = rotated(summed(q_cols))
    value = summed(q_cols + HD).astype(jnp.bfloat16)

    def send_head(h):
        return pltpu.make_async_remote_copy(
            src_ref=sent_heads.at[h],
            dst_ref=got_heads.at[h],
            send_sem=head_send.at[h],
            recv_sem=head_recv.at[h],
            device_id=x_peer,
            device_id_type=MESH,
        )

    for h in range(QH):
        if h % 2 == 0:
            send_sum(h // 2).wait_recv()
        query = rotated(summed(h * HD))
        scores = lax.dot_general(
            query, key, (((1,), (1,)), ((), ())), preferred_element_type=jnp.float32
        ) * HD ** (-0.5)
        scores = jnp.where(masked[...] > 0.5, -1e30, scores)
        exped = jnp.exp(scores - jnp.max(scores, axis=1, keepdims=True))
        chance = (exped / jnp.sum(exped, axis=1, keepdims=True)).astype(jnp.bfloat16)
        mixed = jnp.dot(chance, value, preferred_element_type=jnp.float32).astype(jnp.bfloat16)
        cols = pl.ds(h * HD, HD)
        if n_dp == 2:
            sent_heads[h] = jnp.dot(
                place_there[...], mixed, preferred_element_type=jnp.float32
            ).astype(jnp.bfloat16)
            send_head(h).start()
            out_ref[:, cols] = jnp.dot(
                place_here[...], mixed, preferred_element_type=jnp.float32
            ).astype(jnp.bfloat16)
        else:
            out_ref[:, cols] = mixed

    for q in (role_a, role_b, role_c):
        own_z(q, sent)
    for q in (role_a, role_b, role_c, role_d):
        own_y(q, sent)
    for zz in range(n_z):
        pl.when(can_send(0) & (zz >= z))(lambda zz=zz: gain_z(zz, 0).wait_send())
        pl.when(can_send(1) & (zz <= z))(lambda zz=zz: gain_z(zz, 1).wait_send())
        gain_y(zz).wait_send()
    for s in range(n_shards):
        send_rows(s).wait_send()
    send_inv.wait_send()

    def relayed(sub, zz, up):
        a, b, c = (q * SUBS + sub for q in (role_a, role_b, role_c))
        for p in (a, b, c):
            pl.when(can_send(up))(lambda p=p: send_z(zz, p, up).wait_send())
        send_y(zz, a).wait_send()
        send_y(zz, b).wait_send()
        send_x(zz * 2 + y, a).wait_send()
        send_x(zz * 2 + 1 - y, a).wait_send()
        send_x(zz * 2 + 1 - y, b).wait_send()

    for d in range(1, n_z):
        remote(d, relayed)

    for c in order:
        send_sum(c).wait_send()
    if n_dp == 2:
        for h in range(QH):
            cols = pl.ds(h * HD, HD)
            send_head(h).wait_recv()
            out_ref[:, cols] = out_ref[:, cols] + got_heads[h]
        for h in range(QH):
            send_head(h).wait_send()


def fused(n_dp, n_fsdp, hidden, lengths, learner, slot_offset, norm_gain, query_weight, keyval_weight):
    tokens, width = hidden.shape
    depth, q_cols = query_weight.shape
    n_cols = q_cols + keyval_weight.shape[1]
    n_z = n_fsdp // 4
    n_shards = 2 * n_z
    bf16, f32 = jnp.bfloat16, jnp.float32
    dma = pltpu.SemaphoreType.DMA
    vmem = pl.BlockSpec(memory_space=pltpu.VMEM)
    hbm = pl.BlockSpec(memory_space=pl.ANY)
    return pl.pallas_call(
        functools.partial(kernel, n_dp, n_fsdp),
        out_shape=jax.ShapeDtypeStruct((tokens, q_cols), bf16),
        in_specs=[hbm, hbm, hbm, hbm, vmem, hbm, hbm],
        out_specs=vmem,
        scratch_shapes=[
            pltpu.SMEM(lengths.shape, jnp.int32),
            pltpu.SMEM(lengths.shape, jnp.int32),
            pltpu.SMEM(lengths.shape, jnp.int32),
            pltpu.VMEM((n_shards, depth, n_cols), bf16),
            pltpu.VMEM((n_shards, 8, depth), f32),
            pltpu.VMEM((tokens, width), bf16),
            pltpu.VMEM((n_shards, tokens, depth), bf16),
            pltpu.VMEM((tokens, 128), f32),
            pltpu.VMEM((tokens, 128), f32),
            pltpu.VMEM((2, tokens, n_cols), f32),
            pltpu.VMEM((tokens, n_cols), f32),
            pltpu.VMEM((tokens, HD), f32),
            pltpu.VMEM((tokens, HD), f32),
            pltpu.VMEM((tokens, tokens), f32),
            pltpu.VMEM((tokens, tokens), bf16),
            pltpu.VMEM((tokens, tokens), bf16),
            pltpu.VMEM((QH, tokens, HD), bf16),
            pltpu.VMEM((QH, tokens, HD), bf16),
            dma((6,)),
            dma((n_shards, 4 * SUBS)),
            dma((2, n_z, 4 * SUBS)),
            dma((n_z, 4 * SUBS)),
            dma((n_shards, 4 * SUBS)),
            dma((3, n_z)),
            dma((n_shards,)),
            dma((n_shards,)),
            dma((n_shards,)),
            dma((2,)),
            dma((n_cols // 256,)),
            dma((n_cols // 256,)),
            dma((QH,)),
            dma((QH,)),
        ],
        compiler_params=pltpu.CompilerParams(
            collective_id=0, has_side_effects=True, vmem_limit_bytes=60 * 1024 * 1024
        ),
    )(lengths, learner, slot_offset, hidden, norm_gain, query_weight, keyval_weight)


def route(buffer, tables):
    channels = buffer.shape[1]
    peer_count = lax.axis_size("dp")
    pair_count = tables.shape[1] // (2 * peer_count)
    block_len = buffer.shape[0] // pair_count
    slice_len = block_len // peer_count
    blocks = buffer.reshape(pair_count, peer_count, slice_len, channels)
    spread = lax.all_to_all(blocks, "dp", split_axis=1, concat_axis=0, tiled=True)
    lengths_all = tables[0].reshape(peer_count * pair_count, 2)
    targets = tables[1].reshape(peer_count * pair_count, 2)[:, 0]
    offsets_all = tables[2].reshape(peer_count * pair_count, 2)
    ordering = jnp.argsort(targets, stable=True)
    arranged = jnp.take(spread, ordering, axis=0).reshape(
        peer_count, pair_count, 1, slice_len, channels
    )
    received = lax.all_to_all(arranged, "dp", split_axis=0, concat_axis=2, tiled=True)
    received = received.reshape(pair_count * block_len, channels)
    own_blocks = lax.dynamic_slice_in_dim(ordering, lax.axis_index("dp") * pair_count, pair_count)
    pair_lengths = jnp.take(lengths_all, own_blocks, axis=0)
    sources = jnp.stack([jnp.zeros_like(pair_lengths[:, 0]), pair_lengths[:, 0]], axis=1)
    sources = (sources + (jnp.arange(pair_count, dtype=jnp.int32) * block_len)[:, None]).reshape(-1)
    row_lengths = pair_lengths.reshape(-1)
    row_offsets = jnp.take(offsets_all, own_blocks, axis=0).reshape(-1)
    places = jnp.arange(pair_count * block_len, dtype=jnp.int32)
    relative = places[:, None] - row_offsets[None, :]
    inside = (relative >= 0) & (relative < row_lengths[None, :])
    take_index = jnp.sum(jnp.where(inside, sources[None, :] + relative, 0), axis=1)
    return jnp.take(received, take_index, axis=0)


def solution(mesh):
    n_dp, n_fsdp = mesh.shape["dp"], mesh.shape["fsdp"]

    def shards(hidden, lengths, learner, slot_offset, norm_gain, query_weight, keyval_weight):
        attended = fused(
            n_dp, n_fsdp, hidden, lengths, learner, slot_offset, norm_gain, query_weight, keyval_weight
        )
        if n_dp == 2:
            return attended
        tables = lax.all_gather(
            jnp.stack([lengths, learner, slot_offset]), "dp", axis=1, tiled=True
        )
        return route(attended, tables)

    placed = (
        P(("dp", "fsdp"), None),
        P(("dp", "fsdp")),
        P(("dp", "fsdp")),
        P(("dp", "fsdp")),
        P("fsdp"),
        P("fsdp", None),
        P("fsdp", None),
    )
    return jax.shard_map(
        shards, mesh=mesh, in_specs=placed, out_specs=P(("dp", "fsdp"), None), check_vma=False
    )
```

```python
import functools
import math

import jax
import jax.numpy as jnp
from jax import lax
from jax.experimental import pallas as pl
from jax.experimental.pallas import tpu as pltpu
from jax.sharding import PartitionSpec as P

HD = 128
QH = 4
ROPE_BASE = 500000.0
NORM_EPS = 1e-05
MESH = pl.DeviceIdType.MESH
SUBS = 2


def kernel(
    n_dp,
    n_fsdp,
    lengths_hbm,
    learner_hbm,
    offset_hbm,
    hidden_ref,
    gain_ref,
    query_ref,
    keyval_ref,
    out_ref,
    lengths_ref,
    learner_ref,
    offset_ref,
    weights,
    gains,
    own_rows,
    mate_rows,
    own_inv,
    mate_inv,
    total,
    sent_sums,
    mate_total,
    cosine,
    sine,
    masked,
    place_here,
    place_there,
    sent_heads,
    got_heads,
    local_sem,
    part_recv,
    z_send,
    y_send,
    x_send,
    gain_send,
    gain_recv,
    rows_send,
    rows_recv,
    inv_sem,
    sum_send,
    sum_recv,
    head_send,
    head_recv,
):
    dp = lax.axis_index("dp")
    fs = lax.axis_index("fsdp")
    core = lax.rem(fs, 2)
    y = lax.rem(fs // 2, 2)
    z = fs // 4
    n_z = n_fsdp // 4
    x = lax.rem(dp, 2)
    x_peer = {"dp": dp + 1 - 2 * x}
    mate = {"fsdp": fs + 1 - 2 * core}
    y_peer = {"fsdp": fs + 2 - 4 * y}
    tokens = own_rows.shape[0]
    depth = query_ref.shape[0]
    n_cols = weights.shape[2]
    q_cols = QH * HD
    part = depth // (4 * SUBS)
    own = z * 2 + y
    other = z * 2 + 1 - y
    n_shards = 2 * n_z
    role_a = 3 * x
    role_b = 1 + x
    role_c = 2 - x
    role_d = 3 - 3 * x

    def can_send(up):
        return (z + 2 * up - 1 >= 0) & (z + 2 * up - 1 < n_z)

    load_q = pltpu.make_async_copy(query_ref, weights.at[own, :, pl.ds(0, q_cols)], local_sem.at[0])
    load_kv = pltpu.make_async_copy(
        keyval_ref, weights.at[own, :, pl.ds(q_cols, n_cols - q_cols)], local_sem.at[1]
    )
    load_rows = pltpu.make_async_copy(hidden_ref, own_rows, local_sem.at[2])
    load_tables = [
        pltpu.make_async_copy(src, dst, local_sem.at[3 + i])
        for i, (src, dst) in enumerate(
            ((lengths_hbm, lengths_ref), (learner_hbm, learner_ref), (offset_hbm, offset_ref))
        )
    ]
    load_q.start()
    load_kv.start()
    load_rows.start()
    for load in load_tables:
        load.start()

    barrier = pltpu.get_barrier_semaphore()
    pl.semaphore_signal(barrier, inc=1, device_id=x_peer, device_id_type=MESH)
    pl.semaphore_signal(barrier, inc=1, device_id=mate, device_id_type=MESH)
    pl.semaphore_signal(barrier, inc=1, device_id=y_peer, device_id_type=MESH)
    for up in (0, 1):

        @pl.when(can_send(up))
        def _(up=up):
            pl.semaphore_signal(
                barrier, inc=1, device_id={"fsdp": fs + 8 * up - 4}, device_id_type=MESH
            )

    gains[own] = jnp.broadcast_to(gain_ref[...].astype(jnp.float32).reshape(1, depth), (8, depth))
    inner = (z > 0) & (z < n_z - 1)
    pl.semaphore_wait(barrier, jnp.where(inner, 5, 4))

    def piece(slot, p):
        return weights.at[slot, pl.ds(pl.multiple_of(p * part, part), part), :]

    def send_z(zz, p, up):
        slot = zz * 2 + y
        return pltpu.make_async_remote_copy(
            src_ref=piece(slot, p),
            dst_ref=piece(slot, p),
            send_sem=z_send.at[up, zz, p],
            recv_sem=part_recv.at[slot, p],
            device_id={"fsdp": fs + 8 * up - 4},
            device_id_type=MESH,
        )

    def send_y(zz, p):
        slot = zz * 2 + y
        return pltpu.make_async_remote_copy(
            src_ref=piece(slot, p),
            dst_ref=piece(slot, p),
            send_sem=y_send.at[zz, p],
            recv_sem=part_recv.at[slot, p],
            device_id=y_peer,
            device_id_type=MESH,
        )

    def send_x(slot, p):
        return pltpu.make_async_remote_copy(
            src_ref=piece(slot, p),
            dst_ref=piece(slot, p),
            send_sem=x_send.at[slot, p],
            recv_sem=part_recv.at[slot, p],
            device_id=x_peer,
            device_id_type=MESH,
        )

    def arrived(slot, p):
        send_x(slot, p).wait_recv()

    def send_gain(zz, device, sem):
        slot = zz * 2 + y
        return pltpu.make_async_remote_copy(
            src_ref=gains.at[slot],
            dst_ref=gains.at[slot],
            send_sem=sem,
            recv_sem=gain_recv.at[slot],
            device_id=device,
            device_id_type=MESH,
        )

    def gain_z(zz, up):
        return send_gain(zz, {"fsdp": fs + 8 * up - 4}, gain_send.at[up, zz])

    def gain_y(zz):
        return send_gain(zz, y_peer, gain_send.at[2, zz])

    def gain_arrived(slot):
        pltpu.make_async_remote_copy(
            src_ref=gains.at[slot],
            dst_ref=gains.at[slot],
            send_sem=gain_send.at[2, 0],
            recv_sem=gain_recv.at[slot],
            device_id=y_peer,
            device_id_type=MESH,
        ).wait_recv()

    def send_rows(s):
        start = pl.multiple_of((s * 2 + 1 - core) * depth, depth)
        return pltpu.make_async_remote_copy(
            src_ref=hidden_ref.at[:, pl.ds(start, depth)],
            dst_ref=mate_rows.at[s],
            send_sem=rows_send.at[s],
            recv_sem=rows_recv.at[s],
            device_id=mate,
            device_id_type=MESH,
        )

    send_inv = pltpu.make_async_remote_copy(
        src_ref=own_inv,
        dst_ref=mate_inv,
        send_sem=inv_sem.at[0],
        recv_sem=inv_sem.at[1],
        device_id=mate,
        device_id_type=MESH,
    )

    def each(count, body):
        def step(i, carry):
            body(i)
            return carry

        lax.fori_loop(0, count, step, 0)

    def own_z(q, act):
        def body(j):
            up = lax.rem(j, 2)
            pl.when(can_send(up))(lambda: act(send_z(z, q * SUBS + j // 2, up)))

        each(2 * SUBS, body)

    def own_y(q, act):
        each(SUBS, lambda j: act(send_y(z, q * SUBS + j)))

    def start(copy):
        copy.start()

    def sent(copy):
        copy.wait_send()

    def remote(d, body):
        def step(j):
            up = lax.rem(j, 2)
            zz = z + d - 2 * d * up
            pl.when((zz >= 0) & (zz < n_z))(lambda: body(j // 2, zz, up))

        each(2 * SUBS, step)

    def along_z(d, q, to_y, to_x):
        def body(sub, zz, up):
            p = q * SUBS + sub
            arrived(zz * 2 + y, p)
            pl.when(can_send(up))(lambda: send_z(zz, p, up).start())
            if to_y:
                send_y(zz, p).start()
            if to_x:
                send_x(zz * 2 + y, p).start()

        remote(d, body)

    def gain_along_z(d):
        def step(up):
            zz = z + d - 2 * d * up

            @pl.when((zz >= 0) & (zz < n_z))
            def _():
                gain_arrived(zz * 2 + y)
                pl.when(can_send(up))(lambda: gain_z(zz, up).start())
                gain_y(zz).start()

        each(2, step)

    def along_y(d, q):
        def body(sub, zz, up):
            p = q * SUBS + sub
            arrived(zz * 2 + 1 - y, p)
            send_x(zz * 2 + 1 - y, p).start()

        remote(d, body)

    load_q.wait()
    load_kv.wait()
    own_z(role_a, start)
    own_y(role_a, start)
    own_z(role_b, start)
    for up in (0, 1):
        pl.when(can_send(up))(lambda up=up: gain_z(z, up).start())
    gain_y(z).start()

    def rows_out(i):
        for k in (2 * i, 2 * i + 1):
            send_rows(lax.rem(own + k, n_shards)).start()

    rows_out(0)

    load_rows.wait()
    width = own_rows.shape[1]

    def square(i):
        rows = pl.ds(pl.multiple_of(i * 32, 32), 32)
        values = own_rows[rows, :].astype(jnp.float32)
        mean = jnp.sum(values * values, axis=1, keepdims=True) / width
        own_inv[rows, :] = jnp.broadcast_to(lax.rsqrt(mean + NORM_EPS), (32, 128))

    each(tokens // 32, square)
    send_inv.start()
    rows_out(1)

    for load in load_tables:
        load.wait()
    n_rows = lengths_ref.shape[0]
    across = lax.broadcasted_iota(jnp.int32, (1, tokens), 1)
    down = lax.broadcasted_iota(jnp.int32, (tokens, 1), 0)
    row_across = jnp.zeros_like(across)
    row_down = jnp.zeros_like(down)
    start_down = jnp.zeros_like(down)
    target = jnp.zeros_like(across)
    goes_to = jnp.zeros_like(across)
    first = jnp.int32(0)
    for r in range(n_rows):
        in_across = across >= first
        in_down = down >= first
        row_across = jnp.where(in_across, r, row_across)
        row_down = jnp.where(in_down, r, row_down)
        start_down = jnp.where(in_down, first, start_down)
        target = jnp.where(in_across, offset_ref[r] + across - first, target)
        goes_to = jnp.where(in_across, learner_ref[r], goes_to)
        first = first + lengths_ref[r]
    position = (down - start_down).astype(jnp.float32)
    lane = lax.broadcasted_iota(jnp.int32, (1, HD), 1)
    half = HD // 2
    index = jnp.where(lane < half, lane, lane - half).astype(jnp.float32)
    angle = position * jnp.exp(index * (-2.0 * math.log(ROPE_BASE) / HD))
    cosine[...] = jnp.cos(angle)
    sine[...] = jnp.where(lane < half, -jnp.sin(angle), jnp.sin(angle))

    along_z(1, role_a, True, True)
    gain_along_z(1)
    rows_out(2)
    for i in range(3, n_shards // 2):
        rows_out(i)

    allowed = (row_across == row_down) & (across <= down)
    masked[...] = jnp.where(allowed, 0.0, 1.0)
    if n_dp == 2:
        slot_iota = lax.broadcasted_iota(jnp.int32, (tokens, tokens), 0)
        place_here[...] = jnp.where(
            slot_iota == jnp.where(goes_to == dp, target, -1), 1.0, 0.0
        ).astype(jnp.bfloat16)
        place_there[...] = jnp.where(
            slot_iota == jnp.where(goes_to == 1 - dp, target, -1), 1.0, 0.0
        ).astype(jnp.bfloat16)

    block = depth // 2

    def project(slot, h, whose):
        inner = pl.ds(pl.multiple_of(h * block, block), block)
        gain = gains[slot, 0:1, inner]
        if whose == 0:
            column = pl.multiple_of((slot * 2 + core) * depth + h * block, block)
            rows, inverse = own_rows[:, pl.ds(column, block)], own_inv[:, 0:1]
        else:
            rows, inverse = mate_rows[slot, :, inner], mate_inv[:, 0:1]
        normed = (rows.astype(jnp.float32) * inverse * gain).astype(jnp.bfloat16)
        total[whose] += jnp.dot(normed, weights[slot, inner, :], preferred_element_type=jnp.float32)

    def project_both(slot, h):
        project(slot, h, 1)
        project(slot, h, 0)

    def project_remote(d, column, h, quarters):
        def step(up):
            zz = z + d - 2 * d * up

            @pl.when((zz >= 0) & (zz < n_z))
            def _():
                slot = zz * 2 + (y if column == 0 else 1 - y)
                for q in quarters:
                    each(SUBS, lambda j: arrived(slot, q * SUBS + j))
                project_both(slot, h)

        each(2, step)

    along_z(1, role_b, True, False)
    own_z(role_c, start)
    own_y(role_b, start)
    along_y(1, role_a)
    along_z(2, role_a, True, True)
    gain_along_z(2)
    along_y(1, role_b)
    total[...] = jnp.zeros_like(total)
    send_inv.wait_recv()
    for s in range(n_shards):
        send_rows(s).wait_recv()
    project_both(own, 0)
    along_z(2, role_b, True, False)
    own_y(role_c, start)
    project_both(own, 1)
    along_y(2, role_a)
    along_z(1, role_c, False, False)
    project_remote(1, 0, x, ())
    for d in range(3, n_z):
        along_z(d, role_a, True, True)
        gain_along_z(d)
        along_y(d - 1, role_b)
        along_z(d, role_b, True, False)
    along_z(2, role_c, False, False)
    own_y(role_d, start)
    for zz in range(n_z):
        gain_arrived(zz * 2 + 1 - y)
    project_remote(1, 1, x, ())
    for d in range(3, n_z):
        along_y(d, role_a)
    project_remote(2, 0, x, ())
    along_y(n_z - 1, role_b)
    project_remote(2, 1, x, ())
    project_remote(1, 1, 1 - x, (role_d, role_c))
    project_remote(1, 0, 1 - x, (role_d,))
    for d in range(3, n_z):
        project_remote(d, 0, x, ())
        project_remote(d, 1, x, ())
        along_z(d, role_c, False, False)
    project_remote(2, 0, 1 - x, (role_d,))
    project_remote(2, 1, 1 - x, (role_d, role_c))
    for q in (role_a, role_b):
        each(SUBS, lambda j: arrived(other, q * SUBS + j))
    project_both(other, x)
    for d in range(3, n_z):
        project_remote(d, 0, 1 - x, (role_d,))
    for d in range(3, n_z):
        project_remote(d, 1, 1 - x, (role_d, role_c))
    for q in (role_c, role_d):
        each(SUBS, lambda j: arrived(other, q * SUBS + j))
    project(other, 1 - x, 1)

    groups = ((QH, 2), (0, 1), (1, 1), (2, QH - 2))

    def send_sum(i):
        first, count = groups[i]
        return pltpu.make_async_remote_copy(
            src_ref=sent_sums.at[pl.ds(first, count)],
            dst_ref=mate_total.at[pl.ds(first, count)],
            send_sem=sum_send.at[i],
            recv_sem=sum_recv.at[i],
            device_id=mate,
            device_id_type=MESH,
        )

    for i, (first, count) in enumerate(groups):
        for g in range(first, first + count):
            sent_sums[g] = total[1, :, g * HD : (g + 1) * HD].astype(jnp.bfloat16)
        send_sum(i).start()
    project(other, 1 - x, 0)

    def rotated(values):
        return (values * cosine[...] + pltpu.roll(values, half, 1) * sine[...]).astype(jnp.bfloat16)

    def summed(g):
        return total[0, :, g * HD : (g + 1) * HD] + mate_total[g].astype(jnp.float32)

    send_sum(0).wait_recv()
    key = rotated(summed(QH))
    value = summed(QH + 1).astype(jnp.bfloat16)

    def send_head(h):
        return pltpu.make_async_remote_copy(
            src_ref=sent_heads.at[h],
            dst_ref=got_heads.at[h],
            send_sem=head_send.at[h],
            recv_sem=head_recv.at[h],
            device_id=x_peer,
            device_id_type=MESH,
        )

    for h in range(QH):
        if h < 3:
            send_sum(h + 1).wait_recv()
        query = rotated(summed(h))
        scores = lax.dot_general(
            query, key, (((1,), (1,)), ((), ())), preferred_element_type=jnp.float32
        ) * HD ** (-0.5)
        scores = jnp.where(masked[...] > 0.5, -1e30, scores)
        exped = jnp.exp(scores - jnp.max(scores, axis=1, keepdims=True))
        chance = (exped / jnp.sum(exped, axis=1, keepdims=True)).astype(jnp.bfloat16)
        mixed = jnp.dot(chance, value, preferred_element_type=jnp.float32).astype(jnp.bfloat16)
        cols = pl.ds(h * HD, HD)
        if n_dp == 2:
            sent_heads[h] = jnp.dot(
                place_there[...], mixed, preferred_element_type=jnp.float32
            ).astype(jnp.bfloat16)
            send_head(h).start()
            out_ref[:, cols] = jnp.dot(
                place_here[...], mixed, preferred_element_type=jnp.float32
            ).astype(jnp.bfloat16)
        else:
            out_ref[:, cols] = mixed

    for q in (role_a, role_b, role_c):
        own_z(q, sent)
    for q in (role_a, role_b, role_c, role_d):
        own_y(q, sent)
    for zz in range(n_z):
        pl.when(can_send(0) & (zz >= z))(lambda zz=zz: gain_z(zz, 0).wait_send())
        pl.when(can_send(1) & (zz <= z))(lambda zz=zz: gain_z(zz, 1).wait_send())
        gain_y(zz).wait_send()
    for s in range(n_shards):
        send_rows(s).wait_send()
    send_inv.wait_send()

    def relayed(sub, zz, up):
        a, b, c = (q * SUBS + sub for q in (role_a, role_b, role_c))
        for p in (a, b, c):
            pl.when(can_send(up))(lambda p=p: send_z(zz, p, up).wait_send())
        send_y(zz, a).wait_send()
        send_y(zz, b).wait_send()
        send_x(zz * 2 + y, a).wait_send()
        send_x(zz * 2 + 1 - y, a).wait_send()
        send_x(zz * 2 + 1 - y, b).wait_send()

    for d in range(1, n_z):
        remote(d, relayed)

    for i in range(len(groups)):
        send_sum(i).wait_send()
    if n_dp == 2:
        for h in range(QH):
            cols = pl.ds(h * HD, HD)
            send_head(h).wait_recv()
            out_ref[:, cols] = out_ref[:, cols] + got_heads[h]
        for h in range(QH):
            send_head(h).wait_send()


def fused(n_dp, n_fsdp, hidden, lengths, learner, slot_offset, norm_gain, query_weight, keyval_weight):
    tokens, width = hidden.shape
    depth, q_cols = query_weight.shape
    n_cols = q_cols + keyval_weight.shape[1]
    n_z = n_fsdp // 4
    n_shards = 2 * n_z
    bf16, f32 = jnp.bfloat16, jnp.float32
    dma = pltpu.SemaphoreType.DMA
    vmem = pl.BlockSpec(memory_space=pltpu.VMEM)
    hbm = pl.BlockSpec(memory_space=pl.ANY)
    return pl.pallas_call(
        functools.partial(kernel, n_dp, n_fsdp),
        out_shape=jax.ShapeDtypeStruct((tokens, q_cols), bf16),
        in_specs=[hbm, hbm, hbm, hbm, vmem, hbm, hbm],
        out_specs=vmem,
        scratch_shapes=[
            pltpu.SMEM(lengths.shape, jnp.int32),
            pltpu.SMEM(lengths.shape, jnp.int32),
            pltpu.SMEM(lengths.shape, jnp.int32),
            pltpu.VMEM((n_shards, depth, n_cols), bf16),
            pltpu.VMEM((n_shards, 8, depth), f32),
            pltpu.VMEM((tokens, width), bf16),
            pltpu.VMEM((n_shards, tokens, depth), bf16),
            pltpu.VMEM((tokens, 128), f32),
            pltpu.VMEM((tokens, 128), f32),
            pltpu.VMEM((2, tokens, n_cols), f32),
            pltpu.VMEM((n_cols // HD, tokens, HD), bf16),
            pltpu.VMEM((n_cols // HD, tokens, HD), bf16),
            pltpu.VMEM((tokens, HD), f32),
            pltpu.VMEM((tokens, HD), f32),
            pltpu.VMEM((tokens, tokens), f32),
            pltpu.VMEM((tokens, tokens), bf16),
            pltpu.VMEM((tokens, tokens), bf16),
            pltpu.VMEM((QH, tokens, HD), bf16),
            pltpu.VMEM((QH, tokens, HD), bf16),
            dma((6,)),
            dma((n_shards, 4 * SUBS)),
            dma((2, n_z, 4 * SUBS)),
            dma((n_z, 4 * SUBS)),
            dma((n_shards, 4 * SUBS)),
            dma((3, n_z)),
            dma((n_shards,)),
            dma((n_shards,)),
            dma((n_shards,)),
            dma((2,)),
            dma((4,)),
            dma((4,)),
            dma((QH,)),
            dma((QH,)),
        ],
        compiler_params=pltpu.CompilerParams(
            collective_id=0, has_side_effects=True, vmem_limit_bytes=60 * 1024 * 1024
        ),
    )(lengths, learner, slot_offset, hidden, norm_gain, query_weight, keyval_weight)


def route(buffer, tables):
    channels = buffer.shape[1]
    peer_count = lax.axis_size("dp")
    pair_count = tables.shape[1] // (2 * peer_count)
    block_len = buffer.shape[0] // pair_count
    slice_len = block_len // peer_count
    blocks = buffer.reshape(pair_count, peer_count, slice_len, channels)
    spread = lax.all_to_all(blocks, "dp", split_axis=1, concat_axis=0, tiled=True)
    lengths_all = tables[0].reshape(peer_count * pair_count, 2)
    targets = tables[1].reshape(peer_count * pair_count, 2)[:, 0]
    offsets_all = tables[2].reshape(peer_count * pair_count, 2)
    ordering = jnp.argsort(targets, stable=True)
    arranged = jnp.take(spread, ordering, axis=0).reshape(
        peer_count, pair_count, 1, slice_len, channels
    )
    received = lax.all_to_all(arranged, "dp", split_axis=0, concat_axis=2, tiled=True)
    received = received.reshape(pair_count * block_len, channels)
    own_blocks = lax.dynamic_slice_in_dim(ordering, lax.axis_index("dp") * pair_count, pair_count)
    pair_lengths = jnp.take(lengths_all, own_blocks, axis=0)
    sources = jnp.stack([jnp.zeros_like(pair_lengths[:, 0]), pair_lengths[:, 0]], axis=1)
    sources = (sources + (jnp.arange(pair_count, dtype=jnp.int32) * block_len)[:, None]).reshape(-1)
    row_lengths = pair_lengths.reshape(-1)
    row_offsets = jnp.take(offsets_all, own_blocks, axis=0).reshape(-1)
    places = jnp.arange(pair_count * block_len, dtype=jnp.int32)
    relative = places[:, None] - row_offsets[None, :]
    inside = (relative >= 0) & (relative < row_lengths[None, :])
    take_index = jnp.sum(jnp.where(inside, sources[None, :] + relative, 0), axis=1)
    return jnp.take(received, take_index, axis=0)


def solution(mesh):
    n_dp, n_fsdp = mesh.shape["dp"], mesh.shape["fsdp"]

    def shards(hidden, lengths, learner, slot_offset, norm_gain, query_weight, keyval_weight):
        attended = fused(
            n_dp, n_fsdp, hidden, lengths, learner, slot_offset, norm_gain, query_weight, keyval_weight
        )
        if n_dp == 2:
            return attended
        tables = lax.all_gather(
            jnp.stack([lengths, learner, slot_offset]), "dp", axis=1, tiled=True
        )
        return route(attended, tables)

    placed = (
        P(("dp", "fsdp"), None),
        P(("dp", "fsdp")),
        P(("dp", "fsdp")),
        P(("dp", "fsdp")),
        P("fsdp"),
        P("fsdp", None),
        P("fsdp", None),
    )
    return jax.shard_map(
        shards, mesh=mesh, in_specs=placed, out_specs=P(("dp", "fsdp"), None), check_vma=False
    )
```

```python
import functools
import math

import jax
import jax.numpy as jnp
from jax import lax
from jax.experimental import pallas as pl
from jax.experimental.pallas import tpu as pltpu
from jax.sharding import PartitionSpec as P

HD = 128
QH = 4
ROPE_BASE = 500000.0
NORM_EPS = 1e-05
MESH = pl.DeviceIdType.MESH
SUBS = 4


def kernel(
    n_dp,
    n_fsdp,
    lengths_hbm,
    learner_hbm,
    offset_hbm,
    hidden_ref,
    gain_ref,
    query_ref,
    keyval_ref,
    out_ref,
    lengths_ref,
    learner_ref,
    offset_ref,
    weights,
    gains,
    own_rows,
    mate_rows,
    own_inv,
    mate_inv,
    total,
    mate_total,
    cosine,
    sine,
    masked,
    place_here,
    place_there,
    sent_heads,
    got_heads,
    local_sem,
    part_recv,
    z_send,
    y_send,
    x_send,
    gain_send,
    gain_recv,
    rows_send,
    rows_recv,
    inv_sem,
    sum_send,
    sum_recv,
    head_send,
    head_recv,
):
    dp = lax.axis_index("dp")
    fs = lax.axis_index("fsdp")
    core = lax.rem(fs, 2)
    y = lax.rem(fs // 2, 2)
    z = fs // 4
    n_z = n_fsdp // 4
    x = lax.rem(dp, 2)
    x_peer = {"dp": dp + 1 - 2 * x}
    mate = {"fsdp": fs + 1 - 2 * core}
    y_peer = {"fsdp": fs + 2 - 4 * y}
    tokens = own_rows.shape[0]
    depth = query_ref.shape[0]
    n_cols = weights.shape[2]
    q_cols = QH * HD
    part = depth // (4 * SUBS)
    own = z * 2 + y
    other = z * 2 + 1 - y
    n_shards = 2 * n_z
    role_a = 3 * x
    role_b = 1 + x
    role_c = 2 - x
    role_d = 3 - 3 * x

    def can_send(up):
        return (z + 2 * up - 1 >= 0) & (z + 2 * up - 1 < n_z)

    load_q = pltpu.make_async_copy(query_ref, weights.at[own, :, pl.ds(0, q_cols)], local_sem.at[0])
    load_kv = pltpu.make_async_copy(
        keyval_ref, weights.at[own, :, pl.ds(q_cols, n_cols - q_cols)], local_sem.at[1]
    )
    load_rows = pltpu.make_async_copy(hidden_ref, own_rows, local_sem.at[2])
    load_tables = [
        pltpu.make_async_copy(src, dst, local_sem.at[3 + i])
        for i, (src, dst) in enumerate(
            ((lengths_hbm, lengths_ref), (learner_hbm, learner_ref), (offset_hbm, offset_ref))
        )
    ]
    load_q.start()
    load_kv.start()
    load_rows.start()
    for load in load_tables:
        load.start()

    barrier = pltpu.get_barrier_semaphore()
    pl.semaphore_signal(barrier, inc=1, device_id=x_peer, device_id_type=MESH)
    pl.semaphore_signal(barrier, inc=1, device_id=mate, device_id_type=MESH)
    pl.semaphore_signal(barrier, inc=1, device_id=y_peer, device_id_type=MESH)
    for up in (0, 1):

        @pl.when(can_send(up))
        def _(up=up):
            pl.semaphore_signal(
                barrier, inc=1, device_id={"fsdp": fs + 8 * up - 4}, device_id_type=MESH
            )

    gains[own] = jnp.broadcast_to(gain_ref[...].astype(jnp.float32).reshape(1, depth), (8, depth))
    inner = (z > 0) & (z < n_z - 1)
    pl.semaphore_wait(barrier, jnp.where(inner, 5, 4))

    def piece(slot, p):
        return weights.at[slot, pl.ds(pl.multiple_of(p * part, part), part), :]

    def send_z(zz, p, up):
        slot = zz * 2 + y
        return pltpu.make_async_remote_copy(
            src_ref=piece(slot, p),
            dst_ref=piece(slot, p),
            send_sem=z_send.at[up, zz, p],
            recv_sem=part_recv.at[slot, p],
            device_id={"fsdp": fs + 8 * up - 4},
            device_id_type=MESH,
        )

    def send_y(zz, p):
        slot = zz * 2 + y
        return pltpu.make_async_remote_copy(
            src_ref=piece(slot, p),
            dst_ref=piece(slot, p),
            send_sem=y_send.at[zz, p],
            recv_sem=part_recv.at[slot, p],
            device_id=y_peer,
            device_id_type=MESH,
        )

    def send_x(slot, p):
        return pltpu.make_async_remote_copy(
            src_ref=piece(slot, p),
            dst_ref=piece(slot, p),
            send_sem=x_send.at[slot, p],
            recv_sem=part_recv.at[slot, p],
            device_id=x_peer,
            device_id_type=MESH,
        )

    def arrived(slot, p):
        send_x(slot, p).wait_recv()

    def send_gain(zz, device, sem):
        slot = zz * 2 + y
        return pltpu.make_async_remote_copy(
            src_ref=gains.at[slot],
            dst_ref=gains.at[slot],
            send_sem=sem,
            recv_sem=gain_recv.at[slot],
            device_id=device,
            device_id_type=MESH,
        )

    def gain_z(zz, up):
        return send_gain(zz, {"fsdp": fs + 8 * up - 4}, gain_send.at[up, zz])

    def gain_y(zz):
        return send_gain(zz, y_peer, gain_send.at[2, zz])

    def gain_arrived(slot):
        pltpu.make_async_remote_copy(
            src_ref=gains.at[slot],
            dst_ref=gains.at[slot],
            send_sem=gain_send.at[2, 0],
            recv_sem=gain_recv.at[slot],
            device_id=y_peer,
            device_id_type=MESH,
        ).wait_recv()

    def send_rows(s):
        start = pl.multiple_of((s * 2 + 1 - core) * depth, depth)
        return pltpu.make_async_remote_copy(
            src_ref=hidden_ref.at[:, pl.ds(start, depth)],
            dst_ref=mate_rows.at[s],
            send_sem=rows_send.at[s],
            recv_sem=rows_recv.at[s],
            device_id=mate,
            device_id_type=MESH,
        )

    send_inv = pltpu.make_async_remote_copy(
        src_ref=own_inv,
        dst_ref=mate_inv,
        send_sem=inv_sem.at[0],
        recv_sem=inv_sem.at[1],
        device_id=mate,
        device_id_type=MESH,
    )

    def each(count, body):
        def step(i, carry):
            body(i)
            return carry

        lax.fori_loop(0, count, step, 0)

    def own_z(q, act):
        def body(j):
            up = lax.rem(j, 2)
            pl.when(can_send(up))(lambda: act(send_z(z, q * SUBS + j // 2, up)))

        each(2 * SUBS, body)

    def own_y(q, act):
        each(SUBS, lambda j: act(send_y(z, q * SUBS + j)))

    def start(copy):
        copy.start()

    def sent(copy):
        copy.wait_send()

    def remote(d, body):
        def step(j):
            up = lax.rem(j, 2)
            zz = z + d - 2 * d * up
            pl.when((zz >= 0) & (zz < n_z))(lambda: body(j // 2, zz, up))

        each(2 * SUBS, step)

    def along_z(d, q, to_y, to_x):
        def body(sub, zz, up):
            p = q * SUBS + sub
            arrived(zz * 2 + y, p)
            pl.when(can_send(up))(lambda: send_z(zz, p, up).start())
            if to_y:
                send_y(zz, p).start()
            if to_x:
                send_x(zz * 2 + y, p).start()

        remote(d, body)

    def gain_along_z(d):
        def step(up):
            zz = z + d - 2 * d * up

            @pl.when((zz >= 0) & (zz < n_z))
            def _():
                gain_arrived(zz * 2 + y)
                pl.when(can_send(up))(lambda: gain_z(zz, up).start())
                gain_y(zz).start()

        each(2, step)

    def along_y(d, q):
        def body(sub, zz, up):
            p = q * SUBS + sub
            arrived(zz * 2 + 1 - y, p)
            send_x(zz * 2 + 1 - y, p).start()

        remote(d, body)

    load_q.wait()
    load_kv.wait()
    own_z(role_a, start)
    own_y(role_a, start)
    own_z(role_b, start)
    for up in (0, 1):
        pl.when(can_send(up))(lambda up=up: gain_z(z, up).start())
    gain_y(z).start()

    def rows_out(i):
        for k in (2 * i, 2 * i + 1):
            send_rows(lax.rem(own + k, n_shards)).start()

    rows_out(0)

    load_rows.wait()
    width = own_rows.shape[1]

    def square(i):
        rows = pl.ds(pl.multiple_of(i * 32, 32), 32)
        values = own_rows[rows, :].astype(jnp.float32)
        mean = jnp.sum(values * values, axis=1, keepdims=True) / width
        own_inv[rows, :] = jnp.broadcast_to(lax.rsqrt(mean + NORM_EPS), (32, 128))

    each(tokens // 32, square)
    send_inv.start()
    rows_out(1)

    for load in load_tables:
        load.wait()
    n_rows = lengths_ref.shape[0]
    across = lax.broadcasted_iota(jnp.int32, (1, tokens), 1)
    down = lax.broadcasted_iota(jnp.int32, (tokens, 1), 0)
    row_across = jnp.zeros_like(across)
    row_down = jnp.zeros_like(down)
    start_down = jnp.zeros_like(down)
    target = jnp.zeros_like(across)
    goes_to = jnp.zeros_like(across)
    first = jnp.int32(0)
    for r in range(n_rows):
        in_across = across >= first
        in_down = down >= first
        row_across = jnp.where(in_across, r, row_across)
        row_down = jnp.where(in_down, r, row_down)
        start_down = jnp.where(in_down, first, start_down)
        target = jnp.where(in_across, offset_ref[r] + across - first, target)
        goes_to = jnp.where(in_across, learner_ref[r], goes_to)
        first = first + lengths_ref[r]
    position = (down - start_down).astype(jnp.float32)
    lane = lax.broadcasted_iota(jnp.int32, (1, HD), 1)
    half = HD // 2
    index = jnp.where(lane < half, lane, lane - half).astype(jnp.float32)
    angle = position * jnp.exp(index * (-2.0 * math.log(ROPE_BASE) / HD))
    cosine[...] = jnp.cos(angle)
    sine[...] = jnp.where(lane < half, -jnp.sin(angle), jnp.sin(angle))

    along_z(1, role_a, True, True)
    gain_along_z(1)
    rows_out(2)
    for i in range(3, n_shards // 2):
        rows_out(i)

    allowed = (row_across == row_down) & (across <= down)
    masked[...] = jnp.where(allowed, 0.0, 1.0)
    if n_dp == 2:
        slot_iota = lax.broadcasted_iota(jnp.int32, (tokens, tokens), 0)
        place_here[...] = jnp.where(
            slot_iota == jnp.where(goes_to == dp, target, -1), 1.0, 0.0
        ).astype(jnp.bfloat16)
        place_there[...] = jnp.where(
            slot_iota == jnp.where(goes_to == 1 - dp, target, -1), 1.0, 0.0
        ).astype(jnp.bfloat16)

    block = depth // 2

    def project(slot, h, whose):
        inner = pl.ds(pl.multiple_of(h * block, block), block)
        gain = gains[slot, 0:1, inner]
        if whose == 0:
            column = pl.multiple_of((slot * 2 + core) * depth + h * block, block)
            rows, inverse = own_rows[:, pl.ds(column, block)], own_inv[:, 0:1]
        else:
            rows, inverse = mate_rows[slot, :, inner], mate_inv[:, 0:1]
        normed = (rows.astype(jnp.float32) * inverse * gain).astype(jnp.bfloat16)
        total[whose] += jnp.dot(normed, weights[slot, inner, :], preferred_element_type=jnp.float32)

    def project_both(slot, h):
        project(slot, h, 1)
        project(slot, h, 0)

    def project_remote(d, column, h, quarters):
        def step(up):
            zz = z + d - 2 * d * up

            @pl.when((zz >= 0) & (zz < n_z))
            def _():
                slot = zz * 2 + (y if column == 0 else 1 - y)
                for q in quarters:
                    each(SUBS, lambda j: arrived(slot, q * SUBS + j))
                project_both(slot, h)

        each(2, step)

    along_z(1, role_b, True, False)
    own_z(role_c, start)
    own_y(role_b, start)
    along_y(1, role_a)
    along_z(2, role_a, True, True)
    gain_along_z(2)
    along_y(1, role_b)
    total[...] = jnp.zeros_like(total)
    send_inv.wait_recv()
    for s in range(n_shards):
        send_rows(s).wait_recv()
    project_both(own, 0)
    along_z(2, role_b, True, False)
    own_y(role_c, start)
    project_both(own, 1)
    along_y(2, role_a)
    along_z(1, role_c, False, False)
    project_remote(1, 0, x, ())
    for d in range(3, n_z):
        along_z(d, role_a, True, True)
        gain_along_z(d)
        along_y(d - 1, role_b)
        along_z(d, role_b, True, False)
    along_z(2, role_c, False, False)
    own_y(role_d, start)
    for zz in range(n_z):
        gain_arrived(zz * 2 + 1 - y)
    project_remote(1, 1, x, ())
    for d in range(3, n_z):
        along_y(d, role_a)
    project_remote(2, 0, x, ())
    along_y(n_z - 1, role_b)
    project_remote(2, 1, x, ())
    project_remote(1, 1, 1 - x, (role_d, role_c))
    project_remote(1, 0, 1 - x, (role_d,))
    for d in range(3, n_z):
        project_remote(d, 0, x, ())
        project_remote(d, 1, x, ())
        along_z(d, role_c, False, False)
    project_remote(2, 0, 1 - x, (role_d,))
    project_remote(2, 1, 1 - x, (role_d, role_c))
    for q in (role_a, role_b):
        each(SUBS, lambda j: arrived(other, q * SUBS + j))
    project_both(other, x)
    for d in range(3, n_z):
        project_remote(d, 0, 1 - x, (role_d,))
    for d in range(3, n_z):
        project_remote(d, 1, 1 - x, (role_d, role_c))
    for q in (role_c, role_d):
        each(SUBS, lambda j: arrived(other, q * SUBS + j))
    project(other, 1 - x, 1)

    def send_sum(c):
        cols = pl.ds(c * 256, 256)
        return pltpu.make_async_remote_copy(
            src_ref=total.at[1, :, cols],
            dst_ref=mate_total.at[:, cols],
            send_sem=sum_send.at[c],
            recv_sem=sum_recv.at[c],
            device_id=mate,
            device_id_type=MESH,
        )

    n_sums = n_cols // 256
    order = [n_sums - 1] + list(range(n_sums - 1))
    for c in order:
        send_sum(c).start()
    project(other, 1 - x, 0)

    def rotated(values):
        return (values * cosine[...] + pltpu.roll(values, half, 1) * sine[...]).astype(jnp.bfloat16)

    def summed(col):
        return total[0, :, col : col + HD] + mate_total[:, col : col + HD]

    send_sum(n_sums - 1).wait_recv()
    key = rotated(summed(q_cols))
    value = summed(q_cols + HD).astype(jnp.bfloat16)

    def send_head(h):
        return pltpu.make_async_remote_copy(
            src_ref=sent_heads.at[h],
            dst_ref=got_heads.at[h],
            send_sem=head_send.at[h],
            recv_sem=head_recv.at[h],
            device_id=x_peer,
            device_id_type=MESH,
        )

    for h in range(QH):
        if h % 2 == 0:
            send_sum(h // 2).wait_recv()
        query = rotated(summed(h * HD))
        scores = lax.dot_general(
            query, key, (((1,), (1,)), ((), ())), preferred_element_type=jnp.float32
        ) * HD ** (-0.5)
        scores = jnp.where(masked[...] > 0.5, -1e30, scores)
        exped = jnp.exp(scores - jnp.max(scores, axis=1, keepdims=True))
        chance = (exped / jnp.sum(exped, axis=1, keepdims=True)).astype(jnp.bfloat16)
        mixed = jnp.dot(chance, value, preferred_element_type=jnp.float32).astype(jnp.bfloat16)
        cols = pl.ds(h * HD, HD)
        if n_dp == 2:
            sent_heads[h] = jnp.dot(
                place_there[...], mixed, preferred_element_type=jnp.float32
            ).astype(jnp.bfloat16)
            send_head(h).start()
            out_ref[:, cols] = jnp.dot(
                place_here[...], mixed, preferred_element_type=jnp.float32
            ).astype(jnp.bfloat16)
        else:
            out_ref[:, cols] = mixed

    for q in (role_a, role_b, role_c):
        own_z(q, sent)
    for q in (role_a, role_b, role_c, role_d):
        own_y(q, sent)
    for zz in range(n_z):
        pl.when(can_send(0) & (zz >= z))(lambda zz=zz: gain_z(zz, 0).wait_send())
        pl.when(can_send(1) & (zz <= z))(lambda zz=zz: gain_z(zz, 1).wait_send())
        gain_y(zz).wait_send()
    for s in range(n_shards):
        send_rows(s).wait_send()
    send_inv.wait_send()

    def relayed(sub, zz, up):
        a, b, c = (q * SUBS + sub for q in (role_a, role_b, role_c))
        for p in (a, b, c):
            pl.when(can_send(up))(lambda p=p: send_z(zz, p, up).wait_send())
        send_y(zz, a).wait_send()
        send_y(zz, b).wait_send()
        send_x(zz * 2 + y, a).wait_send()
        send_x(zz * 2 + 1 - y, a).wait_send()
        send_x(zz * 2 + 1 - y, b).wait_send()

    for d in range(1, n_z):
        remote(d, relayed)

    for c in order:
        send_sum(c).wait_send()
    if n_dp == 2:
        for h in range(QH):
            cols = pl.ds(h * HD, HD)
            send_head(h).wait_recv()
            out_ref[:, cols] = out_ref[:, cols] + got_heads[h]
        for h in range(QH):
            send_head(h).wait_send()


def fused(n_dp, n_fsdp, hidden, lengths, learner, slot_offset, norm_gain, query_weight, keyval_weight):
    tokens, width = hidden.shape
    depth, q_cols = query_weight.shape
    n_cols = q_cols + keyval_weight.shape[1]
    n_z = n_fsdp // 4
    n_shards = 2 * n_z
    bf16, f32 = jnp.bfloat16, jnp.float32
    dma = pltpu.SemaphoreType.DMA
    vmem = pl.BlockSpec(memory_space=pltpu.VMEM)
    hbm = pl.BlockSpec(memory_space=pl.ANY)
    return pl.pallas_call(
        functools.partial(kernel, n_dp, n_fsdp),
        out_shape=jax.ShapeDtypeStruct((tokens, q_cols), bf16),
        in_specs=[hbm, hbm, hbm, hbm, vmem, hbm, hbm],
        out_specs=vmem,
        scratch_shapes=[
            pltpu.SMEM(lengths.shape, jnp.int32),
            pltpu.SMEM(lengths.shape, jnp.int32),
            pltpu.SMEM(lengths.shape, jnp.int32),
            pltpu.VMEM((n_shards, depth, n_cols), bf16),
            pltpu.VMEM((n_shards, 8, depth), f32),
            pltpu.VMEM((tokens, width), bf16),
            pltpu.VMEM((n_shards, tokens, depth), bf16),
            pltpu.VMEM((tokens, 128), f32),
            pltpu.VMEM((tokens, 128), f32),
            pltpu.VMEM((2, tokens, n_cols), f32),
            pltpu.VMEM((tokens, n_cols), f32),
            pltpu.VMEM((tokens, HD), f32),
            pltpu.VMEM((tokens, HD), f32),
            pltpu.VMEM((tokens, tokens), f32),
            pltpu.VMEM((tokens, tokens), bf16),
            pltpu.VMEM((tokens, tokens), bf16),
            pltpu.VMEM((QH, tokens, HD), bf16),
            pltpu.VMEM((QH, tokens, HD), bf16),
            dma((6,)),
            dma((n_shards, 4 * SUBS)),
            dma((2, n_z, 4 * SUBS)),
            dma((n_z, 4 * SUBS)),
            dma((n_shards, 4 * SUBS)),
            dma((3, n_z)),
            dma((n_shards,)),
            dma((n_shards,)),
            dma((n_shards,)),
            dma((2,)),
            dma((n_cols // 256,)),
            dma((n_cols // 256,)),
            dma((QH,)),
            dma((QH,)),
        ],
        compiler_params=pltpu.CompilerParams(
            collective_id=0, has_side_effects=True, vmem_limit_bytes=60 * 1024 * 1024
        ),
    )(lengths, learner, slot_offset, hidden, norm_gain, query_weight, keyval_weight)


def route(buffer, tables):
    channels = buffer.shape[1]
    peer_count = lax.axis_size("dp")
    pair_count = tables.shape[1] // (2 * peer_count)
    block_len = buffer.shape[0] // pair_count
    slice_len = block_len // peer_count
    blocks = buffer.reshape(pair_count, peer_count, slice_len, channels)
    spread = lax.all_to_all(blocks, "dp", split_axis=1, concat_axis=0, tiled=True)
    lengths_all = tables[0].reshape(peer_count * pair_count, 2)
    targets = tables[1].reshape(peer_count * pair_count, 2)[:, 0]
    offsets_all = tables[2].reshape(peer_count * pair_count, 2)
    ordering = jnp.argsort(targets, stable=True)
    arranged = jnp.take(spread, ordering, axis=0).reshape(
        peer_count, pair_count, 1, slice_len, channels
    )
    received = lax.all_to_all(arranged, "dp", split_axis=0, concat_axis=2, tiled=True)
    received = received.reshape(pair_count * block_len, channels)
    own_blocks = lax.dynamic_slice_in_dim(ordering, lax.axis_index("dp") * pair_count, pair_count)
    pair_lengths = jnp.take(lengths_all, own_blocks, axis=0)
    sources = jnp.stack([jnp.zeros_like(pair_lengths[:, 0]), pair_lengths[:, 0]], axis=1)
    sources = (sources + (jnp.arange(pair_count, dtype=jnp.int32) * block_len)[:, None]).reshape(-1)
    row_lengths = pair_lengths.reshape(-1)
    row_offsets = jnp.take(offsets_all, own_blocks, axis=0).reshape(-1)
    places = jnp.arange(pair_count * block_len, dtype=jnp.int32)
    relative = places[:, None] - row_offsets[None, :]
    inside = (relative >= 0) & (relative < row_lengths[None, :])
    take_index = jnp.sum(jnp.where(inside, sources[None, :] + relative, 0), axis=1)
    return jnp.take(received, take_index, axis=0)


def solution(mesh):
    n_dp, n_fsdp = mesh.shape["dp"], mesh.shape["fsdp"]

    def shards(hidden, lengths, learner, slot_offset, norm_gain, query_weight, keyval_weight):
        attended = fused(
            n_dp, n_fsdp, hidden, lengths, learner, slot_offset, norm_gain, query_weight, keyval_weight
        )
        if n_dp == 2:
            return attended
        tables = lax.all_gather(
            jnp.stack([lengths, learner, slot_offset]), "dp", axis=1, tiled=True
        )
        return route(attended, tables)

    placed = (
        P(("dp", "fsdp"), None),
        P(("dp", "fsdp")),
        P(("dp", "fsdp")),
        P(("dp", "fsdp")),
        P("fsdp"),
        P("fsdp", None),
        P("fsdp", None),
    )
    return jax.shard_map(
        shards, mesh=mesh, in_specs=placed, out_specs=P(("dp", "fsdp"), None), check_vma=False
    )
```

```python
import functools
import math

import jax
import jax.numpy as jnp
from jax import lax
from jax.experimental import pallas as pl
from jax.experimental.pallas import tpu as pltpu
from jax.sharding import PartitionSpec as P

HD = 128
QH = 4
ROPE_BASE = 500000.0
NORM_EPS = 1e-05
MESH = pl.DeviceIdType.MESH
SUBS = 2


def kernel(
    n_dp,
    n_fsdp,
    lengths_hbm,
    learner_hbm,
    offset_hbm,
    hidden_ref,
    gain_ref,
    query_ref,
    keyval_ref,
    out_ref,
    lengths_ref,
    learner_ref,
    offset_ref,
    weights,
    gains,
    own_rows,
    mate_rows,
    own_inv,
    mate_inv,
    total,
    mate_total,
    cosine,
    sine,
    masked,
    place_here,
    place_there,
    sent_heads,
    got_heads,
    local_sem,
    part_recv,
    z_send,
    y_send,
    x_send,
    gain_send,
    gain_recv,
    rows_send,
    rows_recv,
    inv_sem,
    sum_send,
    sum_recv,
    head_send,
    head_recv,
):
    dp = lax.axis_index("dp")
    fs = lax.axis_index("fsdp")
    core = lax.rem(fs, 2)
    y = lax.rem(fs // 2, 2)
    z = fs // 4
    n_z = n_fsdp // 4
    x = lax.rem(dp, 2)
    x_peer = {"dp": dp + 1 - 2 * x}
    mate = {"fsdp": fs + 1 - 2 * core}
    y_peer = {"fsdp": fs + 2 - 4 * y}
    tokens = own_rows.shape[0]
    depth = query_ref.shape[0]
    n_cols = weights.shape[2]
    q_cols = QH * HD
    part = depth // (4 * SUBS)
    own = z * 2 + y
    other = z * 2 + 1 - y
    n_shards = 2 * n_z
    role_a = 3 * x
    role_b = 1 + x
    role_c = 2 - x
    role_d = 3 - 3 * x

    def can_send(up):
        return (z + 2 * up - 1 >= 0) & (z + 2 * up - 1 < n_z)

    load_q = pltpu.make_async_copy(query_ref, weights.at[own, :, pl.ds(0, q_cols)], local_sem.at[0])
    load_kv = pltpu.make_async_copy(
        keyval_ref, weights.at[own, :, pl.ds(q_cols, n_cols - q_cols)], local_sem.at[1]
    )
    load_rows = pltpu.make_async_copy(hidden_ref, own_rows, local_sem.at[2])
    load_tables = [
        pltpu.make_async_copy(src, dst, local_sem.at[3 + i])
        for i, (src, dst) in enumerate(
            ((lengths_hbm, lengths_ref), (learner_hbm, learner_ref), (offset_hbm, offset_ref))
        )
    ]
    load_q.start()
    load_kv.start()
    load_rows.start()
    for load in load_tables:
        load.start()

    barrier = pltpu.get_barrier_semaphore()
    pl.semaphore_signal(barrier, inc=1, device_id=x_peer, device_id_type=MESH)
    pl.semaphore_signal(barrier, inc=1, device_id=mate, device_id_type=MESH)
    pl.semaphore_signal(barrier, inc=1, device_id=y_peer, device_id_type=MESH)
    for up in (0, 1):

        @pl.when(can_send(up))
        def _(up=up):
            pl.semaphore_signal(
                barrier, inc=1, device_id={"fsdp": fs + 8 * up - 4}, device_id_type=MESH
            )

    gains[own] = jnp.broadcast_to(gain_ref[...].astype(jnp.float32).reshape(1, depth), (8, depth))
    inner = (z > 0) & (z < n_z - 1)
    pl.semaphore_wait(barrier, jnp.where(inner, 5, 4))

    def piece(slot, p, n=1):
        return weights.at[slot, pl.ds(pl.multiple_of(p * part, part), n * part), :]

    def send_z(zz, p, up, n=1):
        slot = zz * 2 + y
        return pltpu.make_async_remote_copy(
            src_ref=piece(slot, p, n),
            dst_ref=piece(slot, p, n),
            send_sem=z_send.at[up, zz, p],
            recv_sem=part_recv.at[slot, p],
            device_id={"fsdp": fs + 8 * up - 4},
            device_id_type=MESH,
        )

    def send_y(zz, p, n=1):
        slot = zz * 2 + y
        return pltpu.make_async_remote_copy(
            src_ref=piece(slot, p, n),
            dst_ref=piece(slot, p, n),
            send_sem=y_send.at[zz, p],
            recv_sem=part_recv.at[slot, p],
            device_id=y_peer,
            device_id_type=MESH,
        )

    def send_x(slot, p, n=1):
        return pltpu.make_async_remote_copy(
            src_ref=piece(slot, p, n),
            dst_ref=piece(slot, p, n),
            send_sem=x_send.at[slot, p],
            recv_sem=part_recv.at[slot, p],
            device_id=x_peer,
            device_id_type=MESH,
        )

    def arrived(slot, p, n=1):
        send_x(slot, p, n).wait_recv()

    def send_gain(zz, device, sem):
        slot = zz * 2 + y
        return pltpu.make_async_remote_copy(
            src_ref=gains.at[slot],
            dst_ref=gains.at[slot],
            send_sem=sem,
            recv_sem=gain_recv.at[slot],
            device_id=device,
            device_id_type=MESH,
        )

    def gain_z(zz, up):
        return send_gain(zz, {"fsdp": fs + 8 * up - 4}, gain_send.at[up, zz])

    def gain_y(zz):
        return send_gain(zz, y_peer, gain_send.at[2, zz])

    def gain_arrived(slot):
        pltpu.make_async_remote_copy(
            src_ref=gains.at[slot],
            dst_ref=gains.at[slot],
            send_sem=gain_send.at[2, 0],
            recv_sem=gain_recv.at[slot],
            device_id=y_peer,
            device_id_type=MESH,
        ).wait_recv()

    def send_rows(s):
        start = pl.multiple_of((s * 2 + 1 - core) * depth, depth)
        return pltpu.make_async_remote_copy(
            src_ref=hidden_ref.at[:, pl.ds(start, depth)],
            dst_ref=mate_rows.at[s],
            send_sem=rows_send.at[s],
            recv_sem=rows_recv.at[s],
            device_id=mate,
            device_id_type=MESH,
        )

    send_inv = pltpu.make_async_remote_copy(
        src_ref=own_inv,
        dst_ref=mate_inv,
        send_sem=inv_sem.at[0],
        recv_sem=inv_sem.at[1],
        device_id=mate,
        device_id_type=MESH,
    )

    def each(count, body):
        def step(i, carry):
            body(i)
            return carry

        lax.fori_loop(0, count, step, 0)

    def own_z(q, act, n=1):
        def body(j):
            up = lax.rem(j, 2)
            pl.when(can_send(up))(lambda: act(send_z(z, q * SUBS + j // 2, up, n)))

        each(2 * SUBS // n, body)

    def own_y(q, act, n=SUBS):
        each(SUBS // n, lambda j: act(send_y(z, q * SUBS + j, n)))

    def start(copy):
        copy.start()

    def sent(copy):
        copy.wait_send()

    def remote(d, body, subs=SUBS):
        def step(j):
            up = lax.rem(j, 2)
            zz = z + d - 2 * d * up
            pl.when((zz >= 0) & (zz < n_z))(lambda: body(j // 2, zz, up))

        each(2 * subs, step)

    def along_z(d, q, to_y, to_x, n=1):
        def body(sub, zz, up):
            p = q * SUBS + sub
            arrived(zz * 2 + y, p, n)
            pl.when(can_send(up))(lambda: send_z(zz, p, up, n).start())
            if to_y:
                send_y(zz, p).start()
            if to_x:
                send_x(zz * 2 + y, p).start()

        remote(d, body, SUBS // n)

    def gain_along_z(d):
        def step(up):
            zz = z + d - 2 * d * up

            @pl.when((zz >= 0) & (zz < n_z))
            def _():
                gain_arrived(zz * 2 + y)
                pl.when(can_send(up))(lambda: gain_z(zz, up).start())
                gain_y(zz).start()

        each(2, step)

    def along_y(d, q):
        def body(sub, zz, up):
            p = q * SUBS + sub
            arrived(zz * 2 + 1 - y, p)
            send_x(zz * 2 + 1 - y, p).start()

        remote(d, body)

    load_q.wait()
    load_kv.wait()
    own_z(role_a, start)
    own_y(role_a, start, 1)
    own_z(role_b, start)
    for up in (0, 1):
        pl.when(can_send(up))(lambda up=up: gain_z(z, up).start())
    gain_y(z).start()

    def rows_out(i):
        for k in (2 * i, 2 * i + 1):
            send_rows(lax.rem(own + k, n_shards)).start()

    rows_out(0)

    load_rows.wait()
    width = own_rows.shape[1]

    def square(i):
        rows = pl.ds(pl.multiple_of(i * 32, 32), 32)
        values = own_rows[rows, :].astype(jnp.float32)
        mean = jnp.sum(values * values, axis=1, keepdims=True) / width
        own_inv[rows, :] = jnp.broadcast_to(lax.rsqrt(mean + NORM_EPS), (32, 128))

    each(tokens // 32, square)
    send_inv.start()
    rows_out(1)

    for load in load_tables:
        load.wait()
    n_rows = lengths_ref.shape[0]
    across = lax.broadcasted_iota(jnp.int32, (1, tokens), 1)
    down = lax.broadcasted_iota(jnp.int32, (tokens, 1), 0)
    row_across = jnp.zeros_like(across)
    row_down = jnp.zeros_like(down)
    start_down = jnp.zeros_like(down)
    target = jnp.zeros_like(across)
    goes_to = jnp.zeros_like(across)
    first = jnp.int32(0)
    for r in range(n_rows):
        in_across = across >= first
        in_down = down >= first
        row_across = jnp.where(in_across, r, row_across)
        row_down = jnp.where(in_down, r, row_down)
        start_down = jnp.where(in_down, first, start_down)
        target = jnp.where(in_across, offset_ref[r] + across - first, target)
        goes_to = jnp.where(in_across, learner_ref[r], goes_to)
        first = first + lengths_ref[r]
    position = (down - start_down).astype(jnp.float32)
    lane = lax.broadcasted_iota(jnp.int32, (1, HD), 1)
    half = HD // 2
    index = jnp.where(lane < half, lane, lane - half).astype(jnp.float32)
    angle = position * jnp.exp(index * (-2.0 * math.log(ROPE_BASE) / HD))
    cosine[...] = jnp.cos(angle)
    sine[...] = jnp.where(lane < half, -jnp.sin(angle), jnp.sin(angle))

    along_z(1, role_a, True, True)
    gain_along_z(1)
    rows_out(2)
    for i in range(3, n_shards // 2):
        rows_out(i)

    allowed = (row_across == row_down) & (across <= down)
    masked[...] = jnp.where(allowed, 0.0, 1.0)
    if n_dp == 2:
        slot_iota = lax.broadcasted_iota(jnp.int32, (tokens, tokens), 0)
        place_here[...] = jnp.where(
            slot_iota == jnp.where(goes_to == dp, target, -1), 1.0, 0.0
        ).astype(jnp.bfloat16)
        place_there[...] = jnp.where(
            slot_iota == jnp.where(goes_to == 1 - dp, target, -1), 1.0, 0.0
        ).astype(jnp.bfloat16)

    block = depth // 2

    def project(slot, h, whose):
        inner = pl.ds(pl.multiple_of(h * block, block), block)
        gain = gains[slot, 0:1, inner]
        if whose == 0:
            column = pl.multiple_of((slot * 2 + core) * depth + h * block, block)
            rows, inverse = own_rows[:, pl.ds(column, block)], own_inv[:, 0:1]
        else:
            rows, inverse = mate_rows[slot, :, inner], mate_inv[:, 0:1]
        normed = (rows.astype(jnp.float32) * inverse * gain).astype(jnp.bfloat16)
        total[whose] += jnp.dot(normed, weights[slot, inner, :], preferred_element_type=jnp.float32)

    def project_both(slot, h):
        project(slot, h, 1)
        project(slot, h, 0)

    def project_remote(d, column, h, quarters):
        def step(up):
            zz = z + d - 2 * d * up

            @pl.when((zz >= 0) & (zz < n_z))
            def _():
                slot = zz * 2 + (y if column == 0 else 1 - y)
                for q in quarters:
                    each(SUBS, lambda j: arrived(slot, q * SUBS + j))
                project_both(slot, h)

        each(2, step)

    along_z(1, role_b, True, False)
    own_z(role_c, start, SUBS)
    own_y(role_b, start)
    along_y(1, role_a)
    along_z(2, role_a, True, True)
    gain_along_z(2)
    along_y(1, role_b)
    total[...] = jnp.zeros_like(total)
    send_inv.wait_recv()
    for s in range(n_shards):
        send_rows(s).wait_recv()
    project_both(own, 0)
    along_z(2, role_b, True, False)
    own_y(role_c, start)
    project_both(own, 1)
    along_y(2, role_a)
    along_z(1, role_c, False, False, SUBS)
    project_remote(1, 0, x, ())
    for d in range(3, n_z):
        along_z(d, role_a, True, True)
        gain_along_z(d)
        along_y(d - 1, role_b)
        along_z(d, role_b, True, False)
    along_z(2, role_c, False, False, SUBS)
    own_y(role_d, start)
    for zz in range(n_z):
        gain_arrived(zz * 2 + 1 - y)
    project_remote(1, 1, x, ())
    for d in range(3, n_z):
        along_y(d, role_a)
    project_remote(2, 0, x, ())
    along_y(n_z - 1, role_b)
    project_remote(2, 1, x, ())
    project_remote(1, 1, 1 - x, (role_d, role_c))
    project_remote(1, 0, 1 - x, (role_d,))
    for d in range(3, n_z):
        project_remote(d, 0, x, ())
        project_remote(d, 1, x, ())
        along_z(d, role_c, False, False, SUBS)
    project_remote(2, 0, 1 - x, (role_d,))
    project_remote(2, 1, 1 - x, (role_d, role_c))
    each(SUBS, lambda j: arrived(other, role_a * SUBS + j))
    arrived(other, role_b * SUBS, SUBS)
    project_both(other, x)
    for d in range(3, n_z):
        project_remote(d, 0, 1 - x, (role_d,))
    for d in range(3, n_z):
        project_remote(d, 1, 1 - x, (role_d, role_c))
    for q in (role_c, role_d):
        arrived(other, q * SUBS, SUBS)
    project(other, 1 - x, 1)

    def send_sum(c):
        cols = pl.ds(c * 256, 256)
        return pltpu.make_async_remote_copy(
            src_ref=total.at[1, :, cols],
            dst_ref=mate_total.at[:, cols],
            send_sem=sum_send.at[c],
            recv_sem=sum_recv.at[c],
            device_id=mate,
            device_id_type=MESH,
        )

    n_sums = n_cols // 256
    order = [n_sums - 1] + list(range(n_sums - 1))
    for c in order:
        send_sum(c).start()
    project(other, 1 - x, 0)

    def rotated(values):
        return (values * cosine[...] + pltpu.roll(values, half, 1) * sine[...]).astype(jnp.bfloat16)

    def summed(col):
        return total[0, :, col : col + HD] + mate_total[:, col : col + HD]

    send_sum(n_sums - 1).wait_recv()
    key = rotated(summed(q_cols))
    value = summed(q_cols + HD).astype(jnp.bfloat16)

    def send_head(h):
        return pltpu.make_async_remote_copy(
            src_ref=sent_heads.at[h],
            dst_ref=got_heads.at[h],
            send_sem=head_send.at[h],
            recv_sem=head_recv.at[h],
            device_id=x_peer,
            device_id_type=MESH,
        )

    for h in range(QH):
        if h % 2 == 0:
            send_sum(h // 2).wait_recv()
        query = rotated(summed(h * HD))
        scores = lax.dot_general(
            query, key, (((1,), (1,)), ((), ())), preferred_element_type=jnp.float32
        ) * HD ** (-0.5)
        scores = jnp.where(masked[...] > 0.5, -1e30, scores)
        exped = jnp.exp(scores - jnp.max(scores, axis=1, keepdims=True))
        chance = (exped / jnp.sum(exped, axis=1, keepdims=True)).astype(jnp.bfloat16)
        mixed = jnp.dot(chance, value, preferred_element_type=jnp.float32).astype(jnp.bfloat16)
        cols = pl.ds(h * HD, HD)
        if n_dp == 2:
            sent_heads[h] = jnp.dot(
                place_there[...], mixed, preferred_element_type=jnp.float32
            ).astype(jnp.bfloat16)
            send_head(h).start()
            out_ref[:, cols] = jnp.dot(
                place_here[...], mixed, preferred_element_type=jnp.float32
            ).astype(jnp.bfloat16)
        else:
            out_ref[:, cols] = mixed

    for q in (role_a, role_b):
        own_z(q, sent)
    own_z(role_c, sent, SUBS)
    own_y(role_a, sent, 1)
    for q in (role_b, role_c, role_d):
        own_y(q, sent)
    for zz in range(n_z):
        pl.when(can_send(0) & (zz >= z))(lambda zz=zz: gain_z(zz, 0).wait_send())
        pl.when(can_send(1) & (zz <= z))(lambda zz=zz: gain_z(zz, 1).wait_send())
        gain_y(zz).wait_send()
    for s in range(n_shards):
        send_rows(s).wait_send()
    send_inv.wait_send()

    def relayed(sub, zz, up):
        a, b = role_a * SUBS + sub, role_b * SUBS + sub
        for p in (a, b):
            pl.when(can_send(up))(lambda p=p: send_z(zz, p, up).wait_send())
        send_y(zz, a).wait_send()
        send_y(zz, b).wait_send()
        send_x(zz * 2 + y, a).wait_send()
        send_x(zz * 2 + 1 - y, a).wait_send()
        send_x(zz * 2 + 1 - y, b).wait_send()

    def relayed_whole(sub, zz, up):
        pl.when(can_send(up))(lambda: send_z(zz, role_c * SUBS, up, SUBS).wait_send())

    for d in range(1, n_z):
        remote(d, relayed)
        remote(d, relayed_whole, 1)

    for c in order:
        send_sum(c).wait_send()
    if n_dp == 2:
        for h in range(QH):
            cols = pl.ds(h * HD, HD)
            send_head(h).wait_recv()
            out_ref[:, cols] = out_ref[:, cols] + got_heads[h]
        for h in range(QH):
            send_head(h).wait_send()


def fused(n_dp, n_fsdp, hidden, lengths, learner, slot_offset, norm_gain, query_weight, keyval_weight):
    tokens, width = hidden.shape
    depth, q_cols = query_weight.shape
    n_cols = q_cols + keyval_weight.shape[1]
    n_z = n_fsdp // 4
    n_shards = 2 * n_z
    bf16, f32 = jnp.bfloat16, jnp.float32
    dma = pltpu.SemaphoreType.DMA
    vmem = pl.BlockSpec(memory_space=pltpu.VMEM)
    hbm = pl.BlockSpec(memory_space=pl.ANY)
    return pl.pallas_call(
        functools.partial(kernel, n_dp, n_fsdp),
        out_shape=jax.ShapeDtypeStruct((tokens, q_cols), bf16),
        in_specs=[hbm, hbm, hbm, hbm, vmem, hbm, hbm],
        out_specs=vmem,
        scratch_shapes=[
            pltpu.SMEM(lengths.shape, jnp.int32),
            pltpu.SMEM(lengths.shape, jnp.int32),
            pltpu.SMEM(lengths.shape, jnp.int32),
            pltpu.VMEM((n_shards, depth, n_cols), bf16),
            pltpu.VMEM((n_shards, 8, depth), f32),
            pltpu.VMEM((tokens, width), bf16),
            pltpu.VMEM((n_shards, tokens, depth), bf16),
            pltpu.VMEM((tokens, 128), f32),
            pltpu.VMEM((tokens, 128), f32),
            pltpu.VMEM((2, tokens, n_cols), f32),
            pltpu.VMEM((tokens, n_cols), f32),
            pltpu.VMEM((tokens, HD), f32),
            pltpu.VMEM((tokens, HD), f32),
            pltpu.VMEM((tokens, tokens), f32),
            pltpu.VMEM((tokens, tokens), bf16),
            pltpu.VMEM((tokens, tokens), bf16),
            pltpu.VMEM((QH, tokens, HD), bf16),
            pltpu.VMEM((QH, tokens, HD), bf16),
            dma((6,)),
            dma((n_shards, 4 * SUBS)),
            dma((2, n_z, 4 * SUBS)),
            dma((n_z, 4 * SUBS)),
            dma((n_shards, 4 * SUBS)),
            dma((3, n_z)),
            dma((n_shards,)),
            dma((n_shards,)),
            dma((n_shards,)),
            dma((2,)),
            dma((n_cols // 256,)),
            dma((n_cols // 256,)),
            dma((QH,)),
            dma((QH,)),
        ],
        compiler_params=pltpu.CompilerParams(
            collective_id=0, has_side_effects=True, vmem_limit_bytes=60 * 1024 * 1024
        ),
    )(lengths, learner, slot_offset, hidden, norm_gain, query_weight, keyval_weight)


def route(buffer, tables):
    channels = buffer.shape[1]
    peer_count = lax.axis_size("dp")
    pair_count = tables.shape[1] // (2 * peer_count)
    block_len = buffer.shape[0] // pair_count
    slice_len = block_len // peer_count
    blocks = buffer.reshape(pair_count, peer_count, slice_len, channels)
    spread = lax.all_to_all(blocks, "dp", split_axis=1, concat_axis=0, tiled=True)
    lengths_all = tables[0].reshape(peer_count * pair_count, 2)
    targets = tables[1].reshape(peer_count * pair_count, 2)[:, 0]
    offsets_all = tables[2].reshape(peer_count * pair_count, 2)
    ordering = jnp.argsort(targets, stable=True)
    arranged = jnp.take(spread, ordering, axis=0).reshape(
        peer_count, pair_count, 1, slice_len, channels
    )
    received = lax.all_to_all(arranged, "dp", split_axis=0, concat_axis=2, tiled=True)
    received = received.reshape(pair_count * block_len, channels)
    own_blocks = lax.dynamic_slice_in_dim(ordering, lax.axis_index("dp") * pair_count, pair_count)
    pair_lengths = jnp.take(lengths_all, own_blocks, axis=0)
    sources = jnp.stack([jnp.zeros_like(pair_lengths[:, 0]), pair_lengths[:, 0]], axis=1)
    sources = (sources + (jnp.arange(pair_count, dtype=jnp.int32) * block_len)[:, None]).reshape(-1)
    row_lengths = pair_lengths.reshape(-1)
    row_offsets = jnp.take(offsets_all, own_blocks, axis=0).reshape(-1)
    places = jnp.arange(pair_count * block_len, dtype=jnp.int32)
    relative = places[:, None] - row_offsets[None, :]
    inside = (relative >= 0) & (relative < row_lengths[None, :])
    take_index = jnp.sum(jnp.where(inside, sources[None, :] + relative, 0), axis=1)
    return jnp.take(received, take_index, axis=0)


def solution(mesh):
    n_dp, n_fsdp = mesh.shape["dp"], mesh.shape["fsdp"]

    def shards(hidden, lengths, learner, slot_offset, norm_gain, query_weight, keyval_weight):
        attended = fused(
            n_dp, n_fsdp, hidden, lengths, learner, slot_offset, norm_gain, query_weight, keyval_weight
        )
        if n_dp == 2:
            return attended
        tables = lax.all_gather(
            jnp.stack([lengths, learner, slot_offset]), "dp", axis=1, tiled=True
        )
        return route(attended, tables)

    placed = (
        P(("dp", "fsdp"), None),
        P(("dp", "fsdp")),
        P(("dp", "fsdp")),
        P(("dp", "fsdp")),
        P("fsdp"),
        P("fsdp", None),
        P("fsdp", None),
    )
    return jax.shard_map(
        shards, mesh=mesh, in_specs=placed, out_specs=P(("dp", "fsdp"), None), check_vma=False
    )
```

```python
import functools
import math

import jax
import jax.numpy as jnp
from jax import lax
from jax.experimental import pallas as pl
from jax.experimental.pallas import tpu as pltpu
from jax.sharding import PartitionSpec as P

HD = 128
QH = 4
ROPE_BASE = 500000.0
NORM_EPS = 1e-05
MESH = pl.DeviceIdType.MESH
SUBS = 2


def kernel(
    n_dp,
    n_fsdp,
    lengths_hbm,
    learner_hbm,
    offset_hbm,
    hidden_ref,
    gain_ref,
    query_ref,
    keyval_ref,
    out_ref,
    lengths_ref,
    learner_ref,
    offset_ref,
    weights,
    gains,
    own_rows,
    mate_rows,
    own_inv,
    mate_inv,
    total,
    mate_total,
    cosine,
    sine,
    masked,
    place_here,
    place_there,
    sent_heads,
    got_heads,
    local_sem,
    part_recv,
    z_send,
    y_send,
    x_send,
    gain_send,
    gain_recv,
    rows_send,
    rows_recv,
    inv_sem,
    sum_send,
    sum_recv,
    head_send,
    head_recv,
):
    dp = lax.axis_index("dp")
    fs = lax.axis_index("fsdp")
    core = lax.rem(fs, 2)
    y = lax.rem(fs // 2, 2)
    z = fs // 4
    n_z = n_fsdp // 4
    x = lax.rem(dp, 2)
    x_peer = {"dp": dp + 1 - 2 * x}
    mate = {"fsdp": fs + 1 - 2 * core}
    y_peer = {"fsdp": fs + 2 - 4 * y}
    tokens = own_rows.shape[0]
    depth = query_ref.shape[0]
    n_cols = weights.shape[2]
    q_cols = QH * HD
    part = depth // (4 * SUBS)
    own = z * 2 + y
    other = z * 2 + 1 - y
    n_shards = 2 * n_z
    role_a = 3 * x
    role_b = 1 + x
    role_c = 2 - x
    role_d = 3 - 3 * x

    def can_send(up):
        return (z + 2 * up - 1 >= 0) & (z + 2 * up - 1 < n_z)

    load_q = pltpu.make_async_copy(query_ref, weights.at[own, :, pl.ds(0, q_cols)], local_sem.at[0])
    load_kv = pltpu.make_async_copy(
        keyval_ref, weights.at[own, :, pl.ds(q_cols, n_cols - q_cols)], local_sem.at[1]
    )
    load_rows = pltpu.make_async_copy(hidden_ref, own_rows, local_sem.at[2])
    load_tables = [
        pltpu.make_async_copy(src, dst, local_sem.at[3 + i])
        for i, (src, dst) in enumerate(
            ((lengths_hbm, lengths_ref), (learner_hbm, learner_ref), (offset_hbm, offset_ref))
        )
    ]
    load_q.start()
    load_kv.start()
    load_rows.start()
    for load in load_tables:
        load.start()

    barrier = pltpu.get_barrier_semaphore()
    pl.semaphore_signal(barrier, inc=1, device_id=x_peer, device_id_type=MESH)
    pl.semaphore_signal(barrier, inc=1, device_id=mate, device_id_type=MESH)
    pl.semaphore_signal(barrier, inc=1, device_id=y_peer, device_id_type=MESH)
    for up in (0, 1):

        @pl.when(can_send(up))
        def _(up=up):
            pl.semaphore_signal(
                barrier, inc=1, device_id={"fsdp": fs + 8 * up - 4}, device_id_type=MESH
            )

    gains[own] = jnp.broadcast_to(gain_ref[...].astype(jnp.float32).reshape(1, depth), (8, depth))
    inner = (z > 0) & (z < n_z - 1)
    pl.semaphore_wait(barrier, jnp.where(inner, 5, 4))

    def piece(slot, p, n=1):
        return weights.at[slot, pl.ds(pl.multiple_of(p * part, part), n * part), :]

    def send_z(zz, p, up, n=1):
        slot = zz * 2 + y
        return pltpu.make_async_remote_copy(
            src_ref=piece(slot, p, n),
            dst_ref=piece(slot, p, n),
            send_sem=z_send.at[up, zz, p],
            recv_sem=part_recv.at[slot, p],
            device_id={"fsdp": fs + 8 * up - 4},
            device_id_type=MESH,
        )

    def send_y(zz, p, n=1):
        slot = zz * 2 + y
        return pltpu.make_async_remote_copy(
            src_ref=piece(slot, p, n),
            dst_ref=piece(slot, p, n),
            send_sem=y_send.at[zz, p],
            recv_sem=part_recv.at[slot, p],
            device_id=y_peer,
            device_id_type=MESH,
        )

    def send_x(slot, p, n=1):
        return pltpu.make_async_remote_copy(
            src_ref=piece(slot, p, n),
            dst_ref=piece(slot, p, n),
            send_sem=x_send.at[slot, p],
            recv_sem=part_recv.at[slot, p],
            device_id=x_peer,
            device_id_type=MESH,
        )

    def arrived(slot, p, n=1):
        send_x(slot, p, n).wait_recv()

    def send_gain(zz, device, sem):
        slot = zz * 2 + y
        return pltpu.make_async_remote_copy(
            src_ref=gains.at[slot],
            dst_ref=gains.at[slot],
            send_sem=sem,
            recv_sem=gain_recv.at[slot],
            device_id=device,
            device_id_type=MESH,
        )

    def gain_z(zz, up):
        return send_gain(zz, {"fsdp": fs + 8 * up - 4}, gain_send.at[up, zz])

    def gain_y(zz):
        return send_gain(zz, y_peer, gain_send.at[2, zz])

    def gain_arrived(slot):
        pltpu.make_async_remote_copy(
            src_ref=gains.at[slot],
            dst_ref=gains.at[slot],
            send_sem=gain_send.at[2, 0],
            recv_sem=gain_recv.at[slot],
            device_id=y_peer,
            device_id_type=MESH,
        ).wait_recv()

    def send_rows(s):
        start = pl.multiple_of((s * 2 + 1 - core) * depth, depth)
        return pltpu.make_async_remote_copy(
            src_ref=hidden_ref.at[:, pl.ds(start, depth)],
            dst_ref=mate_rows.at[s],
            send_sem=rows_send.at[s],
            recv_sem=rows_recv.at[s],
            device_id=mate,
            device_id_type=MESH,
        )

    send_inv = pltpu.make_async_remote_copy(
        src_ref=own_inv,
        dst_ref=mate_inv,
        send_sem=inv_sem.at[0],
        recv_sem=inv_sem.at[1],
        device_id=mate,
        device_id_type=MESH,
    )

    def each(count, body):
        def step(i, carry):
            body(i)
            return carry

        lax.fori_loop(0, count, step, 0)

    def own_z(q, act, n=1):
        def body(j):
            up = lax.rem(j, 2)
            pl.when(can_send(up))(lambda: act(send_z(z, q * SUBS + j // 2, up, n)))

        each(2 * SUBS // n, body)

    def own_y(q, act, n=SUBS):
        each(SUBS // n, lambda j: act(send_y(z, q * SUBS + j, n)))

    def start(copy):
        copy.start()

    def sent(copy):
        copy.wait_send()

    def remote(d, body, subs=SUBS):
        def step(j):
            up = lax.rem(j, 2)
            zz = z + d - 2 * d * up
            pl.when((zz >= 0) & (zz < n_z))(lambda: body(j // 2, zz, up))

        each(2 * subs, step)

    def along_z(d, q, to_y, to_x, n=1):
        def body(sub, zz, up):
            p = q * SUBS + sub
            arrived(zz * 2 + y, p, n)
            pl.when(can_send(up))(lambda: send_z(zz, p, up, n).start())
            if to_y:
                send_y(zz, p).start()
            if to_x:
                send_x(zz * 2 + y, p).start()

        remote(d, body, SUBS // n)

    def gain_along_z(d):
        def step(up):
            zz = z + d - 2 * d * up

            @pl.when((zz >= 0) & (zz < n_z))
            def _():
                gain_arrived(zz * 2 + y)
                pl.when(can_send(up))(lambda: gain_z(zz, up).start())
                gain_y(zz).start()

        each(2, step)

    def along_y(d, q):
        def body(sub, zz, up):
            p = q * SUBS + sub
            arrived(zz * 2 + 1 - y, p)
            send_x(zz * 2 + 1 - y, p).start()

        remote(d, body)

    load_q.wait()
    load_kv.wait()
    own_z(role_a, start)
    own_y(role_a, start, 1)
    own_z(role_b, start)
    for up in (0, 1):
        pl.when(can_send(up))(lambda up=up: gain_z(z, up).start())
    gain_y(z).start()

    def rows_out(i):
        for k in (2 * i, 2 * i + 1):
            send_rows(lax.rem(own + k, n_shards)).start()

    rows_out(0)

    load_rows.wait()
    width = own_rows.shape[1]

    def square(i):
        rows = pl.ds(pl.multiple_of(i * 32, 32), 32)
        values = own_rows[rows, :].astype(jnp.float32)
        mean = jnp.sum(values * values, axis=1, keepdims=True) / width
        own_inv[rows, :] = jnp.broadcast_to(lax.rsqrt(mean + NORM_EPS), (32, 128))

    each(tokens // 32, square)
    send_inv.start()
    rows_out(1)

    for load in load_tables:
        load.wait()
    n_rows = lengths_ref.shape[0]
    across = lax.broadcasted_iota(jnp.int32, (1, tokens), 1)
    down = lax.broadcasted_iota(jnp.int32, (tokens, 1), 0)
    row_across = jnp.zeros_like(across)
    row_down = jnp.zeros_like(down)
    start_down = jnp.zeros_like(down)
    target = jnp.zeros_like(across)
    goes_to = jnp.zeros_like(across)
    first = jnp.int32(0)
    for r in range(n_rows):
        in_across = across >= first
        in_down = down >= first
        row_across = jnp.where(in_across, r, row_across)
        row_down = jnp.where(in_down, r, row_down)
        start_down = jnp.where(in_down, first, start_down)
        target = jnp.where(in_across, offset_ref[r] + across - first, target)
        goes_to = jnp.where(in_across, learner_ref[r], goes_to)
        first = first + lengths_ref[r]
    position = (down - start_down).astype(jnp.float32)
    lane = lax.broadcasted_iota(jnp.int32, (1, HD), 1)
    half = HD // 2
    index = jnp.where(lane < half, lane, lane - half).astype(jnp.float32)
    angle = position * jnp.exp(index * (-2.0 * math.log(ROPE_BASE) / HD))
    cosine[...] = jnp.cos(angle)
    sine[...] = jnp.where(lane < half, -jnp.sin(angle), jnp.sin(angle))

    along_z(1, role_a, True, True)
    gain_along_z(1)
    rows_out(2)
    for i in range(3, n_shards // 2):
        rows_out(i)

    allowed = (row_across == row_down) & (across <= down)
    masked[...] = jnp.where(allowed, 0.0, 1.0)
    if n_dp == 2:
        slot_iota = lax.broadcasted_iota(jnp.int32, (tokens, tokens), 0)
        place_here[...] = jnp.where(
            slot_iota == jnp.where(goes_to == dp, target, -1), 1.0, 0.0
        ).astype(jnp.bfloat16)
        place_there[...] = jnp.where(
            slot_iota == jnp.where(goes_to == 1 - dp, target, -1), 1.0, 0.0
        ).astype(jnp.bfloat16)

    block = depth // 2

    def normed(slot, h, whose):
        inner = pl.ds(pl.multiple_of(h * block, block), block)
        gain = gains[slot, 0:1, inner]
        if whose == 0:
            column = pl.multiple_of((slot * 2 + core) * depth + h * block, block)
            rows, inverse = own_rows[:, pl.ds(column, block)], own_inv[:, 0:1]
        else:
            rows, inverse = mate_rows[slot, :, inner], mate_inv[:, 0:1]
        return (rows.astype(jnp.float32) * inverse * gain).astype(jnp.bfloat16)

    def product(rows, slot, h):
        inner = pl.ds(pl.multiple_of(h * block, block), block)
        return jnp.dot(rows, weights[slot, inner, :], preferred_element_type=jnp.float32)

    def project(slot, h, whose):
        total[whose] += product(normed(slot, h, whose), slot, h)

    def project_both(slot, h):
        rows = jnp.concatenate([normed(slot, h, 0), normed(slot, h, 1)], axis=0)
        total[...] += product(rows, slot, h).reshape(total.shape)

    def project_remote(d, column, h, quarters):
        def step(up):
            zz = z + d - 2 * d * up

            @pl.when((zz >= 0) & (zz < n_z))
            def _():
                slot = zz * 2 + (y if column == 0 else 1 - y)
                for q in quarters:
                    each(SUBS, lambda j: arrived(slot, q * SUBS + j))
                project_both(slot, h)

        each(2, step)

    along_z(1, role_b, True, False)
    own_z(role_c, start, SUBS)
    own_y(role_b, start)
    along_y(1, role_a)
    along_z(2, role_a, True, True)
    gain_along_z(2)
    along_y(1, role_b)
    total[...] = jnp.zeros_like(total)
    send_inv.wait_recv()
    for s in range(n_shards):
        send_rows(s).wait_recv()
    project_both(own, 0)
    along_z(2, role_b, True, False)
    own_y(role_c, start)
    project_both(own, 1)
    along_y(2, role_a)
    along_z(1, role_c, False, False, SUBS)
    project_remote(1, 0, x, ())
    for d in range(3, n_z):
        along_z(d, role_a, True, True)
        gain_along_z(d)
        along_y(d - 1, role_b)
        along_z(d, role_b, True, False)
    along_z(2, role_c, False, False, SUBS)
    own_y(role_d, start)
    for zz in range(n_z):
        gain_arrived(zz * 2 + 1 - y)
    project_remote(1, 1, x, ())
    for d in range(3, n_z):
        along_y(d, role_a)
    project_remote(2, 0, x, ())
    along_y(n_z - 1, role_b)
    project_remote(2, 1, x, ())
    project_remote(1, 1, 1 - x, (role_d, role_c))
    project_remote(1, 0, 1 - x, (role_d,))
    for d in range(3, n_z):
        project_remote(d, 0, x, ())
        project_remote(d, 1, x, ())
        along_z(d, role_c, False, False, SUBS)
    project_remote(2, 0, 1 - x, (role_d,))
    project_remote(2, 1, 1 - x, (role_d, role_c))
    each(SUBS, lambda j: arrived(other, role_a * SUBS + j))
    arrived(other, role_b * SUBS, SUBS)
    project_both(other, x)
    for d in range(3, n_z):
        project_remote(d, 0, 1 - x, (role_d,))
    for d in range(3, n_z):
        project_remote(d, 1, 1 - x, (role_d, role_c))
    for q in (role_c, role_d):
        arrived(other, q * SUBS, SUBS)
    project(other, 1 - x, 1)

    def send_sum(c):
        cols = pl.ds(c * 256, 256)
        return pltpu.make_async_remote_copy(
            src_ref=total.at[1, :, cols],
            dst_ref=mate_total.at[:, cols],
            send_sem=sum_send.at[c],
            recv_sem=sum_recv.at[c],
            device_id=mate,
            device_id_type=MESH,
        )

    n_sums = n_cols // 256
    order = [n_sums - 1] + list(range(n_sums - 1))
    for c in order:
        send_sum(c).start()
    project(other, 1 - x, 0)

    def rotated(values):
        return (values * cosine[...] + pltpu.roll(values, half, 1) * sine[...]).astype(jnp.bfloat16)

    def summed(col):
        return total[0, :, col : col + HD] + mate_total[:, col : col + HD]

    send_sum(n_sums - 1).wait_recv()
    key = rotated(summed(q_cols))
    value = summed(q_cols + HD).astype(jnp.bfloat16)

    def send_head(h):
        return pltpu.make_async_remote_copy(
            src_ref=sent_heads.at[h],
            dst_ref=got_heads.at[h],
            send_sem=head_send.at[h],
            recv_sem=head_recv.at[h],
            device_id=x_peer,
            device_id_type=MESH,
        )

    for h in range(QH):
        if h % 2 == 0:
            send_sum(h // 2).wait_recv()
        query = rotated(summed(h * HD))
        scores = lax.dot_general(
            query, key, (((1,), (1,)), ((), ())), preferred_element_type=jnp.float32
        ) * HD ** (-0.5)
        scores = jnp.where(masked[...] > 0.5, -1e30, scores)
        exped = jnp.exp(scores - jnp.max(scores, axis=1, keepdims=True))
        chance = (exped / jnp.sum(exped, axis=1, keepdims=True)).astype(jnp.bfloat16)
        mixed = jnp.dot(chance, value, preferred_element_type=jnp.float32).astype(jnp.bfloat16)
        cols = pl.ds(h * HD, HD)
        if n_dp == 2:
            sent_heads[h] = jnp.dot(
                place_there[...], mixed, preferred_element_type=jnp.float32
            ).astype(jnp.bfloat16)
            send_head(h).start()
            out_ref[:, cols] = jnp.dot(
                place_here[...], mixed, preferred_element_type=jnp.float32
            ).astype(jnp.bfloat16)
        else:
            out_ref[:, cols] = mixed

    for q in (role_a, role_b):
        own_z(q, sent)
    own_z(role_c, sent, SUBS)
    own_y(role_a, sent, 1)
    for q in (role_b, role_c, role_d):
        own_y(q, sent)
    for zz in range(n_z):
        pl.when(can_send(0) & (zz >= z))(lambda zz=zz: gain_z(zz, 0).wait_send())
        pl.when(can_send(1) & (zz <= z))(lambda zz=zz: gain_z(zz, 1).wait_send())
        gain_y(zz).wait_send()
    for s in range(n_shards):
        send_rows(s).wait_send()
    send_inv.wait_send()

    def relayed(sub, zz, up):
        a, b = role_a * SUBS + sub, role_b * SUBS + sub
        for p in (a, b):
            pl.when(can_send(up))(lambda p=p: send_z(zz, p, up).wait_send())
        send_y(zz, a).wait_send()
        send_y(zz, b).wait_send()
        send_x(zz * 2 + y, a).wait_send()
        send_x(zz * 2 + 1 - y, a).wait_send()
        send_x(zz * 2 + 1 - y, b).wait_send()

    def relayed_whole(sub, zz, up):
        pl.when(can_send(up))(lambda: send_z(zz, role_c * SUBS, up, SUBS).wait_send())

    for d in range(1, n_z):
        remote(d, relayed)
        remote(d, relayed_whole, 1)

    for c in order:
        send_sum(c).wait_send()
    if n_dp == 2:
        for h in range(QH):
            cols = pl.ds(h * HD, HD)
            send_head(h).wait_recv()
            out_ref[:, cols] = out_ref[:, cols] + got_heads[h]
        for h in range(QH):
            send_head(h).wait_send()


def fused(n_dp, n_fsdp, hidden, lengths, learner, slot_offset, norm_gain, query_weight, keyval_weight):
    tokens, width = hidden.shape
    depth, q_cols = query_weight.shape
    n_cols = q_cols + keyval_weight.shape[1]
    n_z = n_fsdp // 4
    n_shards = 2 * n_z
    bf16, f32 = jnp.bfloat16, jnp.float32
    dma = pltpu.SemaphoreType.DMA
    vmem = pl.BlockSpec(memory_space=pltpu.VMEM)
    hbm = pl.BlockSpec(memory_space=pl.ANY)
    return pl.pallas_call(
        functools.partial(kernel, n_dp, n_fsdp),
        out_shape=jax.ShapeDtypeStruct((tokens, q_cols), bf16),
        in_specs=[hbm, hbm, hbm, hbm, vmem, hbm, hbm],
        out_specs=vmem,
        scratch_shapes=[
            pltpu.SMEM(lengths.shape, jnp.int32),
            pltpu.SMEM(lengths.shape, jnp.int32),
            pltpu.SMEM(lengths.shape, jnp.int32),
            pltpu.VMEM((n_shards, depth, n_cols), bf16),
            pltpu.VMEM((n_shards, 8, depth), f32),
            pltpu.VMEM((tokens, width), bf16),
            pltpu.VMEM((n_shards, tokens, depth), bf16),
            pltpu.VMEM((tokens, 128), f32),
            pltpu.VMEM((tokens, 128), f32),
            pltpu.VMEM((2, tokens, n_cols), f32),
            pltpu.VMEM((tokens, n_cols), f32),
            pltpu.VMEM((tokens, HD), f32),
            pltpu.VMEM((tokens, HD), f32),
            pltpu.VMEM((tokens, tokens), f32),
            pltpu.VMEM((tokens, tokens), bf16),
            pltpu.VMEM((tokens, tokens), bf16),
            pltpu.VMEM((QH, tokens, HD), bf16),
            pltpu.VMEM((QH, tokens, HD), bf16),
            dma((6,)),
            dma((n_shards, 4 * SUBS)),
            dma((2, n_z, 4 * SUBS)),
            dma((n_z, 4 * SUBS)),
            dma((n_shards, 4 * SUBS)),
            dma((3, n_z)),
            dma((n_shards,)),
            dma((n_shards,)),
            dma((n_shards,)),
            dma((2,)),
            dma((n_cols // 256,)),
            dma((n_cols // 256,)),
            dma((QH,)),
            dma((QH,)),
        ],
        compiler_params=pltpu.CompilerParams(
            collective_id=0, has_side_effects=True, vmem_limit_bytes=60 * 1024 * 1024
        ),
    )(lengths, learner, slot_offset, hidden, norm_gain, query_weight, keyval_weight)


def route(buffer, tables):
    channels = buffer.shape[1]
    peer_count = lax.axis_size("dp")
    pair_count = tables.shape[1] // (2 * peer_count)
    block_len = buffer.shape[0] // pair_count
    slice_len = block_len // peer_count
    blocks = buffer.reshape(pair_count, peer_count, slice_len, channels)
    spread = lax.all_to_all(blocks, "dp", split_axis=1, concat_axis=0, tiled=True)
    lengths_all = tables[0].reshape(peer_count * pair_count, 2)
    targets = tables[1].reshape(peer_count * pair_count, 2)[:, 0]
    offsets_all = tables[2].reshape(peer_count * pair_count, 2)
    ordering = jnp.argsort(targets, stable=True)
    arranged = jnp.take(spread, ordering, axis=0).reshape(
        peer_count, pair_count, 1, slice_len, channels
    )
    received = lax.all_to_all(arranged, "dp", split_axis=0, concat_axis=2, tiled=True)
    received = received.reshape(pair_count * block_len, channels)
    own_blocks = lax.dynamic_slice_in_dim(ordering, lax.axis_index("dp") * pair_count, pair_count)
    pair_lengths = jnp.take(lengths_all, own_blocks, axis=0)
    sources = jnp.stack([jnp.zeros_like(pair_lengths[:, 0]), pair_lengths[:, 0]], axis=1)
    sources = (sources + (jnp.arange(pair_count, dtype=jnp.int32) * block_len)[:, None]).reshape(-1)
    row_lengths = pair_lengths.reshape(-1)
    row_offsets = jnp.take(offsets_all, own_blocks, axis=0).reshape(-1)
    places = jnp.arange(pair_count * block_len, dtype=jnp.int32)
    relative = places[:, None] - row_offsets[None, :]
    inside = (relative >= 0) & (relative < row_lengths[None, :])
    take_index = jnp.sum(jnp.where(inside, sources[None, :] + relative, 0), axis=1)
    return jnp.take(received, take_index, axis=0)


def solution(mesh):
    n_dp, n_fsdp = mesh.shape["dp"], mesh.shape["fsdp"]

    def shards(hidden, lengths, learner, slot_offset, norm_gain, query_weight, keyval_weight):
        attended = fused(
            n_dp, n_fsdp, hidden, lengths, learner, slot_offset, norm_gain, query_weight, keyval_weight
        )
        if n_dp == 2:
            return attended
        tables = lax.all_gather(
            jnp.stack([lengths, learner, slot_offset]), "dp", axis=1, tiled=True
        )
        return route(attended, tables)

    placed = (
        P(("dp", "fsdp"), None),
        P(("dp", "fsdp")),
        P(("dp", "fsdp")),
        P(("dp", "fsdp")),
        P("fsdp"),
        P("fsdp", None),
        P("fsdp", None),
    )
    return jax.shard_map(
        shards, mesh=mesh, in_specs=placed, out_specs=P(("dp", "fsdp"), None), check_vma=False
    )
```

```python
import functools
import math

import jax
import jax.numpy as jnp
from jax import lax
from jax.experimental import pallas as pl
from jax.experimental.pallas import tpu as pltpu
from jax.sharding import PartitionSpec as P

HD = 128
QH = 4
ROPE_BASE = 500000.0
NORM_EPS = 1e-05
MESH = pl.DeviceIdType.MESH
SUBS = 1


def kernel(
    n_dp,
    n_fsdp,
    lengths_hbm,
    learner_hbm,
    offset_hbm,
    hidden_ref,
    gain_ref,
    query_ref,
    keyval_ref,
    out_ref,
    lengths_ref,
    learner_ref,
    offset_ref,
    weights,
    gains,
    own_rows,
    mate_rows,
    own_inv,
    mate_inv,
    total,
    mate_total,
    cosine,
    sine,
    masked,
    place_here,
    place_there,
    sent_heads,
    got_heads,
    local_sem,
    part_recv,
    z_send,
    y_send,
    x_send,
    gain_send,
    gain_recv,
    rows_send,
    rows_recv,
    inv_sem,
    sum_send,
    sum_recv,
    head_send,
    head_recv,
):
    dp = lax.axis_index("dp")
    fs = lax.axis_index("fsdp")
    core = lax.rem(fs, 2)
    y = lax.rem(fs // 2, 2)
    z = fs // 4
    n_z = n_fsdp // 4
    x = lax.rem(dp, 2)
    x_peer = {"dp": dp + 1 - 2 * x}
    mate = {"fsdp": fs + 1 - 2 * core}
    y_peer = {"fsdp": fs + 2 - 4 * y}
    tokens = own_rows.shape[0]
    depth = query_ref.shape[0]
    n_cols = weights.shape[2]
    q_cols = QH * HD
    part = depth // (4 * SUBS)
    own = z * 2 + y
    other = z * 2 + 1 - y
    n_shards = 2 * n_z
    role_a = 3 * x
    role_b = 1 + x
    role_c = 2 - x
    role_d = 3 - 3 * x

    def can_send(up):
        return (z + 2 * up - 1 >= 0) & (z + 2 * up - 1 < n_z)

    load_q = pltpu.make_async_copy(query_ref, weights.at[own, :, pl.ds(0, q_cols)], local_sem.at[0])
    load_kv = pltpu.make_async_copy(
        keyval_ref, weights.at[own, :, pl.ds(q_cols, n_cols - q_cols)], local_sem.at[1]
    )
    load_rows = pltpu.make_async_copy(hidden_ref, own_rows, local_sem.at[2])
    load_tables = [
        pltpu.make_async_copy(src, dst, local_sem.at[3 + i])
        for i, (src, dst) in enumerate(
            ((lengths_hbm, lengths_ref), (learner_hbm, learner_ref), (offset_hbm, offset_ref))
        )
    ]
    load_q.start()
    load_kv.start()
    load_rows.start()
    for load in load_tables:
        load.start()

    barrier = pltpu.get_barrier_semaphore()
    pl.semaphore_signal(barrier, inc=1, device_id=x_peer, device_id_type=MESH)
    pl.semaphore_signal(barrier, inc=1, device_id=mate, device_id_type=MESH)
    pl.semaphore_signal(barrier, inc=1, device_id=y_peer, device_id_type=MESH)
    for up in (0, 1):

        @pl.when(can_send(up))
        def _(up=up):
            pl.semaphore_signal(
                barrier, inc=1, device_id={"fsdp": fs + 8 * up - 4}, device_id_type=MESH
            )

    gains[own] = jnp.broadcast_to(gain_ref[...].astype(jnp.float32).reshape(1, depth), (8, depth))
    inner = (z > 0) & (z < n_z - 1)
    pl.semaphore_wait(barrier, jnp.where(inner, 5, 4))

    def piece(slot, p, n=1):
        return weights.at[slot, pl.ds(pl.multiple_of(p * part, part), n * part), :]

    def send_z(zz, p, up, n=1):
        slot = zz * 2 + y
        return pltpu.make_async_remote_copy(
            src_ref=piece(slot, p, n),
            dst_ref=piece(slot, p, n),
            send_sem=z_send.at[up, zz, p],
            recv_sem=part_recv.at[slot, p],
            device_id={"fsdp": fs + 8 * up - 4},
            device_id_type=MESH,
        )

    def send_y(zz, p, n=1):
        slot = zz * 2 + y
        return pltpu.make_async_remote_copy(
            src_ref=piece(slot, p, n),
            dst_ref=piece(slot, p, n),
            send_sem=y_send.at[zz, p],
            recv_sem=part_recv.at[slot, p],
            device_id=y_peer,
            device_id_type=MESH,
        )

    def send_x(slot, p, n=1):
        return pltpu.make_async_remote_copy(
            src_ref=piece(slot, p, n),
            dst_ref=piece(slot, p, n),
            send_sem=x_send.at[slot, p],
            recv_sem=part_recv.at[slot, p],
            device_id=x_peer,
            device_id_type=MESH,
        )

    def arrived(slot, p, n=1):
        send_x(slot, p, n).wait_recv()

    def send_gain(zz, device, sem):
        slot = zz * 2 + y
        return pltpu.make_async_remote_copy(
            src_ref=gains.at[slot],
            dst_ref=gains.at[slot],
            send_sem=sem,
            recv_sem=gain_recv.at[slot],
            device_id=device,
            device_id_type=MESH,
        )

    def gain_z(zz, up):
        return send_gain(zz, {"fsdp": fs + 8 * up - 4}, gain_send.at[up, zz])

    def gain_y(zz):
        return send_gain(zz, y_peer, gain_send.at[2, zz])

    def gain_arrived(slot):
        pltpu.make_async_remote_copy(
            src_ref=gains.at[slot],
            dst_ref=gains.at[slot],
            send_sem=gain_send.at[2, 0],
            recv_sem=gain_recv.at[slot],
            device_id=y_peer,
            device_id_type=MESH,
        ).wait_recv()

    def send_rows(s):
        start = pl.multiple_of((s * 2 + 1 - core) * depth, depth)
        return pltpu.make_async_remote_copy(
            src_ref=hidden_ref.at[:, pl.ds(start, depth)],
            dst_ref=mate_rows.at[s],
            send_sem=rows_send.at[s],
            recv_sem=rows_recv.at[s],
            device_id=mate,
            device_id_type=MESH,
        )

    send_inv = pltpu.make_async_remote_copy(
        src_ref=own_inv,
        dst_ref=mate_inv,
        send_sem=inv_sem.at[0],
        recv_sem=inv_sem.at[1],
        device_id=mate,
        device_id_type=MESH,
    )

    def each(count, body):
        def step(i, carry):
            body(i)
            return carry

        lax.fori_loop(0, count, step, 0)

    def own_z(q, act, n=1):
        def body(j):
            up = lax.rem(j, 2)
            pl.when(can_send(up))(lambda: act(send_z(z, q * SUBS + j // 2, up, n)))

        each(2 * SUBS // n, body)

    def own_y(q, act, n=SUBS):
        each(SUBS // n, lambda j: act(send_y(z, q * SUBS + j, n)))

    def start(copy):
        copy.start()

    def sent(copy):
        copy.wait_send()

    def remote(d, body, subs=SUBS):
        def step(j):
            up = lax.rem(j, 2)
            zz = z + d - 2 * d * up
            pl.when((zz >= 0) & (zz < n_z))(lambda: body(j // 2, zz, up))

        each(2 * subs, step)

    def along_z(d, q, to_y, to_x, n=1):
        def body(sub, zz, up):
            p = q * SUBS + sub
            arrived(zz * 2 + y, p, n)
            pl.when(can_send(up))(lambda: send_z(zz, p, up, n).start())
            if to_y:
                send_y(zz, p).start()
            if to_x:
                send_x(zz * 2 + y, p).start()

        remote(d, body, SUBS // n)

    def gain_along_z(d):
        def step(up):
            zz = z + d - 2 * d * up

            @pl.when((zz >= 0) & (zz < n_z))
            def _():
                gain_arrived(zz * 2 + y)
                pl.when(can_send(up))(lambda: gain_z(zz, up).start())
                gain_y(zz).start()

        each(2, step)

    def along_y(d, q):
        def body(sub, zz, up):
            p = q * SUBS + sub
            arrived(zz * 2 + 1 - y, p)
            send_x(zz * 2 + 1 - y, p).start()

        remote(d, body)

    load_q.wait()
    load_kv.wait()
    own_z(role_a, start)
    own_y(role_a, start, 1)
    own_z(role_b, start)
    for up in (0, 1):
        pl.when(can_send(up))(lambda up=up: gain_z(z, up).start())
    gain_y(z).start()

    def rows_out(i):
        for k in (2 * i, 2 * i + 1):
            send_rows(lax.rem(own + k, n_shards)).start()

    rows_out(0)

    load_rows.wait()
    width = own_rows.shape[1]

    def square(i):
        rows = pl.ds(pl.multiple_of(i * 32, 32), 32)
        values = own_rows[rows, :].astype(jnp.float32)
        mean = jnp.sum(values * values, axis=1, keepdims=True) / width
        own_inv[rows, :] = jnp.broadcast_to(lax.rsqrt(mean + NORM_EPS), (32, 128))

    each(tokens // 32, square)
    send_inv.start()
    rows_out(1)

    for load in load_tables:
        load.wait()
    n_rows = lengths_ref.shape[0]
    across = lax.broadcasted_iota(jnp.int32, (1, tokens), 1)
    down = lax.broadcasted_iota(jnp.int32, (tokens, 1), 0)
    row_across = jnp.zeros_like(across)
    row_down = jnp.zeros_like(down)
    start_down = jnp.zeros_like(down)
    target = jnp.zeros_like(across)
    goes_to = jnp.zeros_like(across)
    first = jnp.int32(0)
    for r in range(n_rows):
        in_across = across >= first
        in_down = down >= first
        row_across = jnp.where(in_across, r, row_across)
        row_down = jnp.where(in_down, r, row_down)
        start_down = jnp.where(in_down, first, start_down)
        target = jnp.where(in_across, offset_ref[r] + across - first, target)
        goes_to = jnp.where(in_across, learner_ref[r], goes_to)
        first = first + lengths_ref[r]
    position = (down - start_down).astype(jnp.float32)
    lane = lax.broadcasted_iota(jnp.int32, (1, HD), 1)
    half = HD // 2
    index = jnp.where(lane < half, lane, lane - half).astype(jnp.float32)
    angle = position * jnp.exp(index * (-2.0 * math.log(ROPE_BASE) / HD))
    cosine[...] = jnp.cos(angle)
    sine[...] = jnp.where(lane < half, -jnp.sin(angle), jnp.sin(angle))

    along_z(1, role_a, True, True)
    gain_along_z(1)
    rows_out(2)
    for i in range(3, n_shards // 2):
        rows_out(i)

    allowed = (row_across == row_down) & (across <= down)
    masked[...] = jnp.where(allowed, 0.0, 1.0)
    if n_dp == 2:
        slot_iota = lax.broadcasted_iota(jnp.int32, (tokens, tokens), 0)
        place_here[...] = jnp.where(
            slot_iota == jnp.where(goes_to == dp, target, -1), 1.0, 0.0
        ).astype(jnp.bfloat16)
        place_there[...] = jnp.where(
            slot_iota == jnp.where(goes_to == 1 - dp, target, -1), 1.0, 0.0
        ).astype(jnp.bfloat16)

    block = depth // 2

    def project(slot, h, whose):
        inner = pl.ds(pl.multiple_of(h * block, block), block)
        gain = gains[slot, 0:1, inner]
        if whose == 0:
            column = pl.multiple_of((slot * 2 + core) * depth + h * block, block)
            rows, inverse = own_rows[:, pl.ds(column, block)], own_inv[:, 0:1]
        else:
            rows, inverse = mate_rows[slot, :, inner], mate_inv[:, 0:1]
        normed = (rows.astype(jnp.float32) * inverse * gain).astype(jnp.bfloat16)
        total[whose] += jnp.dot(normed, weights[slot, inner, :], preferred_element_type=jnp.float32)

    def project_both(slot, h):
        project(slot, h, 1)
        project(slot, h, 0)

    def project_remote(d, column, h, quarters):
        def step(up):
            zz = z + d - 2 * d * up

            @pl.when((zz >= 0) & (zz < n_z))
            def _():
                slot = zz * 2 + (y if column == 0 else 1 - y)
                for q in quarters:
                    each(SUBS, lambda j: arrived(slot, q * SUBS + j))
                project_both(slot, h)

        each(2, step)

    along_z(1, role_b, True, False)
    own_z(role_c, start, SUBS)
    own_y(role_b, start)
    along_y(1, role_a)
    along_z(2, role_a, True, True)
    gain_along_z(2)
    along_y(1, role_b)
    total[...] = jnp.zeros_like(total)
    send_inv.wait_recv()
    for s in range(n_shards):
        send_rows(s).wait_recv()
    project_both(own, 0)
    along_z(2, role_b, True, False)
    own_y(role_c, start)
    project_both(own, 1)
    along_y(2, role_a)
    along_z(1, role_c, False, False, SUBS)
    project_remote(1, 0, x, ())
    for d in range(3, n_z):
        along_z(d, role_a, True, True)
        gain_along_z(d)
        along_y(d - 1, role_b)
        along_z(d, role_b, True, False)
    along_z(2, role_c, False, False, SUBS)
    own_y(role_d, start)
    for zz in range(n_z):
        gain_arrived(zz * 2 + 1 - y)
    project_remote(1, 1, x, ())
    for d in range(3, n_z):
        along_y(d, role_a)
    project_remote(2, 0, x, ())
    along_y(n_z - 1, role_b)
    project_remote(2, 1, x, ())
    project_remote(1, 1, 1 - x, (role_d, role_c))
    project_remote(1, 0, 1 - x, (role_d,))
    for d in range(3, n_z):
        project_remote(d, 0, x, ())
        project_remote(d, 1, x, ())
        along_z(d, role_c, False, False, SUBS)
    project_remote(2, 0, 1 - x, (role_d,))
    project_remote(2, 1, 1 - x, (role_d, role_c))
    each(SUBS, lambda j: arrived(other, role_a * SUBS + j))
    arrived(other, role_b * SUBS, SUBS)
    project_both(other, x)
    for d in range(3, n_z):
        project_remote(d, 0, 1 - x, (role_d,))
    for d in range(3, n_z):
        project_remote(d, 1, 1 - x, (role_d, role_c))
    for q in (role_c, role_d):
        arrived(other, q * SUBS, SUBS)
    project(other, 1 - x, 1)

    def send_sum(c):
        cols = pl.ds(c * 256, 256)
        return pltpu.make_async_remote_copy(
            src_ref=total.at[1, :, cols],
            dst_ref=mate_total.at[:, cols],
            send_sem=sum_send.at[c],
            recv_sem=sum_recv.at[c],
            device_id=mate,
            device_id_type=MESH,
        )

    n_sums = n_cols // 256
    order = [n_sums - 1] + list(range(n_sums - 1))
    for c in order:
        send_sum(c).start()
    project(other, 1 - x, 0)

    def rotated(values):
        return (values * cosine[...] + pltpu.roll(values, half, 1) * sine[...]).astype(jnp.bfloat16)

    def summed(col):
        return total[0, :, col : col + HD] + mate_total[:, col : col + HD]

    send_sum(n_sums - 1).wait_recv()
    key = rotated(summed(q_cols))
    value = summed(q_cols + HD).astype(jnp.bfloat16)

    def send_head(h):
        return pltpu.make_async_remote_copy(
            src_ref=sent_heads.at[h],
            dst_ref=got_heads.at[h],
            send_sem=head_send.at[h],
            recv_sem=head_recv.at[h],
            device_id=x_peer,
            device_id_type=MESH,
        )

    for h in range(QH):
        if h % 2 == 0:
            send_sum(h // 2).wait_recv()
        query = rotated(summed(h * HD))
        scores = lax.dot_general(
            query, key, (((1,), (1,)), ((), ())), preferred_element_type=jnp.float32
        ) * HD ** (-0.5)
        scores = jnp.where(masked[...] > 0.5, -1e30, scores)
        exped = jnp.exp(scores - jnp.max(scores, axis=1, keepdims=True))
        chance = (exped / jnp.sum(exped, axis=1, keepdims=True)).astype(jnp.bfloat16)
        mixed = jnp.dot(chance, value, preferred_element_type=jnp.float32).astype(jnp.bfloat16)
        cols = pl.ds(h * HD, HD)
        if n_dp == 2:
            sent_heads[h] = jnp.dot(
                place_there[...], mixed, preferred_element_type=jnp.float32
            ).astype(jnp.bfloat16)
            send_head(h).start()
            out_ref[:, cols] = jnp.dot(
                place_here[...], mixed, preferred_element_type=jnp.float32
            ).astype(jnp.bfloat16)
        else:
            out_ref[:, cols] = mixed

    for q in (role_a, role_b):
        own_z(q, sent)
    own_z(role_c, sent, SUBS)
    own_y(role_a, sent, 1)
    for q in (role_b, role_c, role_d):
        own_y(q, sent)
    for zz in range(n_z):
        pl.when(can_send(0) & (zz >= z))(lambda zz=zz: gain_z(zz, 0).wait_send())
        pl.when(can_send(1) & (zz <= z))(lambda zz=zz: gain_z(zz, 1).wait_send())
        gain_y(zz).wait_send()
    for s in range(n_shards):
        send_rows(s).wait_send()
    send_inv.wait_send()

    def relayed(sub, zz, up):
        a, b = role_a * SUBS + sub, role_b * SUBS + sub
        for p in (a, b):
            pl.when(can_send(up))(lambda p=p: send_z(zz, p, up).wait_send())
        send_y(zz, a).wait_send()
        send_y(zz, b).wait_send()
        send_x(zz * 2 + y, a).wait_send()
        send_x(zz * 2 + 1 - y, a).wait_send()
        send_x(zz * 2 + 1 - y, b).wait_send()

    def relayed_whole(sub, zz, up):
        pl.when(can_send(up))(lambda: send_z(zz, role_c * SUBS, up, SUBS).wait_send())

    for d in range(1, n_z):
        remote(d, relayed)
        remote(d, relayed_whole, 1)

    for c in order:
        send_sum(c).wait_send()
    if n_dp == 2:
        for h in range(QH):
            cols = pl.ds(h * HD, HD)
            send_head(h).wait_recv()
            out_ref[:, cols] = out_ref[:, cols] + got_heads[h]
        for h in range(QH):
            send_head(h).wait_send()


def fused(n_dp, n_fsdp, hidden, lengths, learner, slot_offset, norm_gain, query_weight, keyval_weight):
    tokens, width = hidden.shape
    depth, q_cols = query_weight.shape
    n_cols = q_cols + keyval_weight.shape[1]
    n_z = n_fsdp // 4
    n_shards = 2 * n_z
    bf16, f32 = jnp.bfloat16, jnp.float32
    dma = pltpu.SemaphoreType.DMA
    vmem = pl.BlockSpec(memory_space=pltpu.VMEM)
    hbm = pl.BlockSpec(memory_space=pl.ANY)
    return pl.pallas_call(
        functools.partial(kernel, n_dp, n_fsdp),
        out_shape=jax.ShapeDtypeStruct((tokens, q_cols), bf16),
        in_specs=[hbm, hbm, hbm, hbm, vmem, hbm, hbm],
        out_specs=vmem,
        scratch_shapes=[
            pltpu.SMEM(lengths.shape, jnp.int32),
            pltpu.SMEM(lengths.shape, jnp.int32),
            pltpu.SMEM(lengths.shape, jnp.int32),
            pltpu.VMEM((n_shards, depth, n_cols), bf16),
            pltpu.VMEM((n_shards, 8, depth), f32),
            pltpu.VMEM((tokens, width), bf16),
            pltpu.VMEM((n_shards, tokens, depth), bf16),
            pltpu.VMEM((tokens, 128), f32),
            pltpu.VMEM((tokens, 128), f32),
            pltpu.VMEM((2, tokens, n_cols), f32),
            pltpu.VMEM((tokens, n_cols), f32),
            pltpu.VMEM((tokens, HD), f32),
            pltpu.VMEM((tokens, HD), f32),
            pltpu.VMEM((tokens, tokens), f32),
            pltpu.VMEM((tokens, tokens), bf16),
            pltpu.VMEM((tokens, tokens), bf16),
            pltpu.VMEM((QH, tokens, HD), bf16),
            pltpu.VMEM((QH, tokens, HD), bf16),
            dma((6,)),
            dma((n_shards, 4 * SUBS)),
            dma((2, n_z, 4 * SUBS)),
            dma((n_z, 4 * SUBS)),
            dma((n_shards, 4 * SUBS)),
            dma((3, n_z)),
            dma((n_shards,)),
            dma((n_shards,)),
            dma((n_shards,)),
            dma((2,)),
            dma((n_cols // 256,)),
            dma((n_cols // 256,)),
            dma((QH,)),
            dma((QH,)),
        ],
        compiler_params=pltpu.CompilerParams(
            collective_id=0, has_side_effects=True, vmem_limit_bytes=60 * 1024 * 1024
        ),
    )(lengths, learner, slot_offset, hidden, norm_gain, query_weight, keyval_weight)


def route(buffer, tables):
    channels = buffer.shape[1]
    peer_count = lax.axis_size("dp")
    pair_count = tables.shape[1] // (2 * peer_count)
    block_len = buffer.shape[0] // pair_count
    slice_len = block_len // peer_count
    blocks = buffer.reshape(pair_count, peer_count, slice_len, channels)
    spread = lax.all_to_all(blocks, "dp", split_axis=1, concat_axis=0, tiled=True)
    lengths_all = tables[0].reshape(peer_count * pair_count, 2)
    targets = tables[1].reshape(peer_count * pair_count, 2)[:, 0]
    offsets_all = tables[2].reshape(peer_count * pair_count, 2)
    ordering = jnp.argsort(targets, stable=True)
    arranged = jnp.take(spread, ordering, axis=0).reshape(
        peer_count, pair_count, 1, slice_len, channels
    )
    received = lax.all_to_all(arranged, "dp", split_axis=0, concat_axis=2, tiled=True)
    received = received.reshape(pair_count * block_len, channels)
    own_blocks = lax.dynamic_slice_in_dim(ordering, lax.axis_index("dp") * pair_count, pair_count)
    pair_lengths = jnp.take(lengths_all, own_blocks, axis=0)
    sources = jnp.stack([jnp.zeros_like(pair_lengths[:, 0]), pair_lengths[:, 0]], axis=1)
    sources = (sources + (jnp.arange(pair_count, dtype=jnp.int32) * block_len)[:, None]).reshape(-1)
    row_lengths = pair_lengths.reshape(-1)
    row_offsets = jnp.take(offsets_all, own_blocks, axis=0).reshape(-1)
    places = jnp.arange(pair_count * block_len, dtype=jnp.int32)
    relative = places[:, None] - row_offsets[None, :]
    inside = (relative >= 0) & (relative < row_lengths[None, :])
    take_index = jnp.sum(jnp.where(inside, sources[None, :] + relative, 0), axis=1)
    return jnp.take(received, take_index, axis=0)


def solution(mesh):
    n_dp, n_fsdp = mesh.shape["dp"], mesh.shape["fsdp"]

    def shards(hidden, lengths, learner, slot_offset, norm_gain, query_weight, keyval_weight):
        attended = fused(
            n_dp, n_fsdp, hidden, lengths, learner, slot_offset, norm_gain, query_weight, keyval_weight
        )
        if n_dp == 2:
            return attended
        tables = lax.all_gather(
            jnp.stack([lengths, learner, slot_offset]), "dp", axis=1, tiled=True
        )
        return route(attended, tables)

    placed = (
        P(("dp", "fsdp"), None),
        P(("dp", "fsdp")),
        P(("dp", "fsdp")),
        P(("dp", "fsdp")),
        P("fsdp"),
        P("fsdp", None),
        P("fsdp", None),
    )
    return jax.shard_map(
        shards, mesh=mesh, in_specs=placed, out_specs=P(("dp", "fsdp"), None), check_vma=False
    )
```
